32 devices in a mesh: groups: 2 (over x), lines: 16 (over z, y, core).
Axes of the slice: x: 2, y: 2, z: 4, core: 2. Of those that a mesh axis runs over, the one named last changes fastest.
Arguments:
- raw_echo: bfloat16 [8, 2, 2048, 512], P('groups', None, 'lines'), parts along dimension 0, may hold values from -6 to 6
- range_filter: bfloat16 [2, 512, 512], replicated, may hold values from -0.1875 to 0.1875
- azimuth_phase: float32 [512, 2048], P('lines'), may hold values from -3.140625 to 3.140625
- pair_offset: int32 [4], replicated, may hold values from 1 to 3
Outputs:
- filtered: float32 [8, 2, 128, 1024], P('groups', None, None, 'lines'), parts along dimension 0
The draws below stay inside these ranges and needn't reach their ends.
There are 2 independent parts, one for each index of `groups`. The reference program is written for one: setup_inputs(seed, part) draws one part's arguments, and reference() takes and returns one part's arrays. A program takes and returns all parts, laid end to end along the dimension named above; an argument that names none is the same for every part. Nothing has to cross between parts.
Inputs may be any that keep to these rules, and one draw needn't show every extreme that they name: Date d is paired with date (d + pair_offset[d]) mod 4.
All inputs are finite; a program needn't handle non-finite values.
Results may differ from the reference program's by a relative error of at most 0.0095.
Values may be sent and summed in bfloat16 or wider, within the bound.
No kernel may reach another device: no remote copies, remote signals or barrier semaphores. Data moves between devices by JAX's collectives and lax.ppermute only.
A program may use at most 192 MiB of HBM per device.

```python
import jax
import jax.numpy as jnp
from jax import lax

DATES = 4
GATES = 512
ML_RG = 4
ML_AZ = 2
PATCH = 32
LINES = 2048


def touch_ends(drawn, own_key, low, largest):
    longest = drawn.shape.index(max(drawn.shape))
    spots = []
    for shift in (0, 1):
        where = [jax.random.randint(jax.random.fold_in(own_key, axis), (), 0, length) for axis, length in enumerate(drawn.shape)]
        where[longest] = (where[longest] + shift) % drawn.shape[longest]
        spots.append(tuple(where))
    return drawn.at[spots[0]].set(low).at[spots[1]].set(largest)


def steps_of(stream_key, shape, cuts, low, top_value):
    def one(dim, blocks):
        steps = jax.random.uniform(jax.random.fold_in(jax.random.fold_in(stream_key, 6), dim), (blocks,), jnp.float32, low / len(cuts), top_value / len(cuts))
        return jnp.repeat(jnp.exp(steps), shape[dim] // blocks).reshape((-1,) + (1,) * (len(shape) - dim - 1))

    factor_of = one(*cuts[0])
    for cut in cuts[1:]:
        factor_of = factor_of * one(*cut)
    return factor_of


def scatter_about(key, extent, width, bound, split=(), held_as=jnp.bfloat16):
    loudness = steps_of(key, extent, split, -0.22, 0.18) if split else 1.0
    values = jax.random.normal(key, extent, jnp.float32) * width * loudness
    return jnp.minimum(jnp.maximum(values, -bound), bound).astype(held_as)


def setup_inputs(seed: int = 0, part: int = 0) -> dict:
    key_list = jax.random.split(jax.random.key(seed), 5)
    own_keys = jax.random.split(jax.random.fold_in(key_list[4], part), 5)
    return {
        "raw_echo": scatter_about(own_keys[0], (DATES, 2, LINES, GATES), 1.0, 6.0, ((2, 16),)),
        "range_filter": scatter_about(key_list[1], (2, GATES, GATES), (2 * GATES) ** -0.5, 0.1875),
        "azimuth_phase": jnp.clip(jax.random.uniform(key_list[2], (GATES, LINES), jnp.float32, -3.140625, 3.140625), -3.140625, 3.140625),
        "pair_offset": touch_ends(jax.random.randint(key_list[3], (DATES,), 1, DATES), jax.random.fold_in(key_list[3], 1), 1, DATES - 1).astype(jnp.int32),
    }


PRECISION_MAX = lax.Precision.HIGHEST
BOX_FLOOR = 0.25

def compress(raw_echo, range_filter):
    w_real = jnp.stack([range_filter[0], -range_filter[1]])
    w_imag = jnp.stack([range_filter[1], range_filter[0]])
    stacked = jnp.stack([w_real, w_imag]).astype(jnp.float32)
    result = jnp.einsum('ecog,dclg->deol', stacked, raw_echo.astype(jnp.float32), precision=PRECISION_MAX)
    return result.astype(jnp.bfloat16)

def focus(compressed, azimuth_phase):
    signal = lax.complex(compressed[:, 0].astype(jnp.float32), compressed[:, 1].astype(jnp.float32))
    spectrum = jnp.fft.fft(signal, axis=-1)
    doppler = lax.complex(jnp.cos(azimuth_phase), jnp.sin(azimuth_phase))
    image = jnp.fft.ifft(spectrum * doppler, axis=-1)
    return jnp.stack([jnp.real(image), jnp.imag(image)], axis=1).astype(jnp.bfloat16)

def interfere(focused, pair_offset):
    date_count = focused.shape[0]
    partner_index = (jnp.arange(date_count, dtype=jnp.int32) + pair_offset) % date_count
    current = focused.astype(jnp.float32)
    partner = jnp.take(current, partner_index, axis=0)
    real_part = current[:, 0] * partner[:, 0] + current[:, 1] * partner[:, 1]
    imag_part = current[:, 1] * partner[:, 0] - current[:, 0] * partner[:, 1]
    joined = jnp.stack([real_part, imag_part], axis=1)
    shape_all = joined.shape
    joined = joined.reshape(shape_all[0], 2, shape_all[2] // ML_RG, ML_RG, shape_all[3] // ML_AZ, ML_AZ)
    return lax.optimization_barrier(jnp.mean(joined, axis=(3, 5)))

def tri_window(patch_len):
    position = jnp.arange(patch_len, dtype=jnp.float32)
    return 1.0 - jnp.abs(position - (patch_len - 1) / 2.0) / (patch_len // 2)

def filter_patches(block_real, block_imag):
    spectra = jnp.fft.fft2(lax.complex(block_real, block_imag), axes=(2, 4))
    spectral = jnp.real(spectra) ** 2 + jnp.imag(spectra) ** 2
    smooth = jnp.zeros_like(spectral)
    for shift_gate in (-1, 0, 1):
        for shift_line in (-1, 0, 1):
            smooth = smooth + jnp.roll(spectral, (shift_gate, shift_line), axis=(2, 4))
    smooth = smooth / 9.0
    level_mean = lax.optimization_barrier(jnp.mean(smooth, axis=(2, 4), keepdims=True)) + 1e-06
    weight = jnp.sqrt(smooth / level_mean + BOX_FLOOR)
    inverse = jnp.fft.ifft2(spectra * weight, axes=(2, 4))
    window = tri_window(PATCH)
    window_two = window[:, None, None] * window[None, None, :]
    return (jnp.real(inverse) * window_two, jnp.imag(inverse) * window_two)

def goldstein(pad_real, pad_imag, gate_rows, line_cols):
    half_patch = PATCH // 2
    date_count = pad_real.shape[0]
    out_real = jnp.zeros((date_count, gate_rows, line_cols), jnp.float32)
    out_imag = jnp.zeros((date_count, gate_rows, line_cols), jnp.float32)
    for gate_odd in (0, 1):
        gate_start = gate_odd * half_patch
        gate_len = gate_rows + PATCH - 2 * gate_odd * half_patch
        gate_crop = half_patch - gate_start
        for line_odd in (0, 1):
            line_start = line_odd * half_patch
            line_len = line_cols + PATCH - 2 * line_odd * half_patch
            line_crop = half_patch - line_start
            shape_new = (date_count, gate_len // PATCH, PATCH, line_len // PATCH, PATCH)
            block_real = pad_real[:, gate_start:gate_start + gate_len, line_start:line_start + line_len].reshape(shape_new)
            block_imag = pad_imag[:, gate_start:gate_start + gate_len, line_start:line_start + line_len].reshape(shape_new)
            part_real, part_imag = filter_patches(block_real, block_imag)
            part_real = part_real.reshape(date_count, gate_len, line_len)
            part_imag = part_imag.reshape(date_count, gate_len, line_len)
            out_real = out_real + part_real[:, gate_crop:gate_crop + gate_rows, line_crop:line_crop + line_cols]
            out_imag = out_imag + part_imag[:, gate_crop:gate_crop + gate_rows, line_crop:line_crop + line_cols]
    return (out_real, out_imag)

def reference(raw_echo, range_filter, azimuth_phase, pair_offset):
    compressed = compress(raw_echo, range_filter)
    focused = focus(compressed, azimuth_phase)
    looks = interfere(focused, pair_offset)
    half_patch = PATCH // 2
    padded = jnp.pad(looks, ((0, 0), (0, 0), (half_patch, half_patch), (half_patch, half_patch)))
    out_real, out_imag = goldstein(padded[:, 0], padded[:, 1], looks.shape[2], looks.shape[3])
    return jnp.stack([out_real, out_imag], axis=1)
```

```python
import math

import jax
import jax.numpy as jnp
import numpy as np
from jax import lax
from jax.experimental import pallas as pl
from jax.experimental.pallas import tpu as pltpu
from jax.sharding import PartitionSpec as P

ML_RG = 4
ML_AZ = 2
PATCH = 32
HALF = PATCH // 2
BOX_FLOOR = 0.25
LEVEL_FLOOR = 1e-06
SUB = 8
LANES = 128
VMEM_BYTES = 48 * 1024 * 1024


def real_block(table):
    return np.block([[table.real, table.imag], [-table.imag, table.real]])


def wave(rows, cols, period, direction):
    product = np.asarray(rows)[:, None] * np.asarray(cols)[None, :] % period
    return np.exp(direction * 2j * math.pi / period * product)


def as_bf16(table):
    return jnp.asarray(np.asarray(table, np.float32), jnp.bfloat16)


def line_order(line_len):
    return np.arange(line_len).reshape(line_len // ML_AZ, ML_AZ).T.reshape(-1)


def small_dft(parts, direction):
    count = len(parts)
    if count == 1:
        return parts
    even = small_dft(parts[0::2], direction)
    odd = small_dft(parts[1::2], direction)
    low, high = [], []
    for k in range(count // 2):
        (er, ei), (vr, vi) = even[k], odd[k]
        if k == 0:
            tr, ti = vr, vi
        elif 4 * k == count:
            if direction < 0:
                tr, ti = vi, -vr
            else:
                tr, ti = -vi, vr
        elif 8 * k == count:
            s = math.sqrt(0.5)
            if direction < 0:
                tr, ti = (vr + vi) * s, (vi - vr) * s
            else:
                tr, ti = (vr - vi) * s, (vi + vr) * s
        elif 8 * k == 3 * count:
            s = math.sqrt(0.5)
            if direction < 0:
                tr, ti = (vi - vr) * s, -(vr + vi) * s
            else:
                tr, ti = -(vr + vi) * s, (vr - vi) * s
        else:
            c = math.cos(2 * math.pi * k / count)
            s = direction * math.sin(2 * math.pi * k / count)
            tr, ti = vr * c - vi * s, vr * s + vi * c
        low.append((er + tr, ei + ti))
        high.append((er - tr, ei - ti))
    return low + high


def compress_kernel(shape, raw_ref, filter_ref, out_ref, wide_ref):
    dates, targets, tiles, gates, lines = shape
    looks_rows = gates // ML_RG
    raw = [raw_ref[:, part].reshape(dates * lines, raw_ref.shape[3]) for part in (0, 1)]
    weight = [filter_ref[part] for part in (0, 1)]

    def product(w, x):
        return lax.dot_general(
            w, x, (((1,), (1,)), ((), ())), preferred_element_type=jnp.float32
        )

    real = product(weight[0], raw[0]) - product(weight[1], raw[1])
    imag = product(weight[1], raw[0]) + product(weight[0], raw[1])
    for date in range(dates):
        wide_ref[date, 0] = real[:, date * lines : (date + 1) * lines]
        wide_ref[date, 1] = imag[:, date * lines : (date + 1) * lines]
    for target in range(targets):
        for date in range(dates):
            for tile in range(tiles):
                rows = []
                for part in (0, 1):
                    first, count = tile * SUB, min(looks_rows, SUB)
                    for at in range(first, first + SUB, count):
                        gate = target * gates + at // looks_rows + ML_RG * (at % looks_rows)
                        rows.append(wide_ref[date, part, pl.ds(gate, count, stride=ML_RG), :])
                out_ref[target, date, tile] = jnp.concatenate(rows, axis=0).astype(jnp.bfloat16)


def compress(raw_echo, range_filter, targets):
    dates, _, lines, gates_in = raw_echo.shape
    gates_out = range_filter.shape[1]
    gates = gates_out // targets
    tiles = gates // SUB
    step = 2 if dates % 2 == 0 else 1
    shape = (step, targets, tiles, gates, lines)
    return pl.pallas_call(
        lambda *refs: compress_kernel(shape, *refs),
        grid=(dates // step,),
        out_shape=jax.ShapeDtypeStruct((targets, dates, tiles, 2 * SUB, lines), jnp.bfloat16),
        in_specs=[
            pl.BlockSpec((step, 2, lines, gates_in), lambda i: (i, 0, 0, 0)),
            pl.BlockSpec(range_filter.shape, lambda i: (0, 0, 0)),
        ],
        out_specs=pl.BlockSpec((targets, step, tiles, 2 * SUB, lines), lambda i: (0, i, 0, 0, 0)),
        scratch_shapes=[pltpu.VMEM((step, 2, gates_out, lines), jnp.float32)],
        compiler_params=pltpu.CompilerParams(vmem_limit_bytes=VMEM_BYTES),
        name="compress",
    )(raw_echo, range_filter)


def focus_kernel(
    shape, offset_ref, data_ref, phase_ref, turn_ref, fwd_ref, back_ref, out_ref, image_ref, look_ref
):
    dates, blocks, tiles, gates, lines = shape
    looks_rows = gates // ML_RG
    look_lines = lines // ML_AZ
    for date in range(dates):
        for tile in range(tiles):
            parts = []
            for a in range(blocks):
                both = data_ref[a, date, tile].astype(jnp.float32)
                parts.append((both[:SUB], both[SUB:]))
            parts = small_dft(parts, -1)
            turned = []
            for a, (re, im) in enumerate(parts):
                tr, ti = turn_ref[0, a : a + 1], turn_ref[1, a : a + 1]
                turned.append((re * tr - im * ti, re * ti + im * tr))
            rows = jnp.concatenate(
                [jnp.concatenate([re, im], axis=1) for re, im in turned], axis=0
            ).astype(jnp.bfloat16)
            spectrum = jnp.dot(rows, fwd_ref[...], preferred_element_type=jnp.float32)
            re, im = spectrum[:, :lines], spectrum[:, lines:]
            pr, pi = phase_ref[0, tile], phase_ref[1, tile]
            rows = jnp.concatenate([re * pr - im * pi, re * pi + im * pr], axis=1).astype(
                jnp.bfloat16
            )
            back = jnp.dot(rows, back_ref[...], preferred_element_type=jnp.float32)
            parts = []
            for a in range(blocks):
                re = back[a * SUB : (a + 1) * SUB, :lines]
                im = back[a * SUB : (a + 1) * SUB, lines:]
                tr, ti = turn_ref[2, a : a + 1], turn_ref[3, a : a + 1]
                parts.append((re * tr - im * ti, re * ti + im * tr))
            parts = small_dft(parts, 1)
            for a, (re, im) in enumerate(parts):
                image_ref[date, tile, a, 0] = re
                image_ref[date, tile, a, 1] = im

    lane = lax.broadcasted_iota(jnp.int32, (SUB, lines), 1)
    first = lane < look_lines
    scale = 1.0 / (ML_RG * ML_AZ)
    for date in range(dates):
        partner = lax.rem(date + offset_ref[date], dates)
        for a in range(blocks):
            sums = {}
            for tile in range(tiles):
                cr, ci = image_ref[date, tile, a, 0], image_ref[date, tile, a, 1]
                pr, pi = image_ref[partner, tile, a, 0], image_ref[partner, tile, a, 1]
                re, im = cr * pr + ci * pi, ci * pr - cr * pi
                at = tile * SUB % looks_rows
                if at in sums:
                    re, im = re + sums[at][0], im + sums[at][1]
                sums[at] = (re, im)
            for at, (re, im) in sums.items():
                step = SUB
                while step > looks_rows:
                    step //= 2
                    re = re + pltpu.roll(re, step, 0)
                    im = im + pltpu.roll(im, step, 0)
                re = re + pltpu.roll(re, look_lines, 1)
                im = im + pltpu.roll(im, look_lines, 1)
                count = min(SUB, looks_rows)
                row = date * looks_rows + at
                look_ref[a, row : row + count, :] = (jnp.where(first, re, im) * scale)[:count]

    small = lax.broadcasted_iota(jnp.int32, (looks_rows, lines), 1) % look_lines
    from_high, from_low = small < HALF, small >= look_lines - HALF
    zero = jnp.zeros((looks_rows, lines), jnp.float32)

    def rim(a, date):
        rows = slice(date * looks_rows, (date + 1) * looks_rows)
        high = look_ref[a + 1, rows, :] if a + 1 < blocks else zero
        low = look_ref[a - 1, rows, :] if a > 0 else zero
        return jnp.where(from_high, high, low)

    for a in range(blocks):
        for date in range(0, dates, 2):
            own = rim(a, date)
            other = pltpu.roll(rim(a, date + 1), look_lines // 2, 1)
            row = (dates + date // 2) * looks_rows
            look_ref[a, row : row + looks_rows, :] = jnp.where(from_high | from_low, own, other)
    out_ref[...] = look_ref[...].astype(jnp.bfloat16)


def focus(columns, azimuth_phase, pair_offset):
    blocks, dates, tiles, _, lines = columns.shape
    gates, total = azimuth_phase.shape
    looks_rows = gates // ML_RG
    phase = azimuth_phase.reshape(looks_rows, ML_RG, lines, blocks).transpose(3, 1, 0, 2)
    phase = phase.reshape(blocks, tiles, SUB, lines).transpose(1, 0, 2, 3)
    phase = phase.reshape(tiles, blocks * SUB, lines)
    phase = jnp.stack([jnp.cos(phase), jnp.sin(phase)])
    order = line_order(lines)
    ahead = wave(np.arange(blocks), np.arange(lines), total, -1)
    behind = wave(np.arange(blocks), order, total, 1)
    turn = np.stack([ahead.real, ahead.imag, behind.real, behind.imag]).astype(np.float32)
    fwd = as_bf16(real_block(wave(np.arange(lines), np.arange(lines), lines, -1)))
    back = as_bf16(real_block(wave(np.arange(lines), order, lines, 1) / total))
    slots = dates + dates // 2
    shape = (dates, blocks, tiles, gates, lines)
    whole = pl.BlockSpec(memory_space=pltpu.VMEM)
    return pl.pallas_call(
        lambda *refs: focus_kernel(shape, *refs),
        out_shape=jax.ShapeDtypeStruct((blocks, slots * looks_rows, lines), jnp.bfloat16),
        in_specs=[pl.BlockSpec(memory_space=pltpu.SMEM)] + [whole] * 5,
        out_specs=whole,
        scratch_shapes=[
            pltpu.VMEM((dates, tiles, blocks, 2, SUB, lines), jnp.float32),
            pltpu.VMEM((blocks, slots * looks_rows, lines), jnp.float32),
        ],
        compiler_params=pltpu.CompilerParams(vmem_limit_bytes=VMEM_BYTES),
        name="focus",
    )(pair_offset, columns, phase, jnp.asarray(turn), fwd, back)


def tri_window(offset):
    inside = (offset >= 0) & (offset < PATCH)
    return np.where(inside, 1.0 - np.abs(offset - (PATCH - 1) / 2.0) / HALF, 0.0)


def patch_tables(cells, starts):
    offset = np.asarray(cells)[:, None] - np.asarray(starts)[None, :]
    inside = ((offset >= 0) & (offset < PATCH)).astype(np.float64)
    angle = 2.0 * math.pi / PATCH * (offset[:, :, None] * np.arange(PATCH) % PATCH)
    ahead = np.exp(-1j * angle) * inside[:, :, None]
    behind = np.exp(1j * angle) * tri_window(offset)[:, :, None] / PATCH
    flat = (len(cells), len(starts) * PATCH)
    return ahead.reshape(flat), behind.reshape(flat).T


def goldstein_tables(dates, gate_looks, line_looks):
    per = LANES // PATCH
    starts = np.arange(-HALF, line_looks, HALF)
    cells = np.arange(-HALF, line_looks + HALF)
    ahead, behind = patch_tables(cells, starts)
    main = slice(HALF, HALF + line_looks)
    behind = behind[:, main]
    split = per * PATCH

    def lanes_of(table, shift):
        block = np.zeros((2, line_looks, table.shape[1]), complex)
        block[0], block[1] = table[main], 1j * table[main]
        rim = np.zeros((2, line_looks, table.shape[1]), complex)
        for part, turn in enumerate((1.0, 1j)):
            rim[part, :HALF] = turn * table[HALF + line_looks :]
            rim[part, line_looks - HALF :] = turn * table[:HALF]
        flat = (2 * line_looks, table.shape[1])
        return block.reshape(flat), np.roll(rim.reshape(flat), shift, axis=0)

    def out_parts(table):
        return np.concatenate([table.real, table.imag], axis=1)

    near = [
        out_parts(np.concatenate(lanes_of(ahead[:, :split], parity * (line_looks // 2))))
        for parity in (0, 1)
    ]
    rest = ahead.shape[1] - split
    far_block = np.zeros((dates, 2 * line_looks, dates, rest), complex)
    far_rim = np.zeros((dates // 2, 2 * line_looks, dates, rest), complex)
    for date in range(dates):
        block, rim = lanes_of(ahead[:, split:], date % 2 * (line_looks // 2))
        far_block[date, :, date] = block
        far_rim[date // 2, :, date] = rim
    far = np.concatenate([far_block, far_rim]).reshape(-1, dates * rest)
    gate_starts = np.arange(-HALF, gate_looks, HALF)
    gate_ahead, gate_behind = patch_tables(np.arange(gate_looks), gate_starts)
    ahead_rows = real_block(gate_ahead).T
    behind_rows = real_block(gate_behind).T

    lines_back = []
    for date in range(dates):
        far_back = np.zeros((dates, rest, line_looks), complex)
        far_back[date] = behind[split:]
        lines_back.append(
            np.concatenate(
                [real_block(behind[:split]), real_block(far_back.reshape(-1, line_looks))]
            ).T
        )
    gap = (np.arange(PATCH)[:, None] - np.arange(PATCH)[None, :]) % PATCH
    ring = ((gap == 0) | (gap == 1) | (gap == PATCH - 1)).astype(np.float64)
    box = np.concatenate(
        [np.kron(np.eye(per), ring), np.kron(np.eye(per), np.ones((PATCH, PATCH)))], axis=1
    )
    tables = (np.stack(near), out_parts(far), ahead_rows, box, behind_rows, np.stack(lines_back))
    return [as_bf16(table) for table in tables]


def goldstein_kernel(
    shape, data_ref, near_ref, far_ref, ahead_ref, box_ref, behind_ref, back_ref, out_ref,
    half_ref, spec_ref, weighted_ref,
):
    dates, blocks, looks_rows, line_looks = shape
    slots = dates + dates // 2
    gate_looks = blocks * looks_rows
    cols = dates + 1
    dot = lambda a, b: jnp.dot(a, b, preferred_element_type=jnp.float32)
    if len(data_ref.shape) == 3 and data_ref.shape[0] == slots:
        held = [data_ref[slot] for slot in range(slots)]
    else:
        data = data_ref[...].astype(jnp.float32)
        held = [
            data[:, slot * looks_rows : (slot + 1) * looks_rows]
            .reshape(gate_looks, LANES)
            .astype(jnp.bfloat16)
            for slot in range(slots)
        ]
    for parity in (0, 1):
        rows = jnp.concatenate(
            [
                jnp.concatenate([held[date], held[dates + date // 2]], axis=1)
                for date in range(parity, dates, 2)
            ],
            axis=0,
        )
        both = dot(rows, near_ref[parity]).astype(jnp.bfloat16)
        for index, date in enumerate(range(parity, dates, 2)):
            mine = both[index * gate_looks : (index + 1) * gate_looks]
            half_ref[:gate_looks, date * LANES : (date + 1) * LANES] = mine[:, :LANES]
            half_ref[gate_looks:, date * LANES : (date + 1) * LANES] = mine[:, LANES:]
    both = dot(jnp.concatenate(held, axis=1), far_ref[...]).astype(jnp.bfloat16)
    half_ref[:gate_looks, dates * LANES :] = both[:, :LANES]
    half_ref[gate_looks:, dates * LANES :] = both[:, LANES:]

    spec_ref[...] = dot(ahead_ref[...], half_ref[...])
    bins = ahead_ref.shape[0] // 2
    for col in range(cols):
        lanes = slice(col * LANES, (col + 1) * LANES)
        re, im = spec_ref[:bins, lanes], spec_ref[bins:, lanes]
        power = (re * re + im * im).astype(jnp.bfloat16)
        sums = dot(power, box_ref[...])
        for start in range(0, bins, PATCH):
            rows = slice(start, start + PATCH)
            line = sums[rows, :LANES]
            total = jnp.sum(sums[rows, LANES:], axis=0, keepdims=True)
            smooth = line + pltpu.roll(line, 1, 0) + pltpu.roll(line, PATCH - 1, 0)
            level = total * (1.0 / (PATCH * PATCH)) + LEVEL_FLOOR
            weight = jnp.sqrt(smooth * (1.0 / (9.0 * level)) + BOX_FLOOR)
            weighted_ref[rows, lanes] = (re[rows] * weight).astype(jnp.bfloat16)
            weighted_ref[start + bins : start + bins + PATCH, lanes] = (im[rows] * weight).astype(
                jnp.bfloat16
            )
    inverse = dot(behind_ref[...], weighted_ref[...]).astype(jnp.bfloat16)
    far = [inverse[:gate_looks, dates * LANES :], inverse[gate_looks:, dates * LANES :]]
    for date in range(dates):
        lanes = slice(date * LANES, (date + 1) * LANES)
        rows = jnp.concatenate([inverse[:gate_looks, lanes], inverse[gate_looks:, lanes]] + far, axis=1)
        result = lax.dot_general(
            back_ref[date], rows, (((1,), (1,)), ((), ())), preferred_element_type=jnp.float32
        )
        out_ref[date, 0] = result[:line_looks]
        out_ref[date, 1] = result[line_looks:]


def goldstein(looks, dates, line_looks):
    blocks, rows, _ = looks.shape
    slots = dates + dates // 2
    looks_rows = rows // slots
    gate_looks = blocks * looks_rows
    if looks_rows % SUB:
        looks = looks.reshape(blocks, slots, looks_rows, LANES).transpose(1, 0, 2, 3)
        looks = looks.reshape(slots, gate_looks, LANES)
    tables = goldstein_tables(dates, gate_looks, line_looks)
    bins = tables[2].shape[0] // 2
    width = (dates + 1) * LANES
    shape = (dates, blocks, looks_rows, line_looks)
    whole = pl.BlockSpec(memory_space=pltpu.VMEM)
    filtered = pl.pallas_call(
        lambda *refs: goldstein_kernel(shape, *refs),
        out_shape=jax.ShapeDtypeStruct((dates, 2, line_looks, gate_looks), jnp.float32),
        in_specs=[whole] * 7,
        out_specs=whole,
        scratch_shapes=[
            pltpu.VMEM((2 * gate_looks, width), jnp.bfloat16),
            pltpu.VMEM((2 * bins, width), jnp.float32),
            pltpu.VMEM((2 * bins, width), jnp.bfloat16),
        ],
        compiler_params=pltpu.CompilerParams(vmem_limit_bytes=VMEM_BYTES),
        name="goldstein",
    )(looks, *tables)
    return filtered.swapaxes(2, 3)


def body(raw_echo, range_filter, azimuth_phase, pair_offset):
    dates, _, lines, _ = raw_echo.shape
    devices = lax.axis_size("lines")
    sent = compress(raw_echo, range_filter, devices)
    columns = lax.all_to_all(sent, "lines", split_axis=0, concat_axis=0, tiled=True)
    sent = focus(columns, azimuth_phase, pair_offset)
    looks = lax.all_to_all(sent, "lines", split_axis=0, concat_axis=0, tiled=True)
    return goldstein(looks, dates, lines // ML_AZ)


def solution(mesh):
    placed = (P("groups", None, "lines", None), P(), P("lines", None), P())
    return jax.shard_map(
        body,
        mesh=mesh,
        in_specs=placed,
        out_specs=P("groups", None, None, "lines"),
        check_vma=False,
    )
```

```python
import math

import jax
import jax.numpy as jnp
import numpy as np
from jax import lax
from jax.experimental import pallas as pl
from jax.experimental.pallas import tpu as pltpu
from jax.sharding import PartitionSpec as P

ML_RG = 4
ML_AZ = 2
PATCH = 32
HALF = PATCH // 2
BOX_FLOOR = 0.25
LEVEL_FLOOR = 1e-06
SUB = 8
LANES = 128
VMEM_BYTES = 48 * 1024 * 1024


def real_block(table):
    return np.block([[table.real, table.imag], [-table.imag, table.real]])


def wave(rows, cols, period, direction):
    product = np.asarray(rows)[:, None] * np.asarray(cols)[None, :] % period
    return np.exp(direction * 2j * math.pi / period * product)


def as_bf16(table):
    return jnp.asarray(np.asarray(table, np.float32), jnp.bfloat16)


def line_order(line_len):
    return np.arange(line_len).reshape(line_len // ML_AZ, ML_AZ).T.reshape(-1)


def small_dft(parts, direction):
    count = len(parts)
    if count == 1:
        return parts
    even = small_dft(parts[0::2], direction)
    odd = small_dft(parts[1::2], direction)
    low, high = [], []
    for k in range(count // 2):
        (er, ei), (vr, vi) = even[k], odd[k]
        if k == 0:
            tr, ti = vr, vi
        elif 4 * k == count:
            if direction < 0:
                tr, ti = vi, -vr
            else:
                tr, ti = -vi, vr
        elif 8 * k == count:
            s = math.sqrt(0.5)
            if direction < 0:
                tr, ti = (vr + vi) * s, (vi - vr) * s
            else:
                tr, ti = (vr - vi) * s, (vi + vr) * s
        elif 8 * k == 3 * count:
            s = math.sqrt(0.5)
            if direction < 0:
                tr, ti = (vi - vr) * s, -(vr + vi) * s
            else:
                tr, ti = -(vr + vi) * s, (vr - vi) * s
        else:
            c = math.cos(2 * math.pi * k / count)
            s = direction * math.sin(2 * math.pi * k / count)
            tr, ti = vr * c - vi * s, vr * s + vi * c
        low.append((er + tr, ei + ti))
        high.append((er - tr, ei - ti))
    return low + high


def compress_kernel(
    shape, raw_hbm, filter_hbm, out_ref, raw_ref, filter_ref, wide_ref, raw_sems, filter_sem
):
    chunk, dates, step, targets, tiles, gates, lines = shape
    looks_rows = gates // ML_RG
    gates_in = raw_ref.shape[3]
    copies = [
        pltpu.make_async_copy(
            raw_hbm.at[pl.ds(first, step)], raw_ref.at[pl.ds(first, step)], raw_sems.at[first // step]
        )
        for first in range(0, dates, step)
    ]
    filter_copy = pltpu.make_async_copy(filter_hbm.at[:, :, chunk], filter_ref, filter_sem)
    filter_copy.start()
    for copy in copies:
        copy.start()
    filter_copy.wait()
    weight = [filter_ref[part].reshape(targets * gates, gates_in) for part in (0, 1)]

    def product(w, x):
        return lax.dot_general(
            w, x, (((1,), (1,)), ((), ())), preferred_element_type=jnp.float32
        )

    for first in range(0, dates, step):
        copies[first // step].wait()
        raw = [
            raw_ref[first : first + step, part].reshape(step * lines, gates_in) for part in (0, 1)
        ]
        real = product(weight[0], raw[0]) - product(weight[1], raw[1])
        imag = product(weight[1], raw[0]) + product(weight[0], raw[1])
        for at in range(step):
            wide_ref[first + at, 0] = real[:, at * lines : (at + 1) * lines]
            wide_ref[first + at, 1] = imag[:, at * lines : (at + 1) * lines]
        for target in range(targets):
            for date in range(first, first + step):
                for tile in range(tiles):
                    rows = []
                    for part in (0, 1):
                        begin, count = tile * SUB, min(looks_rows, SUB)
                        for at in range(begin, begin + SUB, count):
                            gate = target * gates + at // looks_rows + ML_RG * (at % looks_rows)
                            rows.append(wide_ref[date, part, pl.ds(gate, count, stride=ML_RG), :])
                    out_ref[target, date, tile] = jnp.concatenate(rows, axis=0).astype(
                        jnp.bfloat16
                    )


def compress(raw_echo, filter_chunks, chunk):
    dates, _, lines, gates_in = raw_echo.shape
    _, targets, _, gates, _ = filter_chunks.shape
    tiles = gates // SUB
    step = 2 if dates % 2 == 0 else 1
    shape = (chunk, dates, step, targets, tiles, gates, lines)
    hbm = pl.BlockSpec(memory_space=pltpu.HBM)
    return pl.pallas_call(
        lambda *refs: compress_kernel(shape, *refs),
        out_shape=jax.ShapeDtypeStruct((targets, dates, tiles, 2 * SUB, lines), jnp.bfloat16),
        in_specs=[hbm, hbm],
        out_specs=pl.BlockSpec(memory_space=pltpu.VMEM),
        scratch_shapes=[
            pltpu.VMEM(raw_echo.shape, jnp.bfloat16),
            pltpu.VMEM((2, targets, gates, gates_in), jnp.bfloat16),
            pltpu.VMEM((dates, 2, targets * gates, lines), jnp.float32),
            pltpu.SemaphoreType.DMA((dates // step,)),
            pltpu.SemaphoreType.DMA,
        ],
        compiler_params=pltpu.CompilerParams(vmem_limit_bytes=VMEM_BYTES),
        cost_estimate=pl.CostEstimate(
            flops=8 * dates * lines * targets * gates * gates_in,
            bytes_accessed=4 * (raw_echo.size + targets * gates * gates_in),
            transcendentals=0,
        ),
        name="compress",
    )(raw_echo, filter_chunks)


def focus_kernel(
    shape, offset_ref, data_ref, cos_ref, sin_ref, turn_ref, fwd_ref, back_ref, out_ref, image_ref,
    look_ref,
):
    chunk, dates, blocks, tiles, gates, lines = shape
    looks_rows = gates // ML_RG
    look_lines = lines // ML_AZ
    for date in range(dates):
        for tile in range(tiles):
            parts = []
            for a in range(blocks):
                both = data_ref[a, date, tile].astype(jnp.float32)
                parts.append((both[:SUB], both[SUB:]))
            parts = small_dft(parts, -1)
            turned = []
            for a, (re, im) in enumerate(parts):
                tr, ti = turn_ref[0, a : a + 1], turn_ref[1, a : a + 1]
                turned.append((re * tr - im * ti, re * ti + im * tr))
            rows = jnp.concatenate(
                [jnp.concatenate([re, im], axis=1) for re, im in turned], axis=0
            ).astype(jnp.bfloat16)
            spectrum = jnp.dot(rows, fwd_ref[...], preferred_element_type=jnp.float32)
            re, im = spectrum[:, :lines], spectrum[:, lines:]
            pr, pi = cos_ref[chunk, tile], sin_ref[chunk, tile]
            rows = jnp.concatenate([re * pr - im * pi, re * pi + im * pr], axis=1).astype(
                jnp.bfloat16
            )
            back = jnp.dot(rows, back_ref[...], preferred_element_type=jnp.float32)
            parts = []
            for a in range(blocks):
                re = back[a * SUB : (a + 1) * SUB, :lines]
                im = back[a * SUB : (a + 1) * SUB, lines:]
                tr, ti = turn_ref[2, a : a + 1], turn_ref[3, a : a + 1]
                parts.append((re * tr - im * ti, re * ti + im * tr))
            parts = small_dft(parts, 1)
            for a, (re, im) in enumerate(parts):
                image_ref[date, tile, a, 0] = re
                image_ref[date, tile, a, 1] = im

    lane = lax.broadcasted_iota(jnp.int32, (SUB, lines), 1)
    first = lane < look_lines
    scale = 1.0 / (ML_RG * ML_AZ)
    for date in range(dates):
        partner = lax.rem(date + offset_ref[date], dates)
        for a in range(blocks):
            sums = {}
            for tile in range(tiles):
                cr, ci = image_ref[date, tile, a, 0], image_ref[date, tile, a, 1]
                pr, pi = image_ref[partner, tile, a, 0], image_ref[partner, tile, a, 1]
                re, im = cr * pr + ci * pi, ci * pr - cr * pi
                at = tile * SUB % looks_rows
                if at in sums:
                    re, im = re + sums[at][0], im + sums[at][1]
                sums[at] = (re, im)
            for at, (re, im) in sums.items():
                look = jnp.where(first, re, im) + pltpu.roll(
                    jnp.where(first, im, re), look_lines, 1
                )
                step = SUB
                while step > looks_rows:
                    step //= 2
                    look = look + pltpu.roll(look, step, 0)
                count = min(SUB, looks_rows)
                row = date * looks_rows + at
                look_ref[a, row : row + count, :] = (look * scale)[:count]

    small = lax.broadcasted_iota(jnp.int32, (looks_rows, lines), 1) % look_lines
    from_high, from_low = small < HALF, small >= look_lines - HALF
    zero = jnp.zeros((looks_rows, lines), jnp.float32)

    def rim(a, date):
        rows = slice(date * looks_rows, (date + 1) * looks_rows)
        high = look_ref[a + 1, rows, :] if a + 1 < blocks else zero
        low = look_ref[a - 1, rows, :] if a > 0 else zero
        return jnp.where(from_high, high, low)

    for a in range(blocks):
        for date in range(0, dates, 2):
            own = rim(a, date)
            other = pltpu.roll(rim(a, date + 1), look_lines // 2, 1)
            row = (dates + date // 2) * looks_rows
            look_ref[a, row : row + looks_rows, :] = jnp.where(from_high | from_low, own, other)
    out_ref[...] = look_ref[...].astype(jnp.bfloat16)


def phase_tables(azimuth_phase, chunks, blocks):
    gates, total = azimuth_phase.shape
    looks_rows = gates // chunks // ML_RG
    lines = total // blocks
    tiles = gates // chunks // SUB
    phase = azimuth_phase.reshape(chunks, looks_rows, ML_RG, lines, blocks)
    phase = phase.transpose(0, 2, 1, 4, 3).reshape(chunks, tiles, SUB, blocks, lines)
    phase = phase.transpose(0, 1, 3, 2, 4).reshape(chunks, tiles, blocks * SUB, lines)
    phase = lax.optimization_barrier(phase)
    return jnp.cos(phase), jnp.sin(phase)


def focus_tables(blocks, lines):
    total = blocks * lines
    order = line_order(lines)
    ahead = wave(np.arange(blocks), np.arange(lines), total, -1)
    behind = wave(np.arange(blocks), order, total, 1)
    turn = np.stack([ahead.real, ahead.imag, behind.real, behind.imag]).astype(np.float32)
    fwd = as_bf16(real_block(wave(np.arange(lines), np.arange(lines), lines, -1)))
    back = as_bf16(real_block(wave(np.arange(lines), order, lines, 1) / total))
    return jnp.asarray(turn), fwd, back


def focus(columns, pair_offset, phases, tables, chunk):
    blocks, dates, tiles, _, lines = columns.shape
    gates = tiles * SUB
    looks_rows = gates // ML_RG
    slots = dates + dates // 2
    shape = (chunk, dates, blocks, tiles, gates, lines)
    whole = pl.BlockSpec(memory_space=pltpu.VMEM)
    return pl.pallas_call(
        lambda *refs: focus_kernel(shape, *refs),
        out_shape=jax.ShapeDtypeStruct((blocks, slots * looks_rows, lines), jnp.bfloat16),
        in_specs=[pl.BlockSpec(memory_space=pltpu.SMEM)] + [whole] * 6,
        out_specs=whole,
        scratch_shapes=[
            pltpu.VMEM((dates, tiles, blocks, 2, SUB, lines), jnp.float32),
            pltpu.VMEM((blocks, slots * looks_rows, lines), jnp.float32),
        ],
        compiler_params=pltpu.CompilerParams(vmem_limit_bytes=VMEM_BYTES),
        cost_estimate=pl.CostEstimate(
            flops=16 * dates * gates * blocks * lines * lines,
            bytes_accessed=4 * columns.size,
            transcendentals=0,
        ),
        name="focus",
    )(pair_offset, columns, *phases, *tables)


def tri_window(offset):
    inside = (offset >= 0) & (offset < PATCH)
    return np.where(inside, 1.0 - np.abs(offset - (PATCH - 1) / 2.0) / HALF, 0.0)


def patch_tables(cells, starts):
    offset = np.asarray(cells)[:, None] - np.asarray(starts)[None, :]
    inside = ((offset >= 0) & (offset < PATCH)).astype(np.float64)
    angle = 2.0 * math.pi / PATCH * (offset[:, :, None] * np.arange(PATCH) % PATCH)
    ahead = np.exp(-1j * angle) * inside[:, :, None]
    behind = np.exp(1j * angle) * tri_window(offset)[:, :, None] / PATCH
    flat = (len(cells), len(starts) * PATCH)
    return ahead.reshape(flat), behind.reshape(flat).T


def goldstein_tables(dates, gate_order, line_looks):
    per = LANES // PATCH
    starts = np.arange(-HALF, line_looks, HALF)
    cells = np.arange(-HALF, line_looks + HALF)
    ahead, behind = patch_tables(cells, starts)
    main = slice(HALF, HALF + line_looks)
    behind = behind[:, main]
    split = per * PATCH

    def lanes_of(table, shift):
        block = np.zeros((2, line_looks, table.shape[1]), complex)
        block[0], block[1] = table[main], 1j * table[main]
        rim = np.zeros((2, line_looks, table.shape[1]), complex)
        for part, turn in enumerate((1.0, 1j)):
            rim[part, :HALF] = turn * table[HALF + line_looks :]
            rim[part, line_looks - HALF :] = turn * table[:HALF]
        flat = (2 * line_looks, table.shape[1])
        return block.reshape(flat), np.roll(rim.reshape(flat), shift, axis=0)

    def out_parts(table):
        return np.concatenate([table.real, table.imag], axis=1)

    near = [
        out_parts(np.concatenate(lanes_of(ahead[:, :split], parity * (line_looks // 2))))
        for parity in (0, 1)
    ]
    rest = ahead.shape[1] - split
    far_block = np.zeros((dates, 2 * line_looks, dates, rest), complex)
    far_rim = np.zeros((dates // 2, 2 * line_looks, dates, rest), complex)
    for date in range(dates):
        block, rim = lanes_of(ahead[:, split:], date % 2 * (line_looks // 2))
        far_block[date, :, date] = block
        far_rim[date // 2, :, date] = rim
    far = np.concatenate([far_block, far_rim]).reshape(-1, dates * rest)
    gate_starts = np.arange(-HALF, len(gate_order), HALF)
    gate_ahead, gate_behind = patch_tables(np.arange(len(gate_order)), gate_starts)
    ahead_rows = real_block(gate_ahead[gate_order]).T
    behind_rows = real_block(gate_behind).T

    lines_back = []
    for date in range(dates):
        far_back = np.zeros((dates, rest, line_looks), complex)
        far_back[date] = behind[split:]
        lines_back.append(
            np.concatenate(
                [real_block(behind[:split]), real_block(far_back.reshape(-1, line_looks))]
            ).T
        )
    gap = (np.arange(PATCH)[:, None] - np.arange(PATCH)[None, :]) % PATCH
    ring = ((gap == 0) | (gap == 1) | (gap == PATCH - 1)).astype(np.float64)
    box = np.concatenate(
        [np.kron(np.eye(per), ring), np.kron(np.eye(per), np.ones((PATCH, PATCH)))], axis=1
    )
    tables = (np.stack(near), out_parts(far), ahead_rows, box, behind_rows, np.stack(lines_back))
    return [as_bf16(table) for table in tables]


def slot_rows(data_ref, slots, looks_rows):
    blocks = data_ref.shape[0]
    data = data_ref[...].astype(jnp.float32)
    if looks_rows % SUB == 0:
        return [
            data[:, slot * looks_rows : (slot + 1) * looks_rows].reshape(-1, LANES)
            for slot in range(slots)
        ]
    top = lax.broadcasted_iota(jnp.int32, (SUB, LANES), 0) < looks_rows
    held = [[] for _ in range(slots)]
    for block in range(0, blocks, 2):
        for slot in range(0, slots, 2):
            rows = slice(slot * looks_rows, (slot + 2) * looks_rows)
            one, two = data[block, rows], data[block + 1, rows]
            held[slot].append(jnp.where(top, one, pltpu.roll(two, looks_rows, 0)))
            held[slot + 1].append(jnp.where(top, pltpu.roll(one, looks_rows, 0), two))
    return [jnp.concatenate(rows, axis=0) for rows in held]


def goldstein_kernel(shape, *refs):
    dates, chunks, looks_rows, gate_looks, line_looks = shape
    data_refs, refs = refs[:chunks], refs[chunks:]
    near_ref, far_ref, ahead_ref, box_ref, behind_ref, back_ref, out_ref = refs[:7]
    half_ref, spec_ref, weighted_ref = refs[7:]
    slots = dates + dates // 2
    cols = dates + 1
    dot = lambda a, b: jnp.dot(a, b, preferred_element_type=jnp.float32)
    if data_refs[0].shape[0] == slots:
        held = [data_refs[0][slot] for slot in range(slots)]
    else:
        held = zip(*[slot_rows(ref, slots, looks_rows) for ref in data_refs])
        held = [jnp.concatenate(rows, axis=0).astype(jnp.bfloat16) for rows in held]
    for parity in (0, 1):
        rows = jnp.concatenate(
            [
                jnp.concatenate([held[date], held[dates + date // 2]], axis=1)
                for date in range(parity, dates, 2)
            ],
            axis=0,
        )
        both = dot(rows, near_ref[parity]).astype(jnp.bfloat16)
        for index, date in enumerate(range(parity, dates, 2)):
            mine = both[index * gate_looks : (index + 1) * gate_looks]
            half_ref[:gate_looks, date * LANES : (date + 1) * LANES] = mine[:, :LANES]
            half_ref[gate_looks:, date * LANES : (date + 1) * LANES] = mine[:, LANES:]
    both = dot(jnp.concatenate(held, axis=1), far_ref[...]).astype(jnp.bfloat16)
    half_ref[:gate_looks, dates * LANES :] = both[:, :LANES]
    half_ref[gate_looks:, dates * LANES :] = both[:, LANES:]

    spec_ref[...] = dot(ahead_ref[...], half_ref[...])
    bins = ahead_ref.shape[0] // 2
    for col in range(cols):
        lanes = slice(col * LANES, (col + 1) * LANES)
        re, im = spec_ref[:bins, lanes], spec_ref[bins:, lanes]
        power = (re * re + im * im).astype(jnp.bfloat16)
        sums = dot(power, box_ref[...])
        for start in range(0, bins, PATCH):
            rows = slice(start, start + PATCH)
            line = sums[rows, :LANES]
            total = jnp.sum(sums[rows, LANES:], axis=0, keepdims=True)
            smooth = line + pltpu.roll(line, 1, 0) + pltpu.roll(line, PATCH - 1, 0)
            level = total * (1.0 / (PATCH * PATCH)) + LEVEL_FLOOR
            weight = jnp.sqrt(smooth * (1.0 / (9.0 * level)) + BOX_FLOOR)
            weighted_ref[rows, lanes] = (re[rows] * weight).astype(jnp.bfloat16)
            weighted_ref[start + bins : start + bins + PATCH, lanes] = (im[rows] * weight).astype(
                jnp.bfloat16
            )
    inverse = dot(behind_ref[...], weighted_ref[...]).astype(jnp.bfloat16)
    far = [inverse[:gate_looks, dates * LANES :], inverse[gate_looks:, dates * LANES :]]
    for date in range(dates):
        lanes = slice(date * LANES, (date + 1) * LANES)
        rows = jnp.concatenate([inverse[:gate_looks, lanes], inverse[gate_looks:, lanes]] + far, axis=1)
        result = lax.dot_general(
            back_ref[date], rows, (((1,), (1,)), ((), ())), preferred_element_type=jnp.float32
        )
        out_ref[date, 0] = result[:line_looks]
        out_ref[date, 1] = result[line_looks:]


def goldstein(looks, dates, line_looks):
    chunks = len(looks)
    blocks, rows, _ = looks[0].shape
    slots = dates + dates // 2
    looks_rows = rows // slots
    gate_looks = chunks * blocks * looks_rows
    order = np.arange(gate_looks).reshape(blocks, chunks, looks_rows).swapaxes(0, 1).reshape(-1)
    if looks_rows % SUB and 2 * looks_rows != SUB:
        looks = [
            each.reshape(blocks, slots, looks_rows, LANES)
            .swapaxes(0, 1)
            .reshape(slots, blocks * looks_rows, LANES)
            for each in looks
        ]
        looks = [jnp.concatenate(looks, axis=1)]
    tables = goldstein_tables(dates, order, line_looks)
    bins = tables[2].shape[0] // 2
    width = (dates + 1) * LANES
    shape = (dates, len(looks), looks_rows, gate_looks, line_looks)
    whole = pl.BlockSpec(memory_space=pltpu.VMEM)
    filtered = pl.pallas_call(
        lambda *refs: goldstein_kernel(shape, *refs),
        out_shape=jax.ShapeDtypeStruct((dates, 2, line_looks, gate_looks), jnp.float32),
        in_specs=[whole] * (len(looks) + len(tables)),
        out_specs=whole,
        scratch_shapes=[
            pltpu.VMEM((2 * gate_looks, width), jnp.bfloat16),
            pltpu.VMEM((2 * bins, width), jnp.float32),
            pltpu.VMEM((2 * bins, width), jnp.bfloat16),
        ],
        compiler_params=pltpu.CompilerParams(vmem_limit_bytes=VMEM_BYTES),
        name="goldstein",
    )(*looks, *tables)
    return filtered.swapaxes(2, 3)


def body(raw_echo, range_filter, azimuth_phase, pair_offset):
    dates, _, lines, gates_in = raw_echo.shape
    devices = lax.axis_size("lines")
    gates = azimuth_phase.shape[0]
    chunks = 2 if gates % (4 * SUB) == 0 else 1
    filter_chunks = range_filter.reshape(2, devices, chunks, gates // chunks, gates_in)
    phases = phase_tables(azimuth_phase, chunks, devices)
    tables = focus_tables(devices, lines)

    def exchange(blocks):
        return lax.all_to_all(blocks, "lines", split_axis=0, concat_axis=0, tiled=True)

    columns = [exchange(compress(raw_echo, filter_chunks, chunk)) for chunk in range(chunks)]
    looks = [
        exchange(focus(columns[chunk], pair_offset, phases, tables, chunk))
        for chunk in range(chunks)
    ]
    return goldstein(looks, dates, lines // ML_AZ)


def solution(mesh):
    placed = (P("groups", None, "lines", None), P(), P("lines", None), P())
    return jax.shard_map(
        body,
        mesh=mesh,
        in_specs=placed,
        out_specs=P("groups", None, None, "lines"),
        check_vma=False,
    )
```

```python
import math

import jax
import jax.numpy as jnp
import numpy as np
from jax import lax
from jax.experimental import pallas as pl
from jax.experimental.pallas import tpu as pltpu
from jax.sharding import PartitionSpec as P

ML_RG = 4
ML_AZ = 2
PATCH = 32
HALF = PATCH // 2
BOX_FLOOR = 0.25
LEVEL_FLOOR = 1e-06
SUB = 8
LANES = 128
VMEM_BYTES = 32 * 1024 * 1024


def real_block(table):
    return np.block([[table.real, table.imag], [-table.imag, table.real]])


def wave(rows, cols, period, direction):
    product = np.asarray(rows)[:, None] * np.asarray(cols)[None, :] % period
    return np.exp(direction * 2j * math.pi / period * product)


def as_bf16(table):
    return jnp.asarray(np.asarray(table, np.float32), jnp.bfloat16)


def line_order(line_len):
    return np.arange(line_len).reshape(line_len // ML_AZ, ML_AZ).T.reshape(-1)


def small_dft(parts, direction):
    count = len(parts)
    if count == 1:
        return parts
    even = small_dft(parts[0::2], direction)
    odd = small_dft(parts[1::2], direction)
    low, high = [], []
    for k in range(count // 2):
        (er, ei), (vr, vi) = even[k], odd[k]
        if k == 0:
            tr, ti = vr, vi
        elif 4 * k == count:
            if direction < 0:
                tr, ti = vi, -vr
            else:
                tr, ti = -vi, vr
        elif 8 * k == count:
            s = math.sqrt(0.5)
            if direction < 0:
                tr, ti = (vr + vi) * s, (vi - vr) * s
            else:
                tr, ti = (vr - vi) * s, (vi + vr) * s
        elif 8 * k == 3 * count:
            s = math.sqrt(0.5)
            if direction < 0:
                tr, ti = (vi - vr) * s, -(vr + vi) * s
            else:
                tr, ti = -(vr + vi) * s, (vr - vi) * s
        else:
            c = math.cos(2 * math.pi * k / count)
            s = direction * math.sin(2 * math.pi * k / count)
            tr, ti = vr * c - vi * s, vr * s + vi * c
        low.append((er + tr, ei + ti))
        high.append((er - tr, ei - ti))
    return low + high


def compress_kernel(shape, raw_hbm, filter_hbm, *refs):
    region, dates, step, devices, gates, lines = shape
    count = devices // 2
    tiles, looks_rows = gates // SUB, gates // ML_RG
    out_refs, refs = refs[:-5], refs[-5:]
    raw_ref, filter_ref, wide_ref, raw_sems, filter_sem = refs
    gates_in = raw_ref.shape[3]
    me = lax.axis_index("lines")
    half = me // count if region == 0 else 1 - me // count
    copies = [
        pltpu.make_async_copy(
            raw_hbm.at[pl.ds(first, step)], raw_ref.at[pl.ds(first, step)], raw_sems.at[first // step]
        )
        for first in range(0, dates, step)
    ]
    filter_copy = pltpu.make_async_copy(
        filter_hbm.at[:, pl.ds(pl.multiple_of(half * count * gates, count * gates), count * gates)],
        filter_ref,
        filter_sem,
    )
    filter_copy.start()
    for copy in copies:
        copy.start()
    filter_copy.wait()

    def product(w, x):
        return lax.dot_general(
            w, x, (((1,), (1,)), ((), ())), preferred_element_type=jnp.float32
        )

    for first in range(0, dates, step):
        copies[first // step].wait()
        raw = [
            raw_ref[first : first + step, part].reshape(step * lines, gates_in) for part in (0, 1)
        ]
        real = product(filter_ref[0], raw[0]) - product(filter_ref[1], raw[1])
        imag = product(filter_ref[1], raw[0]) + product(filter_ref[0], raw[1])
        for at in range(step):
            wide_ref[first + at, 0] = real[:, at * lines : (at + 1) * lines]
            wide_ref[first + at, 1] = imag[:, at * lines : (at + 1) * lines]
        for index in range(count):
            base = pl.multiple_of((me % count ^ index) * gates, gates)
            for date in range(first, first + step):
                for tile in range(tiles):
                    rows = []
                    for part in (0, 1):
                        begin, run = tile * SUB, min(looks_rows, SUB)
                        for at in range(begin, begin + SUB, run):
                            gate = base + at // looks_rows + ML_RG * (at % looks_rows)
                            rows.append(wide_ref[date, part, pl.ds(gate, run, stride=ML_RG), :])
                    tile_rows = jnp.concatenate(rows, axis=0).astype(jnp.bfloat16)
                    if len(out_refs) == 1:
                        out_refs[0][index, date, tile] = tile_rows
                    else:
                        out_refs[index][date, tile] = tile_rows


def compress(raw_echo, range_filter, devices, region, after=None):
    dates, _, lines, gates_in = raw_echo.shape
    gates = range_filter.shape[1] // devices
    count = devices // 2
    tiles = gates // SUB
    step = 2 if dates % 2 == 0 else 1
    shape = (region, dates, step, devices, gates, lines)
    hbm = pl.BlockSpec(memory_space=pltpu.HBM)
    block = (dates, tiles, 2 * SUB, lines)
    operands = [pltpu.with_memory_space_constraint(x, pltpu.HBM) for x in (raw_echo, range_filter)]
    extra = [] if after is None else [after]

    def kernel(raw_hbm, filter_hbm, *refs):
        compress_kernel(shape, raw_hbm, filter_hbm, *refs[len(extra) :])

    return pl.pallas_call(
        kernel,
        out_shape=[jax.ShapeDtypeStruct(block, jnp.bfloat16)] * count,
        in_specs=[hbm, hbm] + [pl.BlockSpec(memory_space=pl.ANY)] * len(extra),
        out_specs=[pl.BlockSpec(memory_space=pltpu.VMEM)] * count,
        scratch_shapes=[
            pltpu.VMEM(raw_echo.shape, jnp.bfloat16),
            pltpu.VMEM((2, count * gates, gates_in), jnp.bfloat16),
            pltpu.VMEM((dates, 2, count * gates, lines), jnp.float32),
            pltpu.SemaphoreType.DMA((dates // step,)),
            pltpu.SemaphoreType.DMA,
        ],
        compiler_params=pltpu.CompilerParams(vmem_limit_bytes=VMEM_BYTES),
        cost_estimate=pl.CostEstimate(
            flops=8 * dates * lines * count * gates * gates_in,
            bytes_accessed=4 * (raw_echo.size + count * gates * gates_in),
            transcendentals=0,
        ),
        name="compress",
    )(*operands, *extra)


def focus_kernel(shape, offset_ref, cos_ref, sin_ref, turn_ref, fwd_ref, back_ref, *refs):
    dates, blocks, tiles, gates, lines = shape
    block_refs, (out_ref, data_ref, image_ref, look_ref) = refs[:blocks], refs[blocks:]
    me = lax.axis_index("lines")
    for index, block_ref in enumerate(block_refs):
        data_ref[me ^ index] = block_ref[...]
    looks_rows = gates // ML_RG
    look_lines = lines // ML_AZ
    for date in range(dates):
        for tile in range(tiles):
            parts = []
            for a in range(blocks):
                both = data_ref[a, date, tile].astype(jnp.float32)
                parts.append((both[:SUB], both[SUB:]))
            parts = small_dft(parts, -1)
            turned = []
            for a, (re, im) in enumerate(parts):
                tr, ti = turn_ref[0, a : a + 1], turn_ref[1, a : a + 1]
                turned.append((re * tr - im * ti, re * ti + im * tr))
            rows = jnp.concatenate(
                [jnp.concatenate([re, im], axis=1) for re, im in turned], axis=0
            ).astype(jnp.bfloat16)
            spectrum = jnp.dot(rows, fwd_ref[...], preferred_element_type=jnp.float32)
            re, im = spectrum[:, :lines], spectrum[:, lines:]
            pr, pi = cos_ref[tile], sin_ref[tile]
            rows = jnp.concatenate([re * pr - im * pi, re * pi + im * pr], axis=1).astype(
                jnp.bfloat16
            )
            back = jnp.dot(rows, back_ref[...], preferred_element_type=jnp.float32)
            parts = []
            for a in range(blocks):
                re = back[a * SUB : (a + 1) * SUB, :lines]
                im = back[a * SUB : (a + 1) * SUB, lines:]
                tr, ti = turn_ref[2, a : a + 1], turn_ref[3, a : a + 1]
                parts.append((re * tr - im * ti, re * ti + im * tr))
            parts = small_dft(parts, 1)
            for a, (re, im) in enumerate(parts):
                image_ref[date, tile, a, 0] = re
                image_ref[date, tile, a, 1] = im

    lane = lax.broadcasted_iota(jnp.int32, (SUB, lines), 1)
    first = lane < look_lines
    scale = 1.0 / (ML_RG * ML_AZ)
    for date in range(dates):
        partner = lax.rem(date + offset_ref[date], dates)
        for a in range(blocks):
            sums = {}
            for tile in range(tiles):
                cr, ci = image_ref[date, tile, a, 0], image_ref[date, tile, a, 1]
                pr, pi = image_ref[partner, tile, a, 0], image_ref[partner, tile, a, 1]
                re, im = cr * pr + ci * pi, ci * pr - cr * pi
                at = tile * SUB % looks_rows
                if at in sums:
                    re, im = re + sums[at][0], im + sums[at][1]
                sums[at] = (re, im)
            for at, (re, im) in sums.items():
                look = jnp.where(first, re, im) + pltpu.roll(
                    jnp.where(first, im, re), look_lines, 1
                )
                step = SUB
                while step > looks_rows:
                    step //= 2
                    look = look + pltpu.roll(look, step, 0)
                count = min(SUB, looks_rows)
                row = date * looks_rows + at
                look_ref[a, row : row + count, :] = (look * scale)[:count]

    small = lax.broadcasted_iota(jnp.int32, (looks_rows, lines), 1) % look_lines
    from_high, from_low = small < HALF, small >= look_lines - HALF
    zero = jnp.zeros((looks_rows, lines), jnp.float32)

    def rim(a, date):
        rows = slice(date * looks_rows, (date + 1) * looks_rows)
        high = look_ref[a + 1, rows, :] if a + 1 < blocks else zero
        low = look_ref[a - 1, rows, :] if a > 0 else zero
        return jnp.where(from_high, high, low)

    for a in range(blocks):
        for date in range(0, dates, 2):
            own = rim(a, date)
            other = pltpu.roll(rim(a, date + 1), look_lines // 2, 1)
            row = (dates + date // 2) * looks_rows
            look_ref[a, row : row + looks_rows, :] = jnp.where(from_high | from_low, own, other)
    out_ref[...] = look_ref[...].astype(jnp.bfloat16)


def phase_tables(azimuth_phase, blocks):
    gates, total = azimuth_phase.shape
    looks_rows = gates // ML_RG
    lines = total // blocks
    tiles = gates // SUB
    phase = azimuth_phase.reshape(looks_rows, ML_RG, lines, blocks)
    phase = phase.transpose(1, 0, 3, 2).reshape(tiles, SUB, blocks, lines)
    phase = phase.transpose(0, 2, 1, 3).reshape(tiles, blocks * SUB, lines)
    phase = lax.optimization_barrier(phase)
    return jnp.cos(phase), jnp.sin(phase)


def focus_tables(blocks, lines):
    total = blocks * lines
    order = line_order(lines)
    ahead = wave(np.arange(blocks), np.arange(lines), total, -1)
    behind = wave(np.arange(blocks), order, total, 1)
    turn = np.stack([ahead.real, ahead.imag, behind.real, behind.imag]).astype(np.float32)
    fwd = as_bf16(real_block(wave(np.arange(lines), np.arange(lines), lines, -1)))
    back = as_bf16(real_block(wave(np.arange(lines), order, lines, 1) / total))
    return jnp.asarray(turn), fwd, back


def focus(columns, pair_offset, phases, tables):
    blocks = len(columns)
    dates, tiles, _, lines = columns[0].shape
    gates = tiles * SUB
    looks_rows = gates // ML_RG
    slots = dates + dates // 2
    shape = (dates, blocks, tiles, gates, lines)
    whole = pl.BlockSpec(memory_space=pltpu.VMEM)
    return pl.pallas_call(
        lambda *refs: focus_kernel(shape, *refs),
        out_shape=jax.ShapeDtypeStruct((blocks, slots * looks_rows, lines), jnp.bfloat16),
        in_specs=[pl.BlockSpec(memory_space=pltpu.SMEM)] + [whole] * (5 + blocks),
        out_specs=whole,
        scratch_shapes=[
            pltpu.VMEM((blocks, dates, tiles, 2 * SUB, lines), jnp.bfloat16),
            pltpu.VMEM((dates, tiles, blocks, 2, SUB, lines), jnp.float32),
            pltpu.VMEM((blocks, slots * looks_rows, lines), jnp.float32),
        ],
        compiler_params=pltpu.CompilerParams(vmem_limit_bytes=VMEM_BYTES),
        cost_estimate=pl.CostEstimate(
            flops=16 * dates * gates * blocks * lines * lines,
            bytes_accessed=4 * blocks * columns[0].size,
            transcendentals=0,
        ),
        name="focus",
    )(pair_offset, *phases, *tables, *columns)


def tri_window(offset):
    inside = (offset >= 0) & (offset < PATCH)
    return np.where(inside, 1.0 - np.abs(offset - (PATCH - 1) / 2.0) / HALF, 0.0)


def patch_tables(cells, starts):
    offset = np.asarray(cells)[:, None] - np.asarray(starts)[None, :]
    inside = ((offset >= 0) & (offset < PATCH)).astype(np.float64)
    angle = 2.0 * math.pi / PATCH * (offset[:, :, None] * np.arange(PATCH) % PATCH)
    ahead = np.exp(-1j * angle) * inside[:, :, None]
    behind = np.exp(1j * angle) * tri_window(offset)[:, :, None] / PATCH
    flat = (len(cells), len(starts) * PATCH)
    return ahead.reshape(flat), behind.reshape(flat).T


def goldstein_tables(dates, gate_order, line_looks):
    per = LANES // PATCH
    starts = np.arange(-HALF, line_looks, HALF)
    cells = np.arange(-HALF, line_looks + HALF)
    ahead, behind = patch_tables(cells, starts)
    main = slice(HALF, HALF + line_looks)
    behind = behind[:, main]
    split = per * PATCH

    def lanes_of(table, shift):
        block = np.zeros((2, line_looks, table.shape[1]), complex)
        block[0], block[1] = table[main], 1j * table[main]
        rim = np.zeros((2, line_looks, table.shape[1]), complex)
        for part, turn in enumerate((1.0, 1j)):
            rim[part, :HALF] = turn * table[HALF + line_looks :]
            rim[part, line_looks - HALF :] = turn * table[:HALF]
        flat = (2 * line_looks, table.shape[1])
        return block.reshape(flat), np.roll(rim.reshape(flat), shift, axis=0)

    def out_parts(table):
        return np.concatenate([table.real, table.imag], axis=1)

    near = [
        out_parts(np.concatenate(lanes_of(ahead[:, :split], parity * (line_looks // 2))))
        for parity in (0, 1)
    ]
    rest = ahead.shape[1] - split
    far_block = np.zeros((dates, 2 * line_looks, dates, rest), complex)
    far_rim = np.zeros((dates // 2, 2 * line_looks, dates, rest), complex)
    for date in range(dates):
        block, rim = lanes_of(ahead[:, split:], date % 2 * (line_looks // 2))
        far_block[date, :, date] = block
        far_rim[date // 2, :, date] = rim
    far = np.concatenate([far_block, far_rim]).reshape(-1, dates * rest)
    gate_starts = np.arange(-HALF, len(gate_order), HALF)
    gate_ahead, gate_behind = patch_tables(np.arange(len(gate_order)), gate_starts)
    ahead_rows = real_block(gate_ahead[gate_order]).T
    behind_rows = real_block(gate_behind).T

    lines_back = []
    for date in range(dates):
        far_back = np.zeros((dates, rest, line_looks), complex)
        far_back[date] = behind[split:]
        lines_back.append(
            np.concatenate(
                [real_block(behind[:split]), real_block(far_back.reshape(-1, line_looks))]
            ).T
        )
    gap = (np.arange(PATCH)[:, None] - np.arange(PATCH)[None, :]) % PATCH
    ring = ((gap == 0) | (gap == 1) | (gap == PATCH - 1)).astype(np.float64)
    box = np.concatenate(
        [np.kron(np.eye(per), ring), np.kron(np.eye(per), np.ones((PATCH, PATCH)))], axis=1
    )
    tables = (np.stack(near), out_parts(far), ahead_rows, box, behind_rows, np.stack(lines_back))
    return [as_bf16(table) for table in tables]


def slot_rows(data_ref, slots, looks_rows):
    blocks = data_ref.shape[0]
    data = data_ref[...].astype(jnp.float32)
    if looks_rows % SUB == 0:
        return [
            data[:, slot * looks_rows : (slot + 1) * looks_rows].reshape(-1, LANES)
            for slot in range(slots)
        ]
    top = lax.broadcasted_iota(jnp.int32, (SUB, LANES), 0) < looks_rows
    held = [[] for _ in range(slots)]
    for block in range(0, blocks, 2):
        for slot in range(0, slots, 2):
            rows = slice(slot * looks_rows, (slot + 2) * looks_rows)
            one, two = data[block, rows], data[block + 1, rows]
            held[slot].append(jnp.where(top, one, pltpu.roll(two, looks_rows, 0)))
            held[slot + 1].append(jnp.where(top, pltpu.roll(one, looks_rows, 0), two))
    return [jnp.concatenate(rows, axis=0) for rows in held]


def goldstein_kernel(shape, *refs):
    dates, chunks, looks_rows, gate_looks, line_looks = shape
    data_refs, refs = refs[:chunks], refs[chunks:]
    near_ref, far_ref, ahead_ref, box_ref, behind_ref, back_ref, out_ref = refs[:7]
    half_ref, spec_ref, weighted_ref = refs[7:]
    slots = dates + dates // 2
    cols = dates + 1
    dot = lambda a, b: jnp.dot(a, b, preferred_element_type=jnp.float32)
    if data_refs[0].shape[0] == slots:
        held = [data_refs[0][slot] for slot in range(slots)]
    else:
        held = zip(*[slot_rows(ref, slots, looks_rows) for ref in data_refs])
        held = [jnp.concatenate(rows, axis=0).astype(jnp.bfloat16) for rows in held]
    for parity in (0, 1):
        rows = jnp.concatenate(
            [
                jnp.concatenate([held[date], held[dates + date // 2]], axis=1)
                for date in range(parity, dates, 2)
            ],
            axis=0,
        )
        both = dot(rows, near_ref[parity]).astype(jnp.bfloat16)
        for index, date in enumerate(range(parity, dates, 2)):
            mine = both[index * gate_looks : (index + 1) * gate_looks]
            half_ref[:gate_looks, date * LANES : (date + 1) * LANES] = mine[:, :LANES]
            half_ref[gate_looks:, date * LANES : (date + 1) * LANES] = mine[:, LANES:]
    both = dot(jnp.concatenate(held, axis=1), far_ref[...]).astype(jnp.bfloat16)
    half_ref[:gate_looks, dates * LANES :] = both[:, :LANES]
    half_ref[gate_looks:, dates * LANES :] = both[:, LANES:]

    spec_ref[...] = dot(ahead_ref[...], half_ref[...])
    bins = ahead_ref.shape[0] // 2
    for col in range(cols):
        lanes = slice(col * LANES, (col + 1) * LANES)
        re, im = spec_ref[:bins, lanes], spec_ref[bins:, lanes]
        power = (re * re + im * im).astype(jnp.bfloat16)
        sums = dot(power, box_ref[...])
        for start in range(0, bins, PATCH):
            rows = slice(start, start + PATCH)
            line = sums[rows, :LANES]
            total = jnp.sum(sums[rows, LANES:], axis=0, keepdims=True)
            smooth = line + pltpu.roll(line, 1, 0) + pltpu.roll(line, PATCH - 1, 0)
            level = total * (1.0 / (PATCH * PATCH)) + LEVEL_FLOOR
            weight = jnp.sqrt(smooth * (1.0 / (9.0 * level)) + BOX_FLOOR)
            weighted_ref[rows, lanes] = (re[rows] * weight).astype(jnp.bfloat16)
            weighted_ref[start + bins : start + bins + PATCH, lanes] = (im[rows] * weight).astype(
                jnp.bfloat16
            )
    inverse = dot(behind_ref[...], weighted_ref[...]).astype(jnp.bfloat16)
    far = [inverse[:gate_looks, dates * LANES :], inverse[gate_looks:, dates * LANES :]]
    for date in range(dates):
        lanes = slice(date * LANES, (date + 1) * LANES)
        rows = jnp.concatenate([inverse[:gate_looks, lanes], inverse[gate_looks:, lanes]] + far, axis=1)
        result = lax.dot_general(
            back_ref[date], rows, (((1,), (1,)), ((), ())), preferred_element_type=jnp.float32
        )
        out_ref[date, 0] = result[:line_looks]
        out_ref[date, 1] = result[line_looks:]


def goldstein(looks, dates, line_looks):
    chunks = len(looks)
    blocks, rows, _ = looks[0].shape
    slots = dates + dates // 2
    looks_rows = rows // slots
    gate_looks = chunks * blocks * looks_rows
    order = np.arange(gate_looks).reshape(blocks, chunks, looks_rows).swapaxes(0, 1).reshape(-1)
    if looks_rows % SUB and 2 * looks_rows != SUB:
        looks = [
            each.reshape(blocks, slots, looks_rows, LANES)
            .swapaxes(0, 1)
            .reshape(slots, blocks * looks_rows, LANES)
            for each in looks
        ]
        looks = [jnp.concatenate(looks, axis=1)]
    tables = goldstein_tables(dates, order, line_looks)
    bins = tables[2].shape[0] // 2
    width = (dates + 1) * LANES
    shape = (dates, len(looks), looks_rows, gate_looks, line_looks)
    whole = pl.BlockSpec(memory_space=pltpu.VMEM)
    filtered = pl.pallas_call(
        lambda *refs: goldstein_kernel(shape, *refs),
        out_shape=jax.ShapeDtypeStruct((dates, 2, line_looks, gate_looks), jnp.float32),
        in_specs=[whole] * (len(looks) + len(tables)),
        out_specs=whole,
        scratch_shapes=[
            pltpu.VMEM((2 * gate_looks, width), jnp.bfloat16),
            pltpu.VMEM((2 * bins, width), jnp.float32),
            pltpu.VMEM((2 * bins, width), jnp.bfloat16),
        ],
        compiler_params=pltpu.CompilerParams(vmem_limit_bytes=VMEM_BYTES),
        name="goldstein",
    )(*looks, *tables)
    return filtered.swapaxes(2, 3)


def body(raw_echo, range_filter, azimuth_phase, pair_offset):
    dates, _, lines, _ = raw_echo.shape
    devices = lax.axis_size("lines")
    phases = phase_tables(azimuth_phase, devices)
    tables = focus_tables(devices, lines)
    far = compress(raw_echo, range_filter, devices, 1)
    near = compress(raw_echo, range_filter, devices, 0, far[0])
    columns = []
    for index, block in enumerate(near + far):
        if index:
            pairs = [(i, i ^ index) for i in range(devices)]
            block = lax.ppermute(block, "lines", pairs)
        columns.append(block)
    sent = focus(columns, pair_offset, phases, tables)
    looks = lax.all_to_all(sent, "lines", split_axis=0, concat_axis=0, tiled=True)
    return goldstein([looks], dates, lines // ML_AZ)


def solution(mesh):
    placed = (P("groups", None, "lines", None), P(), P("lines", None), P())
    return jax.shard_map(
        body,
        mesh=mesh,
        in_specs=placed,
        out_specs=P("groups", None, None, "lines"),
        check_vma=False,
    )
```

```python
import math

import jax
import jax.numpy as jnp
import numpy as np
from jax import lax
from jax.experimental import pallas as pl
from jax.experimental.pallas import tpu as pltpu
from jax.sharding import PartitionSpec as P

ML_RG = 4
ML_AZ = 2
PATCH = 32
HALF = PATCH // 2
BOX_FLOOR = 0.25
LEVEL_FLOOR = 1e-06
SUB = 8
LANES = 128
VMEM_BYTES = 32 * 1024 * 1024


def real_block(table):
    return np.block([[table.real, table.imag], [-table.imag, table.real]])


def wave(rows, cols, period, direction):
    product = np.asarray(rows)[:, None] * np.asarray(cols)[None, :] % period
    return np.exp(direction * 2j * math.pi / period * product)


def as_bf16(table):
    return jnp.asarray(np.asarray(table, np.float32), jnp.bfloat16)


def line_order(line_len):
    return np.arange(line_len).reshape(line_len // ML_AZ, ML_AZ).T.reshape(-1)


def small_dft(parts, direction):
    count = len(parts)
    if count == 1:
        return parts
    even = small_dft(parts[0::2], direction)
    odd = small_dft(parts[1::2], direction)
    low, high = [], []
    for k in range(count // 2):
        (er, ei), (vr, vi) = even[k], odd[k]
        if k == 0:
            tr, ti = vr, vi
        elif 4 * k == count:
            if direction < 0:
                tr, ti = vi, -vr
            else:
                tr, ti = -vi, vr
        elif 8 * k == count:
            s = math.sqrt(0.5)
            if direction < 0:
                tr, ti = (vr + vi) * s, (vi - vr) * s
            else:
                tr, ti = (vr - vi) * s, (vi + vr) * s
        elif 8 * k == 3 * count:
            s = math.sqrt(0.5)
            if direction < 0:
                tr, ti = (vi - vr) * s, -(vr + vi) * s
            else:
                tr, ti = -(vr + vi) * s, (vr - vi) * s
        else:
            c = math.cos(2 * math.pi * k / count)
            s = direction * math.sin(2 * math.pi * k / count)
            tr, ti = vr * c - vi * s, vr * s + vi * c
        low.append((er + tr, ei + ti))
        high.append((er - tr, ei - ti))
    return low + high


def compress_kernel(shape, raw_hbm, filter_hbm, *refs):
    region, dates, step, devices, gates, lines = shape
    count = devices // 2
    tiles, looks_rows = gates // SUB, gates // ML_RG
    out_refs, refs = refs[:-5], refs[-5:]
    raw_ref, filter_ref, wide_ref, raw_sems, filter_sem = refs
    gates_in = raw_ref.shape[3]
    me = lax.axis_index("lines")
    half = me // count if region == 0 else 1 - me // count
    copies = [
        pltpu.make_async_copy(
            raw_hbm.at[pl.ds(first, step)], raw_ref.at[pl.ds(first, step)], raw_sems.at[first // step]
        )
        for first in range(0, dates, step)
    ]
    filter_copy = pltpu.make_async_copy(
        filter_hbm.at[:, pl.ds(pl.multiple_of(half * count * gates, count * gates), count * gates)],
        filter_ref,
        filter_sem,
    )
    filter_copy.start()
    for copy in copies:
        copy.start()
    filter_copy.wait()

    def product(w, x):
        return lax.dot_general(
            w, x, (((1,), (1,)), ((), ())), preferred_element_type=jnp.float32
        )

    for first in range(0, dates, step):
        copies[first // step].wait()
        raw = [
            raw_ref[first : first + step, part].reshape(step * lines, gates_in) for part in (0, 1)
        ]
        real = product(filter_ref[0], raw[0]) - product(filter_ref[1], raw[1])
        imag = product(filter_ref[1], raw[0]) + product(filter_ref[0], raw[1])
        for at in range(step):
            wide_ref[first + at, 0] = real[:, at * lines : (at + 1) * lines]
            wide_ref[first + at, 1] = imag[:, at * lines : (at + 1) * lines]
        for index in range(count):
            base = pl.multiple_of((me % count ^ index) * gates, gates)
            for date in range(first, first + step):
                for tile in range(tiles):
                    rows = []
                    for part in (0, 1):
                        begin, run = tile * SUB, min(looks_rows, SUB)
                        for at in range(begin, begin + SUB, run):
                            gate = base + at // looks_rows + ML_RG * (at % looks_rows)
                            rows.append(wide_ref[date, part, pl.ds(gate, run, stride=ML_RG), :])
                    tile_rows = jnp.concatenate(rows, axis=0).astype(jnp.bfloat16)
                    if len(out_refs) == 1:
                        out_refs[0][index, date, tile] = tile_rows
                    else:
                        out_refs[index][date, tile] = tile_rows


def compress(raw_echo, range_filter, devices, region, after=None):
    dates, _, lines, gates_in = raw_echo.shape
    gates = range_filter.shape[1] // devices
    count = devices // 2
    tiles = gates // SUB
    step = 2 if dates % 2 == 0 else 1
    shape = (region, dates, step, devices, gates, lines)
    hbm = pl.BlockSpec(memory_space=pltpu.HBM)
    block = (dates, tiles, 2 * SUB, lines)
    operands = [pltpu.with_memory_space_constraint(x, pltpu.HBM) for x in (raw_echo, range_filter)]
    extra = [] if after is None else [after]

    def kernel(raw_hbm, filter_hbm, *refs):
        compress_kernel(shape, raw_hbm, filter_hbm, *refs[len(extra) :])

    return pl.pallas_call(
        kernel,
        out_shape=[jax.ShapeDtypeStruct(block, jnp.bfloat16)] * count,
        in_specs=[hbm, hbm] + [pl.BlockSpec(memory_space=pl.ANY)] * len(extra),
        out_specs=[pl.BlockSpec(memory_space=pltpu.VMEM)] * count,
        scratch_shapes=[
            pltpu.VMEM(raw_echo.shape, jnp.bfloat16),
            pltpu.VMEM((2, count * gates, gates_in), jnp.bfloat16),
            pltpu.VMEM((dates, 2, count * gates, lines), jnp.float32),
            pltpu.SemaphoreType.DMA((dates // step,)),
            pltpu.SemaphoreType.DMA,
        ],
        compiler_params=pltpu.CompilerParams(vmem_limit_bytes=VMEM_BYTES),
        cost_estimate=pl.CostEstimate(
            flops=8 * dates * lines * count * gates * gates_in,
            bytes_accessed=4 * (raw_echo.size + count * gates * gates_in),
            transcendentals=0,
        ),
        name="compress",
    )(*operands, *extra)


def focus_kernel(shape, offset_ref, cos_ref, sin_ref, turn_ref, fwd_ref, back_ref, *refs):
    dates, blocks, tiles, gates, lines = shape
    block_refs, out_refs, refs = refs[:blocks], refs[blocks : 2 * blocks], refs[2 * blocks :]
    data_ref, image_ref, look_ref = refs
    me = lax.axis_index("lines")
    for index, block_ref in enumerate(block_refs):
        data_ref[me ^ index] = block_ref[...]
    looks_rows = gates // ML_RG
    look_lines = lines // ML_AZ
    for date in range(dates):
        for tile in range(tiles):
            parts = []
            for a in range(blocks):
                both = data_ref[a, date, tile].astype(jnp.float32)
                parts.append((both[:SUB], both[SUB:]))
            parts = small_dft(parts, -1)
            turned = []
            for a, (re, im) in enumerate(parts):
                tr, ti = turn_ref[0, a : a + 1], turn_ref[1, a : a + 1]
                turned.append((re * tr - im * ti, re * ti + im * tr))
            rows = jnp.concatenate(
                [jnp.concatenate([re, im], axis=1) for re, im in turned], axis=0
            ).astype(jnp.bfloat16)
            spectrum = jnp.dot(rows, fwd_ref[...], preferred_element_type=jnp.float32)
            re, im = spectrum[:, :lines], spectrum[:, lines:]
            pr, pi = cos_ref[tile], sin_ref[tile]
            rows = jnp.concatenate([re * pr - im * pi, re * pi + im * pr], axis=1).astype(
                jnp.bfloat16
            )
            back = jnp.dot(rows, back_ref[...], preferred_element_type=jnp.float32)
            parts = []
            for a in range(blocks):
                re = back[a * SUB : (a + 1) * SUB, :lines]
                im = back[a * SUB : (a + 1) * SUB, lines:]
                tr, ti = turn_ref[2, a : a + 1], turn_ref[3, a : a + 1]
                parts.append((re * tr - im * ti, re * ti + im * tr))
            parts = small_dft(parts, 1)
            for a, (re, im) in enumerate(parts):
                image_ref[date, tile, a, 0] = re
                image_ref[date, tile, a, 1] = im

    lane = lax.broadcasted_iota(jnp.int32, (SUB, lines), 1)
    first = lane < look_lines
    scale = 1.0 / (ML_RG * ML_AZ)
    for date in range(dates):
        partner = lax.rem(date + offset_ref[date], dates)
        for a in range(blocks):
            sums = {}
            for tile in range(tiles):
                cr, ci = image_ref[date, tile, a, 0], image_ref[date, tile, a, 1]
                pr, pi = image_ref[partner, tile, a, 0], image_ref[partner, tile, a, 1]
                re, im = cr * pr + ci * pi, ci * pr - cr * pi
                at = tile * SUB % looks_rows
                if at in sums:
                    re, im = re + sums[at][0], im + sums[at][1]
                sums[at] = (re, im)
            for at, (re, im) in sums.items():
                look = jnp.where(first, re, im) + pltpu.roll(
                    jnp.where(first, im, re), look_lines, 1
                )
                step = SUB
                while step > looks_rows:
                    step //= 2
                    look = look + pltpu.roll(look, step, 0)
                count = min(SUB, looks_rows)
                row = date * looks_rows + at
                look_ref[a, row : row + count, :] = (look * scale)[:count]

    small = lax.broadcasted_iota(jnp.int32, (looks_rows, lines), 1) % look_lines
    from_high, from_low = small < HALF, small >= look_lines - HALF
    zero = jnp.zeros((looks_rows, lines), jnp.float32)

    def rim(a, date):
        rows = slice(date * looks_rows, (date + 1) * looks_rows)
        high = look_ref[a + 1, rows, :] if a + 1 < blocks else zero
        low = look_ref[a - 1, rows, :] if a > 0 else zero
        return jnp.where(from_high, high, low)

    for a in range(blocks):
        for date in range(0, dates, 2):
            own = rim(a, date)
            other = pltpu.roll(rim(a, date + 1), look_lines // 2, 1)
            row = (dates + date // 2) * looks_rows
            look_ref[a, row : row + looks_rows, :] = jnp.where(from_high | from_low, own, other)
    for index, out_ref in enumerate(out_refs):
        out_ref[...] = look_ref[me ^ index].astype(jnp.bfloat16)


def phase_tables(azimuth_phase, blocks):
    gates, total = azimuth_phase.shape
    looks_rows = gates // ML_RG
    lines = total // blocks
    tiles = gates // SUB
    phase = azimuth_phase.reshape(looks_rows, ML_RG, lines, blocks)
    phase = phase.transpose(1, 0, 3, 2).reshape(tiles, SUB, blocks, lines)
    phase = phase.transpose(0, 2, 1, 3).reshape(tiles, blocks * SUB, lines)
    phase = lax.optimization_barrier(phase)
    return jnp.cos(phase), jnp.sin(phase)


def focus_tables(blocks, lines):
    total = blocks * lines
    order = line_order(lines)
    ahead = wave(np.arange(blocks), np.arange(lines), total, -1)
    behind = wave(np.arange(blocks), order, total, 1)
    turn = np.stack([ahead.real, ahead.imag, behind.real, behind.imag]).astype(np.float32)
    fwd = as_bf16(real_block(wave(np.arange(lines), np.arange(lines), lines, -1)))
    back = as_bf16(real_block(wave(np.arange(lines), order, lines, 1) / total))
    return jnp.asarray(turn), fwd, back


def focus(columns, pair_offset, phases, tables):
    blocks = len(columns)
    dates, tiles, _, lines = columns[0].shape
    gates = tiles * SUB
    looks_rows = gates // ML_RG
    slots = dates + dates // 2
    shape = (dates, blocks, tiles, gates, lines)
    whole = pl.BlockSpec(memory_space=pltpu.VMEM)
    return pl.pallas_call(
        lambda *refs: focus_kernel(shape, *refs),
        out_shape=[jax.ShapeDtypeStruct((slots * looks_rows, lines), jnp.bfloat16)] * blocks,
        in_specs=[pl.BlockSpec(memory_space=pltpu.SMEM)] + [whole] * (5 + blocks),
        out_specs=[whole] * blocks,
        scratch_shapes=[
            pltpu.VMEM((blocks, dates, tiles, 2 * SUB, lines), jnp.bfloat16),
            pltpu.VMEM((dates, tiles, blocks, 2, SUB, lines), jnp.float32),
            pltpu.VMEM((blocks, slots * looks_rows, lines), jnp.float32),
        ],
        compiler_params=pltpu.CompilerParams(vmem_limit_bytes=VMEM_BYTES),
        cost_estimate=pl.CostEstimate(
            flops=16 * dates * gates * blocks * lines * lines,
            bytes_accessed=4 * blocks * columns[0].size,
            transcendentals=0,
        ),
        name="focus",
    )(pair_offset, *phases, *tables, *columns)


def tri_window(offset):
    inside = (offset >= 0) & (offset < PATCH)
    return np.where(inside, 1.0 - np.abs(offset - (PATCH - 1) / 2.0) / HALF, 0.0)


def patch_tables(cells, starts):
    offset = np.asarray(cells)[:, None] - np.asarray(starts)[None, :]
    inside = ((offset >= 0) & (offset < PATCH)).astype(np.float64)
    angle = 2.0 * math.pi / PATCH * (offset[:, :, None] * np.arange(PATCH) % PATCH)
    ahead = np.exp(-1j * angle) * inside[:, :, None]
    behind = np.exp(1j * angle) * tri_window(offset)[:, :, None] / PATCH
    flat = (len(cells), len(starts) * PATCH)
    return ahead.reshape(flat), behind.reshape(flat).T


def goldstein_tables(dates, gate_looks, line_looks):
    per = LANES // PATCH
    starts = np.arange(-HALF, line_looks, HALF)
    cells = np.arange(-HALF, line_looks + HALF)
    ahead, behind = patch_tables(cells, starts)
    main = slice(HALF, HALF + line_looks)
    behind = behind[:, main]
    split = per * PATCH

    def lanes_of(table, shift):
        block = np.zeros((2, line_looks, table.shape[1]), complex)
        block[0], block[1] = table[main], 1j * table[main]
        rim = np.zeros((2, line_looks, table.shape[1]), complex)
        for part, turn in enumerate((1.0, 1j)):
            rim[part, :HALF] = turn * table[HALF + line_looks :]
            rim[part, line_looks - HALF :] = turn * table[:HALF]
        flat = (2 * line_looks, table.shape[1])
        return block.reshape(flat), np.roll(rim.reshape(flat), shift, axis=0)

    def out_parts(table):
        return np.concatenate([table.real, table.imag], axis=1)

    near = [
        out_parts(np.concatenate(lanes_of(ahead[:, :split], parity * (line_looks // 2))))
        for parity in (0, 1)
    ]
    rest = ahead.shape[1] - split
    far_block = np.zeros((dates, 2 * line_looks, dates, rest), complex)
    far_rim = np.zeros((dates // 2, 2 * line_looks, dates, rest), complex)
    for date in range(dates):
        block, rim = lanes_of(ahead[:, split:], date % 2 * (line_looks // 2))
        far_block[date, :, date] = block
        far_rim[date // 2, :, date] = rim
    far = np.concatenate([far_block, far_rim]).reshape(-1, dates * rest)
    gate_starts = np.arange(-HALF, gate_looks, HALF)
    gate_ahead, gate_behind = patch_tables(np.arange(gate_looks), gate_starts)
    ahead_rows = real_block(gate_ahead).T
    behind_rows = real_block(gate_behind).T

    lines_back = []
    for date in range(dates):
        far_back = np.zeros((dates, rest, line_looks), complex)
        far_back[date] = behind[split:]
        lines_back.append(
            np.concatenate(
                [real_block(behind[:split]), real_block(far_back.reshape(-1, line_looks))]
            ).T
        )
    gap = (np.arange(PATCH)[:, None] - np.arange(PATCH)[None, :]) % PATCH
    ring = ((gap == 0) | (gap == 1) | (gap == PATCH - 1)).astype(np.float64)
    box = np.concatenate(
        [np.kron(np.eye(per), ring), np.kron(np.eye(per), np.ones((PATCH, PATCH)))], axis=1
    )
    tables = (np.stack(near), out_parts(far), ahead_rows, box, behind_rows, np.stack(lines_back))
    return [as_bf16(table) for table in tables]


def goldstein_kernel(shape, *refs):
    dates, blocks, looks_rows, line_looks = shape
    block_refs, refs = refs[:blocks], refs[blocks:]
    near_ref, far_ref, ahead_ref, box_ref, behind_ref, back_ref, out_ref = refs[:7]
    data_ref, half_ref, spec_ref, weighted_ref = refs[7:]
    slots = dates + dates // 2
    gate_looks = blocks * looks_rows
    cols = dates + 1
    dot = lambda a, b: jnp.dot(a, b, preferred_element_type=jnp.float32)
    me = lax.axis_index("lines")
    for index, block_ref in enumerate(block_refs):
        block = block_ref[...].astype(jnp.float32)
        rows = pl.ds(pl.multiple_of((me ^ index) * looks_rows, looks_rows), looks_rows)
        for slot in range(slots):
            data_ref[slot, rows, :] = block[slot * looks_rows : (slot + 1) * looks_rows]
    held = [data_ref[slot].astype(jnp.bfloat16) for slot in range(slots)]
    for parity in (0, 1):
        rows = jnp.concatenate(
            [
                jnp.concatenate([held[date], held[dates + date // 2]], axis=1)
                for date in range(parity, dates, 2)
            ],
            axis=0,
        )
        both = dot(rows, near_ref[parity]).astype(jnp.bfloat16)
        for index, date in enumerate(range(parity, dates, 2)):
            mine = both[index * gate_looks : (index + 1) * gate_looks]
            half_ref[:gate_looks, date * LANES : (date + 1) * LANES] = mine[:, :LANES]
            half_ref[gate_looks:, date * LANES : (date + 1) * LANES] = mine[:, LANES:]
    both = dot(jnp.concatenate(held, axis=1), far_ref[...]).astype(jnp.bfloat16)
    half_ref[:gate_looks, dates * LANES :] = both[:, :LANES]
    half_ref[gate_looks:, dates * LANES :] = both[:, LANES:]

    spec_ref[...] = dot(ahead_ref[...], half_ref[...])
    bins = ahead_ref.shape[0] // 2
    for col in range(cols):
        lanes = slice(col * LANES, (col + 1) * LANES)
        re, im = spec_ref[:bins, lanes], spec_ref[bins:, lanes]
        power = (re * re + im * im).astype(jnp.bfloat16)
        sums = dot(power, box_ref[...])
        for start in range(0, bins, PATCH):
            rows = slice(start, start + PATCH)
            line = sums[rows, :LANES]
            total = jnp.sum(sums[rows, LANES:], axis=0, keepdims=True)
            smooth = line + pltpu.roll(line, 1, 0) + pltpu.roll(line, PATCH - 1, 0)
            level = total * (1.0 / (PATCH * PATCH)) + LEVEL_FLOOR
            weight = jnp.sqrt(smooth * (1.0 / (9.0 * level)) + BOX_FLOOR)
            weighted_ref[rows, lanes] = (re[rows] * weight).astype(jnp.bfloat16)
            weighted_ref[start + bins : start + bins + PATCH, lanes] = (im[rows] * weight).astype(
                jnp.bfloat16
            )
    inverse = dot(behind_ref[...], weighted_ref[...]).astype(jnp.bfloat16)
    far = [inverse[:gate_looks, dates * LANES :], inverse[gate_looks:, dates * LANES :]]
    for date in range(dates):
        lanes = slice(date * LANES, (date + 1) * LANES)
        rows = jnp.concatenate([inverse[:gate_looks, lanes], inverse[gate_looks:, lanes]] + far, axis=1)
        result = lax.dot_general(
            back_ref[date], rows, (((1,), (1,)), ((), ())), preferred_element_type=jnp.float32
        )
        out_ref[date, 0] = result[:line_looks]
        out_ref[date, 1] = result[line_looks:]


def goldstein(looks, dates, line_looks):
    blocks = len(looks)
    slots = dates + dates // 2
    looks_rows = looks[0].shape[0] // slots
    gate_looks = blocks * looks_rows
    tables = goldstein_tables(dates, gate_looks, line_looks)
    bins = tables[2].shape[0] // 2
    width = (dates + 1) * LANES
    shape = (dates, blocks, looks_rows, line_looks)
    whole = pl.BlockSpec(memory_space=pltpu.VMEM)
    filtered = pl.pallas_call(
        lambda *refs: goldstein_kernel(shape, *refs),
        out_shape=jax.ShapeDtypeStruct((dates, 2, line_looks, gate_looks), jnp.float32),
        in_specs=[whole] * (len(looks) + len(tables)),
        out_specs=whole,
        scratch_shapes=[
            pltpu.VMEM((slots, gate_looks, LANES), jnp.float32),
            pltpu.VMEM((2 * gate_looks, width), jnp.bfloat16),
            pltpu.VMEM((2 * bins, width), jnp.float32),
            pltpu.VMEM((2 * bins, width), jnp.bfloat16),
        ],
        compiler_params=pltpu.CompilerParams(vmem_limit_bytes=VMEM_BYTES),
        name="goldstein",
    )(*looks, *tables)
    return filtered.swapaxes(2, 3)


def exchange(blocks, devices, first):
    held = []
    for index, block in enumerate(blocks, first):
        if index:
            block = lax.ppermute(block, "lines", [(i, i ^ index) for i in range(devices)])
        held.append(block)
    return held


def body(raw_echo, range_filter, azimuth_phase, pair_offset):
    dates, _, lines, _ = raw_echo.shape
    devices = lax.axis_size("lines")
    phases = phase_tables(azimuth_phase, devices)
    tables = focus_tables(devices, lines)
    far = compress(raw_echo, range_filter, devices, 1)
    far = exchange(far, devices, devices // 2)
    near = compress(raw_echo, range_filter, devices, 0, far[0])
    near = exchange(near, devices, 0)
    looks = exchange(focus(near + far, pair_offset, phases, tables), devices, 0)
    return goldstein(looks, dates, lines // ML_AZ)


def solution(mesh):
    placed = (P("groups", None, "lines", None), P(), P("lines", None), P())
    return jax.shard_map(
        body,
        mesh=mesh,
        in_specs=placed,
        out_specs=P("groups", None, None, "lines"),
        check_vma=False,
    )
```

```python
import math

import jax
import jax.numpy as jnp
import numpy as np
from jax import lax
from jax.experimental import pallas as pl
from jax.experimental.pallas import tpu as pltpu
from jax.sharding import PartitionSpec as P

ML_RG = 4
ML_AZ = 2
PATCH = 32
HALF = PATCH // 2
BOX_FLOOR = 0.25
LEVEL_FLOOR = 1e-06
SUB = 8
LANES = 128
VMEM_BYTES = 32 * 1024 * 1024


def real_block(table):
    return np.block([[table.real, table.imag], [-table.imag, table.real]])


def wave(rows, cols, period, direction):
    product = np.asarray(rows)[:, None] * np.asarray(cols)[None, :] % period
    return np.exp(direction * 2j * math.pi / period * product)


def as_bf16(table):
    return jnp.asarray(np.asarray(table, np.float32), jnp.bfloat16)


def line_order(line_len):
    return np.arange(line_len).reshape(line_len // ML_AZ, ML_AZ).T.reshape(-1)


def small_dft(parts, direction):
    count = len(parts)
    if count == 1:
        return parts
    even = small_dft(parts[0::2], direction)
    odd = small_dft(parts[1::2], direction)
    low, high = [], []
    for k in range(count // 2):
        (er, ei), (vr, vi) = even[k], odd[k]
        if k == 0:
            tr, ti = vr, vi
        elif 4 * k == count:
            if direction < 0:
                tr, ti = vi, -vr
            else:
                tr, ti = -vi, vr
        elif 8 * k == count:
            s = math.sqrt(0.5)
            if direction < 0:
                tr, ti = (vr + vi) * s, (vi - vr) * s
            else:
                tr, ti = (vr - vi) * s, (vi + vr) * s
        elif 8 * k == 3 * count:
            s = math.sqrt(0.5)
            if direction < 0:
                tr, ti = (vi - vr) * s, -(vr + vi) * s
            else:
                tr, ti = -(vr + vi) * s, (vr - vi) * s
        else:
            c = math.cos(2 * math.pi * k / count)
            s = direction * math.sin(2 * math.pi * k / count)
            tr, ti = vr * c - vi * s, vr * s + vi * c
        low.append((er + tr, ei + ti))
        high.append((er - tr, ei - ti))
    return low + high


def compress_kernel(
    shape, raw_hbm, filter_hbm, out_ref, raw_ref, filter_ref, wide_ref, raw_sems, filter_sems
):
    chunk, dates, step, targets, tiles, gates, lines = shape
    looks_rows = gates // ML_RG
    gates_in = raw_ref.shape[3]
    copies = [
        pltpu.make_async_copy(
            raw_hbm.at[pl.ds(first, step)], raw_ref.at[pl.ds(first, step)], raw_sems.at[first // step]
        )
        for first in range(0, dates, step)
    ]
    parts = 2
    held = targets // parts
    filter_copies = [
        pltpu.make_async_copy(
            filter_hbm.at[:, pl.ds(part * held, held), chunk],
            filter_ref.at[:, pl.ds(part * held, held)],
            filter_sems.at[part],
        )
        for part in range(parts)
    ]
    for copy in [filter_copies[0], *copies[:1], *filter_copies[1:], *copies[1:]]:
        copy.start()

    def product(w, x):
        return lax.dot_general(
            w, x, (((1,), (1,)), ((), ())), preferred_element_type=jnp.float32
        )

    for first in range(0, dates, step):
        copies[first // step].wait()
        raw = [
            raw_ref[first : first + step, part].reshape(step * lines, gates_in) for part in (0, 1)
        ]
        for group in range(parts):
            if first == 0:
                filter_copies[group].wait()
            weight = [
                filter_ref[part, group * held : (group + 1) * held].reshape(held * gates, gates_in)
                for part in (0, 1)
            ]
            real = product(weight[0], raw[0]) - product(weight[1], raw[1])
            imag = product(weight[1], raw[0]) + product(weight[0], raw[1])
            rows = slice(group * held * gates, (group + 1) * held * gates)
            for at in range(step):
                wide_ref[first + at, 0, rows] = real[:, at * lines : (at + 1) * lines]
                wide_ref[first + at, 1, rows] = imag[:, at * lines : (at + 1) * lines]
        for target in range(targets):
            for date in range(first, first + step):
                for tile in range(tiles):
                    rows = []
                    for part in (0, 1):
                        begin, count = tile * SUB, min(looks_rows, SUB)
                        for at in range(begin, begin + SUB, count):
                            gate = target * gates + at // looks_rows + ML_RG * (at % looks_rows)
                            rows.append(wide_ref[date, part, pl.ds(gate, count, stride=ML_RG), :])
                    out_ref[target, date, tile] = jnp.concatenate(rows, axis=0).astype(
                        jnp.bfloat16
                    )


def compress(raw_echo, filter_chunks, chunk):
    dates, _, lines, gates_in = raw_echo.shape
    _, targets, _, gates, _ = filter_chunks.shape
    tiles = gates // SUB
    step = 2 if dates % 2 == 0 else 1
    shape = (chunk, dates, step, targets, tiles, gates, lines)
    hbm = pl.BlockSpec(memory_space=pltpu.HBM)
    return pl.pallas_call(
        lambda *refs: compress_kernel(shape, *refs),
        out_shape=jax.ShapeDtypeStruct((targets, dates, tiles, 2 * SUB, lines), jnp.bfloat16),
        in_specs=[hbm, hbm],
        out_specs=pl.BlockSpec(memory_space=pltpu.VMEM),
        scratch_shapes=[
            pltpu.VMEM(raw_echo.shape, jnp.bfloat16),
            pltpu.VMEM((2, targets, gates, gates_in), jnp.bfloat16),
            pltpu.VMEM((dates, 2, targets * gates, lines), jnp.float32),
            pltpu.SemaphoreType.DMA((dates // step,)),
            pltpu.SemaphoreType.DMA((2,)),
        ],
        compiler_params=pltpu.CompilerParams(vmem_limit_bytes=VMEM_BYTES),
        cost_estimate=pl.CostEstimate(
            flops=8 * dates * lines * targets * gates * gates_in,
            bytes_accessed=4 * (raw_echo.size + targets * gates * gates_in),
            transcendentals=0,
        ),
        name="compress",
    )(*[pltpu.with_memory_space_constraint(x, pltpu.HBM) for x in (raw_echo, filter_chunks)])


def focus_kernel(
    shape, offset_ref, data_ref, cos_ref, sin_ref, turn_ref, fwd_ref, back_ref, out_ref, image_ref,
    look_ref,
):
    chunk, dates, blocks, tiles, gates, lines = shape
    looks_rows = gates // ML_RG
    look_lines = lines // ML_AZ
    for date in range(dates):
        for tile in range(tiles):
            parts = []
            for a in range(blocks):
                both = data_ref[a, date, tile].astype(jnp.float32)
                parts.append((both[:SUB], both[SUB:]))
            parts = small_dft(parts, -1)
            turned = []
            for a, (re, im) in enumerate(parts):
                tr, ti = turn_ref[0, a : a + 1], turn_ref[1, a : a + 1]
                turned.append((re * tr - im * ti, re * ti + im * tr))
            rows = jnp.concatenate(
                [jnp.concatenate([re, im], axis=1) for re, im in turned], axis=0
            ).astype(jnp.bfloat16)
            spectrum = jnp.dot(rows, fwd_ref[...], preferred_element_type=jnp.float32)
            re, im = spectrum[:, :lines], spectrum[:, lines:]
            pr, pi = cos_ref[chunk, tile], sin_ref[chunk, tile]
            rows = jnp.concatenate([re * pr - im * pi, re * pi + im * pr], axis=1).astype(
                jnp.bfloat16
            )
            back = jnp.dot(rows, back_ref[...], preferred_element_type=jnp.float32)
            parts = []
            for a in range(blocks):
                re = back[a * SUB : (a + 1) * SUB, :lines]
                im = back[a * SUB : (a + 1) * SUB, lines:]
                tr, ti = turn_ref[2, a : a + 1], turn_ref[3, a : a + 1]
                parts.append((re * tr - im * ti, re * ti + im * tr))
            parts = small_dft(parts, 1)
            for a, (re, im) in enumerate(parts):
                image_ref[date, tile, a, 0] = re
                image_ref[date, tile, a, 1] = im

    lane = lax.broadcasted_iota(jnp.int32, (SUB, lines), 1)
    first = lane < look_lines
    scale = 1.0 / (ML_RG * ML_AZ)
    for date in range(dates):
        partner = lax.rem(date + offset_ref[date], dates)
        for a in range(blocks):
            sums = {}
            for tile in range(tiles):
                cr, ci = image_ref[date, tile, a, 0], image_ref[date, tile, a, 1]
                pr, pi = image_ref[partner, tile, a, 0], image_ref[partner, tile, a, 1]
                re, im = cr * pr + ci * pi, ci * pr - cr * pi
                at = tile * SUB % looks_rows
                if at in sums:
                    re, im = re + sums[at][0], im + sums[at][1]
                sums[at] = (re, im)
            for at, (re, im) in sums.items():
                look = jnp.where(first, re, im) + pltpu.roll(
                    jnp.where(first, im, re), look_lines, 1
                )
                step = SUB
                while step > looks_rows:
                    step //= 2
                    look = look + pltpu.roll(look, step, 0)
                count = min(SUB, looks_rows)
                row = date * looks_rows + at
                look_ref[a, row : row + count, :] = (look * scale)[:count]

    small = lax.broadcasted_iota(jnp.int32, (looks_rows, lines), 1) % look_lines
    from_high, from_low = small < HALF, small >= look_lines - HALF
    zero = jnp.zeros((looks_rows, lines), jnp.float32)

    def rim(a, date):
        rows = slice(date * looks_rows, (date + 1) * looks_rows)
        high = look_ref[a + 1, rows, :] if a + 1 < blocks else zero
        low = look_ref[a - 1, rows, :] if a > 0 else zero
        return jnp.where(from_high, high, low)

    for a in range(blocks):
        for date in range(0, dates, 2):
            own = rim(a, date)
            other = pltpu.roll(rim(a, date + 1), look_lines // 2, 1)
            row = (dates + date // 2) * looks_rows
            look_ref[a, row : row + looks_rows, :] = jnp.where(from_high | from_low, own, other)
    out_ref[...] = look_ref[...].astype(jnp.bfloat16)


def phase_tables(azimuth_phase, chunks, blocks):
    gates, total = azimuth_phase.shape
    looks_rows = gates // chunks // ML_RG
    lines = total // blocks
    tiles = gates // chunks // SUB
    phase = azimuth_phase.reshape(chunks, looks_rows, ML_RG, lines, blocks)
    phase = phase.transpose(0, 2, 1, 4, 3).reshape(chunks, tiles, SUB, blocks, lines)
    phase = phase.transpose(0, 1, 3, 2, 4).reshape(chunks, tiles, blocks * SUB, lines)
    phase = lax.optimization_barrier(phase)
    return jnp.cos(phase), jnp.sin(phase)


def focus_tables(blocks, lines):
    total = blocks * lines
    order = line_order(lines)
    ahead = wave(np.arange(blocks), np.arange(lines), total, -1)
    behind = wave(np.arange(blocks), order, total, 1)
    turn = np.stack([ahead.real, ahead.imag, behind.real, behind.imag]).astype(np.float32)
    fwd = as_bf16(real_block(wave(np.arange(lines), np.arange(lines), lines, -1)))
    back = as_bf16(real_block(wave(np.arange(lines), order, lines, 1) / total))
    return jnp.asarray(turn), fwd, back


def focus(columns, pair_offset, phases, tables, chunk):
    blocks, dates, tiles, _, lines = columns.shape
    gates = tiles * SUB
    looks_rows = gates // ML_RG
    slots = dates + dates // 2
    shape = (chunk, dates, blocks, tiles, gates, lines)
    whole = pl.BlockSpec(memory_space=pltpu.VMEM)
    return pl.pallas_call(
        lambda *refs: focus_kernel(shape, *refs),
        out_shape=jax.ShapeDtypeStruct((blocks, slots * looks_rows, lines), jnp.bfloat16),
        in_specs=[pl.BlockSpec(memory_space=pltpu.SMEM)] + [whole] * 6,
        out_specs=whole,
        scratch_shapes=[
            pltpu.VMEM((dates, tiles, blocks, 2, SUB, lines), jnp.float32),
            pltpu.VMEM((blocks, slots * looks_rows, lines), jnp.float32),
        ],
        compiler_params=pltpu.CompilerParams(vmem_limit_bytes=VMEM_BYTES),
        cost_estimate=pl.CostEstimate(
            flops=16 * dates * gates * blocks * lines * lines,
            bytes_accessed=4 * columns.size,
            transcendentals=0,
        ),
        name="focus",
    )(pair_offset, columns, *phases, *tables)


def tri_window(offset):
    inside = (offset >= 0) & (offset < PATCH)
    return np.where(inside, 1.0 - np.abs(offset - (PATCH - 1) / 2.0) / HALF, 0.0)


def patch_tables(cells, starts):
    offset = np.asarray(cells)[:, None] - np.asarray(starts)[None, :]
    inside = ((offset >= 0) & (offset < PATCH)).astype(np.float64)
    angle = 2.0 * math.pi / PATCH * (offset[:, :, None] * np.arange(PATCH) % PATCH)
    ahead = np.exp(-1j * angle) * inside[:, :, None]
    behind = np.exp(1j * angle) * tri_window(offset)[:, :, None] / PATCH
    flat = (len(cells), len(starts) * PATCH)
    return ahead.reshape(flat), behind.reshape(flat).T


def goldstein_tables(dates, gate_order, line_looks):
    per = LANES // PATCH
    starts = np.arange(-HALF, line_looks, HALF)
    cells = np.arange(-HALF, line_looks + HALF)
    ahead, behind = patch_tables(cells, starts)
    main = slice(HALF, HALF + line_looks)
    behind = behind[:, main]
    split = per * PATCH

    def lanes_of(table, shift):
        block = np.zeros((2, line_looks, table.shape[1]), complex)
        block[0], block[1] = table[main], 1j * table[main]
        rim = np.zeros((2, line_looks, table.shape[1]), complex)
        for part, turn in enumerate((1.0, 1j)):
            rim[part, :HALF] = turn * table[HALF + line_looks :]
            rim[part, line_looks - HALF :] = turn * table[:HALF]
        flat = (2 * line_looks, table.shape[1])
        return block.reshape(flat), np.roll(rim.reshape(flat), shift, axis=0)

    def out_parts(table):
        return np.concatenate([table.real, table.imag], axis=1)

    near = [
        out_parts(np.concatenate(lanes_of(ahead[:, :split], parity * (line_looks // 2))))
        for parity in (0, 1)
    ]
    rest = ahead.shape[1] - split
    far_block = np.zeros((dates, 2 * line_looks, dates, rest), complex)
    far_rim = np.zeros((dates // 2, 2 * line_looks, dates, rest), complex)
    for date in range(dates):
        block, rim = lanes_of(ahead[:, split:], date % 2 * (line_looks // 2))
        far_block[date, :, date] = block
        far_rim[date // 2, :, date] = rim
    far = np.concatenate([far_block, far_rim]).reshape(-1, dates * rest)
    gate_starts = np.arange(-HALF, len(gate_order), HALF)
    gate_ahead, gate_behind = patch_tables(np.arange(len(gate_order)), gate_starts)
    ahead_rows = real_block(gate_ahead[gate_order]).T
    behind_rows = real_block(gate_behind).T

    lines_back = []
    for date in range(dates):
        far_back = np.zeros((dates, rest, line_looks), complex)
        far_back[date] = behind[split:]
        lines_back.append(
            np.concatenate(
                [real_block(behind[:split]), real_block(far_back.reshape(-1, line_looks))]
            ).T
        )
    gap = (np.arange(PATCH)[:, None] - np.arange(PATCH)[None, :]) % PATCH
    ring = ((gap == 0) | (gap == 1) | (gap == PATCH - 1)).astype(np.float64)
    box = np.concatenate(
        [np.kron(np.eye(per), ring), np.kron(np.eye(per), np.ones((PATCH, PATCH)))], axis=1
    )
    tables = (np.stack(near), out_parts(far), ahead_rows, box, behind_rows, np.stack(lines_back))
    return [as_bf16(table) for table in tables]


def slot_rows(data_ref, slots, looks_rows):
    blocks = data_ref.shape[0]
    data = data_ref[...].astype(jnp.float32)
    if looks_rows % SUB == 0:
        return [
            data[:, slot * looks_rows : (slot + 1) * looks_rows].reshape(-1, LANES)
            for slot in range(slots)
        ]
    top = lax.broadcasted_iota(jnp.int32, (SUB, LANES), 0) < looks_rows
    held = [[] for _ in range(slots)]
    for block in range(0, blocks, 2):
        for slot in range(0, slots, 2):
            rows = slice(slot * looks_rows, (slot + 2) * looks_rows)
            one, two = data[block, rows], data[block + 1, rows]
            held[slot].append(jnp.where(top, one, pltpu.roll(two, looks_rows, 0)))
            held[slot + 1].append(jnp.where(top, pltpu.roll(one, looks_rows, 0), two))
    return [jnp.concatenate(rows, axis=0) for rows in held]


def goldstein_kernel(shape, *refs):
    dates, chunks, looks_rows, gate_looks, line_looks = shape
    data_refs, refs = refs[:chunks], refs[chunks:]
    near_ref, far_ref, ahead_ref, box_ref, behind_ref, back_ref, out_ref = refs[:7]
    half_ref, spec_ref, weighted_ref = refs[7:]
    slots = dates + dates // 2
    cols = dates + 1
    dot = lambda a, b: jnp.dot(a, b, preferred_element_type=jnp.float32)
    if data_refs[0].shape[0] == slots:
        held = [data_refs[0][slot] for slot in range(slots)]
    else:
        held = zip(*[slot_rows(ref, slots, looks_rows) for ref in data_refs])
        held = [jnp.concatenate(rows, axis=0).astype(jnp.bfloat16) for rows in held]
    for parity in (0, 1):
        rows = jnp.concatenate(
            [
                jnp.concatenate([held[date], held[dates + date // 2]], axis=1)
                for date in range(parity, dates, 2)
            ],
            axis=0,
        )
        both = dot(rows, near_ref[parity]).astype(jnp.bfloat16)
        for index, date in enumerate(range(parity, dates, 2)):
            mine = both[index * gate_looks : (index + 1) * gate_looks]
            half_ref[:gate_looks, date * LANES : (date + 1) * LANES] = mine[:, :LANES]
            half_ref[gate_looks:, date * LANES : (date + 1) * LANES] = mine[:, LANES:]
    both = dot(jnp.concatenate(held, axis=1), far_ref[...]).astype(jnp.bfloat16)
    half_ref[:gate_looks, dates * LANES :] = both[:, :LANES]
    half_ref[gate_looks:, dates * LANES :] = both[:, LANES:]

    spec_ref[...] = dot(ahead_ref[...], half_ref[...])
    bins = ahead_ref.shape[0] // 2
    for col in range(cols):
        lanes = slice(col * LANES, (col + 1) * LANES)
        re, im = spec_ref[:bins, lanes], spec_ref[bins:, lanes]
        power = (re * re + im * im).astype(jnp.bfloat16)
        sums = dot(power, box_ref[...])
        for start in range(0, bins, PATCH):
            rows = slice(start, start + PATCH)
            line = sums[rows, :LANES]
            total = jnp.sum(sums[rows, LANES:], axis=0, keepdims=True)
            smooth = line + pltpu.roll(line, 1, 0) + pltpu.roll(line, PATCH - 1, 0)
            level = total * (1.0 / (PATCH * PATCH)) + LEVEL_FLOOR
            weight = jnp.sqrt(smooth * (1.0 / (9.0 * level)) + BOX_FLOOR)
            weighted_ref[rows, lanes] = (re[rows] * weight).astype(jnp.bfloat16)
            weighted_ref[start + bins : start + bins + PATCH, lanes] = (im[rows] * weight).astype(
                jnp.bfloat16
            )
    inverse = dot(behind_ref[...], weighted_ref[...]).astype(jnp.bfloat16)
    far = [inverse[:gate_looks, dates * LANES :], inverse[gate_looks:, dates * LANES :]]
    for date in range(dates):
        lanes = slice(date * LANES, (date + 1) * LANES)
        rows = jnp.concatenate([inverse[:gate_looks, lanes], inverse[gate_looks:, lanes]] + far, axis=1)
        result = lax.dot_general(
            back_ref[date], rows, (((1,), (1,)), ((), ())), preferred_element_type=jnp.float32
        )
        out_ref[date, 0] = result[:line_looks]
        out_ref[date, 1] = result[line_looks:]


def goldstein(looks, dates, line_looks):
    chunks = len(looks)
    blocks, rows, _ = looks[0].shape
    slots = dates + dates // 2
    looks_rows = rows // slots
    gate_looks = chunks * blocks * looks_rows
    order = np.arange(gate_looks).reshape(blocks, chunks, looks_rows).swapaxes(0, 1).reshape(-1)
    if looks_rows % SUB and 2 * looks_rows != SUB:
        looks = [
            each.reshape(blocks, slots, looks_rows, LANES)
            .swapaxes(0, 1)
            .reshape(slots, blocks * looks_rows, LANES)
            for each in looks
        ]
        looks = [jnp.concatenate(looks, axis=1)]
    tables = goldstein_tables(dates, order, line_looks)
    bins = tables[2].shape[0] // 2
    width = (dates + 1) * LANES
    shape = (dates, len(looks), looks_rows, gate_looks, line_looks)
    whole = pl.BlockSpec(memory_space=pltpu.VMEM)
    filtered = pl.pallas_call(
        lambda *refs: goldstein_kernel(shape, *refs),
        out_shape=jax.ShapeDtypeStruct((dates, 2, line_looks, gate_looks), jnp.float32),
        in_specs=[whole] * (len(looks) + len(tables)),
        out_specs=whole,
        scratch_shapes=[
            pltpu.VMEM((2 * gate_looks, width), jnp.bfloat16),
            pltpu.VMEM((2 * bins, width), jnp.float32),
            pltpu.VMEM((2 * bins, width), jnp.bfloat16),
        ],
        compiler_params=pltpu.CompilerParams(vmem_limit_bytes=VMEM_BYTES),
        name="goldstein",
    )(*looks, *tables)
    return filtered.swapaxes(2, 3)


def body(raw_echo, range_filter, azimuth_phase, pair_offset):
    dates, _, lines, gates_in = raw_echo.shape
    devices = lax.axis_size("lines")
    gates = azimuth_phase.shape[0]
    chunks = 1
    filter_chunks = range_filter.reshape(2, devices, chunks, gates // chunks, gates_in)
    phases = phase_tables(azimuth_phase, chunks, devices)
    tables = focus_tables(devices, lines)

    def exchange(blocks):
        return lax.all_to_all(blocks, "lines", split_axis=0, concat_axis=0, tiled=True)

    columns = [exchange(compress(raw_echo, filter_chunks, chunk)) for chunk in range(chunks)]
    looks = [
        exchange(focus(columns[chunk], pair_offset, phases, tables, chunk))
        for chunk in range(chunks)
    ]
    return goldstein(looks, dates, lines // ML_AZ)


def solution(mesh):
    placed = (P("groups", None, "lines", None), P(), P("lines", None), P())
    return jax.shard_map(
        body,
        mesh=mesh,
        in_specs=placed,
        out_specs=P("groups", None, None, "lines"),
        check_vma=False,
    )
```

```python
import math

import jax
import jax.numpy as jnp
import numpy as np
from jax import lax
from jax.experimental import pallas as pl
from jax.experimental.pallas import tpu as pltpu
from jax.sharding import PartitionSpec as P

ML_RG = 4
ML_AZ = 2
PATCH = 32
HALF = PATCH // 2
BOX_FLOOR = 0.25
LEVEL_FLOOR = 1e-06
SUB = 8
LANES = 128
VMEM_BYTES = 32 * 1024 * 1024


def real_block(table):
    return np.block([[table.real, table.imag], [-table.imag, table.real]])


def wave(rows, cols, period, direction):
    product = np.asarray(rows)[:, None] * np.asarray(cols)[None, :] % period
    return np.exp(direction * 2j * math.pi / period * product)


def as_bf16(table):
    return jnp.asarray(np.asarray(table, np.float32), jnp.bfloat16)


def line_order(line_len):
    return np.arange(line_len).reshape(line_len // ML_AZ, ML_AZ).T.reshape(-1)


def small_dft(parts, direction):
    count = len(parts)
    if count == 1:
        return parts
    even = small_dft(parts[0::2], direction)
    odd = small_dft(parts[1::2], direction)
    low, high = [], []
    for k in range(count // 2):
        (er, ei), (vr, vi) = even[k], odd[k]
        if k == 0:
            tr, ti = vr, vi
        elif 4 * k == count:
            if direction < 0:
                tr, ti = vi, -vr
            else:
                tr, ti = -vi, vr
        elif 8 * k == count:
            s = math.sqrt(0.5)
            if direction < 0:
                tr, ti = (vr + vi) * s, (vi - vr) * s
            else:
                tr, ti = (vr - vi) * s, (vi + vr) * s
        elif 8 * k == 3 * count:
            s = math.sqrt(0.5)
            if direction < 0:
                tr, ti = (vi - vr) * s, -(vr + vi) * s
            else:
                tr, ti = -(vr + vi) * s, (vr - vi) * s
        else:
            c = math.cos(2 * math.pi * k / count)
            s = direction * math.sin(2 * math.pi * k / count)
            tr, ti = vr * c - vi * s, vr * s + vi * c
        low.append((er + tr, ei + ti))
        high.append((er - tr, ei - ti))
    return low + high


def compress_kernel(
    shape, raw_hbm, filter_hbm, out_hbm, raw_ref, filter_ref, wide_ref, out_ref, raw_sems,
    filter_sems, out_sems,
):
    chunk, dates, step, targets, tiles, gates, lines = shape
    looks_rows = gates // ML_RG
    gates_in = raw_ref.shape[3]
    copies = [
        pltpu.make_async_copy(
            raw_hbm.at[pl.ds(first, step)], raw_ref.at[pl.ds(first, step)], raw_sems.at[first // step]
        )
        for first in range(0, dates, step)
    ]
    out_copies = [
        pltpu.make_async_copy(out_ref.at[:, date], out_hbm.at[:, date], out_sems.at[date])
        for date in range(dates)
    ]
    parts = 2
    held = targets // parts
    filter_copies = [
        pltpu.make_async_copy(
            filter_hbm.at[:, pl.ds(part * held, held), chunk],
            filter_ref.at[:, pl.ds(part * held, held)],
            filter_sems.at[part],
        )
        for part in range(parts)
    ]
    for copy in [filter_copies[0], *copies[:1], *filter_copies[1:], *copies[1:]]:
        copy.start()

    def product(w, x):
        return lax.dot_general(
            w, x, (((1,), (1,)), ((), ())), preferred_element_type=jnp.float32
        )

    for first in range(0, dates, step):
        copies[first // step].wait()
        raw = [
            raw_ref[first : first + step, part].reshape(step * lines, gates_in) for part in (0, 1)
        ]
        for group in range(parts):
            if first == 0:
                filter_copies[group].wait()
            weight = [
                filter_ref[part, group * held : (group + 1) * held].reshape(held * gates, gates_in)
                for part in (0, 1)
            ]
            real = product(weight[0], raw[0]) - product(weight[1], raw[1])
            imag = product(weight[1], raw[0]) + product(weight[0], raw[1])
            rows = slice(group * held * gates, (group + 1) * held * gates)
            for at in range(step):
                wide_ref[first + at, 0, rows] = real[:, at * lines : (at + 1) * lines]
                wide_ref[first + at, 1, rows] = imag[:, at * lines : (at + 1) * lines]
        for date in range(first, first + step):
            for target in range(targets):
                for tile in range(tiles):
                    rows = []
                    for part in (0, 1):
                        begin, count = tile * SUB, min(looks_rows, SUB)
                        for at in range(begin, begin + SUB, count):
                            gate = target * gates + at // looks_rows + ML_RG * (at % looks_rows)
                            rows.append(wide_ref[date, part, pl.ds(gate, count, stride=ML_RG), :])
                    out_ref[target, date, tile] = jnp.concatenate(rows, axis=0).astype(
                        jnp.bfloat16
                    )
            out_copies[date].start()
    for copy in out_copies:
        copy.wait()


def compress(raw_echo, filter_chunks, chunk):
    dates, _, lines, gates_in = raw_echo.shape
    _, targets, _, gates, _ = filter_chunks.shape
    tiles = gates // SUB
    step = 2 if dates % 2 == 0 else 1
    shape = (chunk, dates, step, targets, tiles, gates, lines)
    hbm = pl.BlockSpec(memory_space=pltpu.HBM)
    return pl.pallas_call(
        lambda *refs: compress_kernel(shape, *refs),
        out_shape=jax.ShapeDtypeStruct((targets, dates, tiles, 2 * SUB, lines), jnp.bfloat16),
        in_specs=[hbm, hbm],
        out_specs=pl.BlockSpec(memory_space=pl.ANY),
        scratch_shapes=[
            pltpu.VMEM(raw_echo.shape, jnp.bfloat16),
            pltpu.VMEM((2, targets, gates, gates_in), jnp.bfloat16),
            pltpu.VMEM((dates, 2, targets * gates, lines), jnp.float32),
            pltpu.VMEM((targets, dates, tiles, 2 * SUB, lines), jnp.bfloat16),
            pltpu.SemaphoreType.DMA((dates // step,)),
            pltpu.SemaphoreType.DMA((2,)),
            pltpu.SemaphoreType.DMA((dates,)),
        ],
        compiler_params=pltpu.CompilerParams(vmem_limit_bytes=VMEM_BYTES),
        cost_estimate=pl.CostEstimate(
            flops=8 * dates * lines * targets * gates * gates_in,
            bytes_accessed=4 * (raw_echo.size + targets * gates * gates_in),
            transcendentals=0,
        ),
        name="compress",
    )(*[pltpu.with_memory_space_constraint(x, pltpu.HBM) for x in (raw_echo, filter_chunks)])


def focus_kernel(
    shape, offset_ref, data_ref, cos_ref, sin_ref, turn_ref, fwd_ref, back_ref, out_ref, image_ref,
    look_ref,
):
    chunk, dates, blocks, tiles, gates, lines = shape
    looks_rows = gates // ML_RG
    look_lines = lines // ML_AZ
    for date in range(dates):
        for tile in range(tiles):
            parts = []
            for a in range(blocks):
                both = data_ref[a, date, tile].astype(jnp.float32)
                parts.append((both[:SUB], both[SUB:]))
            parts = small_dft(parts, -1)
            turned = []
            for a, (re, im) in enumerate(parts):
                tr, ti = turn_ref[0, a : a + 1], turn_ref[1, a : a + 1]
                turned.append((re * tr - im * ti, re * ti + im * tr))
            rows = jnp.concatenate(
                [jnp.concatenate([re, im], axis=1) for re, im in turned], axis=0
            ).astype(jnp.bfloat16)
            spectrum = jnp.dot(rows, fwd_ref[...], preferred_element_type=jnp.float32)
            re, im = spectrum[:, :lines], spectrum[:, lines:]
            pr, pi = cos_ref[chunk, tile], sin_ref[chunk, tile]
            rows = jnp.concatenate([re * pr - im * pi, re * pi + im * pr], axis=1).astype(
                jnp.bfloat16
            )
            back = jnp.dot(rows, back_ref[...], preferred_element_type=jnp.float32)
            parts = []
            for a in range(blocks):
                re = back[a * SUB : (a + 1) * SUB, :lines]
                im = back[a * SUB : (a + 1) * SUB, lines:]
                tr, ti = turn_ref[2, a : a + 1], turn_ref[3, a : a + 1]
                parts.append((re * tr - im * ti, re * ti + im * tr))
            parts = small_dft(parts, 1)
            for a, (re, im) in enumerate(parts):
                image_ref[date, tile, a, 0] = re
                image_ref[date, tile, a, 1] = im

    lane = lax.broadcasted_iota(jnp.int32, (SUB, lines), 1)
    first = lane < look_lines
    scale = 1.0 / (ML_RG * ML_AZ)
    for date in range(dates):
        partner = lax.rem(date + offset_ref[date], dates)
        for a in range(blocks):
            sums = {}
            for tile in range(tiles):
                cr, ci = image_ref[date, tile, a, 0], image_ref[date, tile, a, 1]
                pr, pi = image_ref[partner, tile, a, 0], image_ref[partner, tile, a, 1]
                re, im = cr * pr + ci * pi, ci * pr - cr * pi
                at = tile * SUB % looks_rows
                if at in sums:
                    re, im = re + sums[at][0], im + sums[at][1]
                sums[at] = (re, im)
            for at, (re, im) in sums.items():
                look = jnp.where(first, re, im) + pltpu.roll(
                    jnp.where(first, im, re), look_lines, 1
                )
                step = SUB
                while step > looks_rows:
                    step //= 2
                    look = look + pltpu.roll(look, step, 0)
                count = min(SUB, looks_rows)
                row = date * looks_rows + at
                look_ref[a, row : row + count, :] = (look * scale)[:count]

    small = lax.broadcasted_iota(jnp.int32, (looks_rows, lines), 1) % look_lines
    from_high, from_low = small < HALF, small >= look_lines - HALF
    zero = jnp.zeros((looks_rows, lines), jnp.float32)

    def rim(a, date):
        rows = slice(date * looks_rows, (date + 1) * looks_rows)
        high = look_ref[a + 1, rows, :] if a + 1 < blocks else zero
        low = look_ref[a - 1, rows, :] if a > 0 else zero
        return jnp.where(from_high, high, low)

    for a in range(blocks):
        for date in range(0, dates, 2):
            own = rim(a, date)
            other = pltpu.roll(rim(a, date + 1), look_lines // 2, 1)
            row = (dates + date // 2) * looks_rows
            look_ref[a, row : row + looks_rows, :] = jnp.where(from_high | from_low, own, other)
    out_ref[...] = look_ref[...].astype(jnp.bfloat16)


def phase_tables(azimuth_phase, chunks, blocks):
    gates, total = azimuth_phase.shape
    looks_rows = gates // chunks // ML_RG
    lines = total // blocks
    tiles = gates // chunks // SUB
    phase = azimuth_phase.reshape(chunks, looks_rows, ML_RG, lines, blocks)
    phase = phase.transpose(0, 2, 1, 4, 3).reshape(chunks, tiles, SUB, blocks, lines)
    phase = phase.transpose(0, 1, 3, 2, 4).reshape(chunks, tiles, blocks * SUB, lines)
    phase = lax.optimization_barrier(phase)
    return jnp.cos(phase), jnp.sin(phase)


def focus_tables(blocks, lines):
    total = blocks * lines
    order = line_order(lines)
    ahead = wave(np.arange(blocks), np.arange(lines), total, -1)
    behind = wave(np.arange(blocks), order, total, 1)
    turn = np.stack([ahead.real, ahead.imag, behind.real, behind.imag]).astype(np.float32)
    fwd = as_bf16(real_block(wave(np.arange(lines), np.arange(lines), lines, -1)))
    back = as_bf16(real_block(wave(np.arange(lines), order, lines, 1) / total))
    return jnp.asarray(turn), fwd, back


def staged(tables, after):
    count = len(tables)

    def kernel(*refs):
        sems = refs[-1]
        copies = [
            pltpu.make_async_copy(source, target, sems.at[index])
            for index, (source, target) in enumerate(zip(refs[:count], refs[count + 1 : -1]))
        ]
        for copy in copies:
            copy.start()
        for copy in copies:
            copy.wait()

    return pl.pallas_call(
        kernel,
        out_shape=[jax.ShapeDtypeStruct(table.shape, table.dtype) for table in tables],
        in_specs=[pl.BlockSpec(memory_space=pltpu.HBM)] * count
        + [pl.BlockSpec(memory_space=pl.ANY)],
        out_specs=[pl.BlockSpec(memory_space=pltpu.VMEM)] * count,
        scratch_shapes=[pltpu.SemaphoreType.DMA((count,))],
        compiler_params=pltpu.CompilerParams(vmem_limit_bytes=VMEM_BYTES),
        cost_estimate=pl.CostEstimate(
            flops=0, bytes_accessed=4 * sum(table.size for table in tables), transcendentals=0
        ),
        name="staged",
    )(*[pltpu.with_memory_space_constraint(table, pltpu.HBM) for table in tables], after)


def focus(columns, pair_offset, phases, tables, chunk):
    blocks, dates, tiles, _, lines = columns.shape
    gates = tiles * SUB
    looks_rows = gates // ML_RG
    slots = dates + dates // 2
    shape = (chunk, dates, blocks, tiles, gates, lines)
    whole = pl.BlockSpec(memory_space=pltpu.VMEM)
    return pl.pallas_call(
        lambda *refs: focus_kernel(shape, *refs),
        out_shape=jax.ShapeDtypeStruct((blocks, slots * looks_rows, lines), jnp.bfloat16),
        in_specs=[pl.BlockSpec(memory_space=pltpu.SMEM)] + [whole] * 6,
        out_specs=whole,
        scratch_shapes=[
            pltpu.VMEM((dates, tiles, blocks, 2, SUB, lines), jnp.float32),
            pltpu.VMEM((blocks, slots * looks_rows, lines), jnp.float32),
        ],
        compiler_params=pltpu.CompilerParams(vmem_limit_bytes=VMEM_BYTES),
        cost_estimate=pl.CostEstimate(
            flops=16 * dates * gates * blocks * lines * lines,
            bytes_accessed=4 * columns.size,
            transcendentals=0,
        ),
        name="focus",
    )(pair_offset, columns, *phases, *tables)


def tri_window(offset):
    inside = (offset >= 0) & (offset < PATCH)
    return np.where(inside, 1.0 - np.abs(offset - (PATCH - 1) / 2.0) / HALF, 0.0)


def patch_tables(cells, starts):
    offset = np.asarray(cells)[:, None] - np.asarray(starts)[None, :]
    inside = ((offset >= 0) & (offset < PATCH)).astype(np.float64)
    angle = 2.0 * math.pi / PATCH * (offset[:, :, None] * np.arange(PATCH) % PATCH)
    ahead = np.exp(-1j * angle) * inside[:, :, None]
    behind = np.exp(1j * angle) * tri_window(offset)[:, :, None] / PATCH
    flat = (len(cells), len(starts) * PATCH)
    return ahead.reshape(flat), behind.reshape(flat).T


def goldstein_tables(dates, gate_order, line_looks):
    per = LANES // PATCH
    starts = np.arange(-HALF, line_looks, HALF)
    cells = np.arange(-HALF, line_looks + HALF)
    ahead, behind = patch_tables(cells, starts)
    main = slice(HALF, HALF + line_looks)
    behind = behind[:, main]
    split = per * PATCH

    def lanes_of(table, shift):
        block = np.zeros((2, line_looks, table.shape[1]), complex)
        block[0], block[1] = table[main], 1j * table[main]
        rim = np.zeros((2, line_looks, table.shape[1]), complex)
        for part, turn in enumerate((1.0, 1j)):
            rim[part, :HALF] = turn * table[HALF + line_looks :]
            rim[part, line_looks - HALF :] = turn * table[:HALF]
        flat = (2 * line_looks, table.shape[1])
        return block.reshape(flat), np.roll(rim.reshape(flat), shift, axis=0)

    def out_parts(table):
        return np.concatenate([table.real, table.imag], axis=1)

    near = [
        out_parts(np.concatenate(lanes_of(ahead[:, :split], parity * (line_looks // 2))))
        for parity in (0, 1)
    ]
    rest = ahead.shape[1] - split
    far_block = np.zeros((dates, 2 * line_looks, dates, rest), complex)
    far_rim = np.zeros((dates // 2, 2 * line_looks, dates, rest), complex)
    for date in range(dates):
        block, rim = lanes_of(ahead[:, split:], date % 2 * (line_looks // 2))
        far_block[date, :, date] = block
        far_rim[date // 2, :, date] = rim
    far = np.concatenate([far_block, far_rim]).reshape(-1, dates * rest)
    gate_starts = np.arange(-HALF, len(gate_order), HALF)
    gate_ahead, gate_behind = patch_tables(np.arange(len(gate_order)), gate_starts)
    ahead_rows = real_block(gate_ahead[gate_order]).T
    behind_rows = real_block(gate_behind).T

    lines_back = []
    for date in range(dates):
        far_back = np.zeros((dates, rest, line_looks), complex)
        far_back[date] = behind[split:]
        lines_back.append(
            np.concatenate(
                [real_block(behind[:split]), real_block(far_back.reshape(-1, line_looks))]
            ).T
        )
    gap = (np.arange(PATCH)[:, None] - np.arange(PATCH)[None, :]) % PATCH
    ring = ((gap == 0) | (gap == 1) | (gap == PATCH - 1)).astype(np.float64)
    box = np.concatenate(
        [np.kron(np.eye(per), ring), np.kron(np.eye(per), np.ones((PATCH, PATCH)))], axis=1
    )
    tables = (np.stack(near), out_parts(far), ahead_rows, box, behind_rows, np.stack(lines_back))
    return [as_bf16(table) for table in tables]


def slot_rows(data_ref, slots, looks_rows):
    blocks = data_ref.shape[0]
    data = data_ref[...].astype(jnp.float32)
    if looks_rows % SUB == 0:
        return [
            data[:, slot * looks_rows : (slot + 1) * looks_rows].reshape(-1, LANES)
            for slot in range(slots)
        ]
    top = lax.broadcasted_iota(jnp.int32, (SUB, LANES), 0) < looks_rows
    held = [[] for _ in range(slots)]
    for block in range(0, blocks, 2):
        for slot in range(0, slots, 2):
            rows = slice(slot * looks_rows, (slot + 2) * looks_rows)
            one, two = data[block, rows], data[block + 1, rows]
            held[slot].append(jnp.where(top, one, pltpu.roll(two, looks_rows, 0)))
            held[slot + 1].append(jnp.where(top, pltpu.roll(one, looks_rows, 0), two))
    return [jnp.concatenate(rows, axis=0) for rows in held]


def goldstein_kernel(shape, *refs):
    dates, chunks, looks_rows, gate_looks, line_looks = shape
    data_refs, refs = refs[:chunks], refs[chunks:]
    near_ref, far_ref, ahead_ref, box_ref, behind_ref, back_ref, out_ref = refs[:7]
    half_ref, spec_ref, weighted_ref = refs[7:]
    slots = dates + dates // 2
    cols = dates + 1
    dot = lambda a, b: jnp.dot(a, b, preferred_element_type=jnp.float32)
    if data_refs[0].shape[0] == slots:
        held = [data_refs[0][slot] for slot in range(slots)]
    else:
        held = zip(*[slot_rows(ref, slots, looks_rows) for ref in data_refs])
        held = [jnp.concatenate(rows, axis=0).astype(jnp.bfloat16) for rows in held]
    for parity in (0, 1):
        rows = jnp.concatenate(
            [
                jnp.concatenate([held[date], held[dates + date // 2]], axis=1)
                for date in range(parity, dates, 2)
            ],
            axis=0,
        )
        both = dot(rows, near_ref[parity]).astype(jnp.bfloat16)
        for index, date in enumerate(range(parity, dates, 2)):
            mine = both[index * gate_looks : (index + 1) * gate_looks]
            half_ref[:gate_looks, date * LANES : (date + 1) * LANES] = mine[:, :LANES]
            half_ref[gate_looks:, date * LANES : (date + 1) * LANES] = mine[:, LANES:]
    both = dot(jnp.concatenate(held, axis=1), far_ref[...]).astype(jnp.bfloat16)
    half_ref[:gate_looks, dates * LANES :] = both[:, :LANES]
    half_ref[gate_looks:, dates * LANES :] = both[:, LANES:]

    spec_ref[...] = dot(ahead_ref[...], half_ref[...])
    bins = ahead_ref.shape[0] // 2
    for col in range(cols):
        lanes = slice(col * LANES, (col + 1) * LANES)
        re, im = spec_ref[:bins, lanes], spec_ref[bins:, lanes]
        power = (re * re + im * im).astype(jnp.bfloat16)
        sums = dot(power, box_ref[...])
        for start in range(0, bins, PATCH):
            rows = slice(start, start + PATCH)
            line = sums[rows, :LANES]
            total = jnp.sum(sums[rows, LANES:], axis=0, keepdims=True)
            smooth = line + pltpu.roll(line, 1, 0) + pltpu.roll(line, PATCH - 1, 0)
            level = total * (1.0 / (PATCH * PATCH)) + LEVEL_FLOOR
            weight = jnp.sqrt(smooth * (1.0 / (9.0 * level)) + BOX_FLOOR)
            weighted_ref[rows, lanes] = (re[rows] * weight).astype(jnp.bfloat16)
            weighted_ref[start + bins : start + bins + PATCH, lanes] = (im[rows] * weight).astype(
                jnp.bfloat16
            )
    inverse = dot(behind_ref[...], weighted_ref[...]).astype(jnp.bfloat16)
    far = [inverse[:gate_looks, dates * LANES :], inverse[gate_looks:, dates * LANES :]]
    for date in range(dates):
        lanes = slice(date * LANES, (date + 1) * LANES)
        rows = jnp.concatenate([inverse[:gate_looks, lanes], inverse[gate_looks:, lanes]] + far, axis=1)
        result = lax.dot_general(
            back_ref[date], rows, (((1,), (1,)), ((), ())), preferred_element_type=jnp.float32
        )
        out_ref[date, 0] = result[:line_looks]
        out_ref[date, 1] = result[line_looks:]


def goldstein(looks, dates, line_looks):
    chunks = len(looks)
    blocks, rows, _ = looks[0].shape
    slots = dates + dates // 2
    looks_rows = rows // slots
    gate_looks = chunks * blocks * looks_rows
    order = np.arange(gate_looks).reshape(blocks, chunks, looks_rows).swapaxes(0, 1).reshape(-1)
    if looks_rows % SUB and 2 * looks_rows != SUB:
        looks = [
            each.reshape(blocks, slots, looks_rows, LANES)
            .swapaxes(0, 1)
            .reshape(slots, blocks * looks_rows, LANES)
            for each in looks
        ]
        looks = [jnp.concatenate(looks, axis=1)]
    tables = goldstein_tables(dates, order, line_looks)
    bins = tables[2].shape[0] // 2
    width = (dates + 1) * LANES
    shape = (dates, len(looks), looks_rows, gate_looks, line_looks)
    whole = pl.BlockSpec(memory_space=pltpu.VMEM)
    filtered = pl.pallas_call(
        lambda *refs: goldstein_kernel(shape, *refs),
        out_shape=jax.ShapeDtypeStruct((dates, 2, line_looks, gate_looks), jnp.float32),
        in_specs=[whole] * (len(looks) + len(tables)),
        out_specs=whole,
        scratch_shapes=[
            pltpu.VMEM((2 * gate_looks, width), jnp.bfloat16),
            pltpu.VMEM((2 * bins, width), jnp.float32),
            pltpu.VMEM((2 * bins, width), jnp.bfloat16),
        ],
        compiler_params=pltpu.CompilerParams(vmem_limit_bytes=VMEM_BYTES),
        name="goldstein",
    )(*looks, *tables)
    return filtered.swapaxes(2, 3)


def body(raw_echo, range_filter, azimuth_phase, pair_offset):
    dates, _, lines, gates_in = raw_echo.shape
    devices = lax.axis_size("lines")
    gates = azimuth_phase.shape[0]
    chunks = 1
    filter_chunks = range_filter.reshape(2, devices, chunks, gates // chunks, gates_in)
    phases = phase_tables(azimuth_phase, chunks, devices)

    def exchange(blocks):
        return lax.all_to_all(blocks, "lines", split_axis=0, concat_axis=0, tiled=True)

    sent = compress(raw_echo, filter_chunks, 0)
    tables = staged(focus_tables(devices, lines), sent)
    looks = [exchange(focus(exchange(sent), pair_offset, phases, tables, 0))]
    return goldstein(looks, dates, lines // ML_AZ)


def solution(mesh):
    placed = (P("groups", None, "lines", None), P(), P("lines", None), P())
    return jax.shard_map(
        body,
        mesh=mesh,
        in_specs=placed,
        out_specs=P("groups", None, None, "lines"),
        check_vma=False,
    )
```

```python
import math

import jax
import jax.numpy as jnp
import numpy as np
from jax import lax
from jax.experimental import pallas as pl
from jax.experimental.pallas import tpu as pltpu
from jax.sharding import PartitionSpec as P

ML_RG = 4
ML_AZ = 2
PATCH = 32
HALF = PATCH // 2
BOX_FLOOR = 0.25
LEVEL_FLOOR = 1e-06
SUB = 8
LANES = 128
VMEM_BYTES = 20 * 1024 * 1024


def real_block(table):
    return np.block([[table.real, table.imag], [-table.imag, table.real]])


def wave(rows, cols, period, direction):
    product = np.asarray(rows)[:, None] * np.asarray(cols)[None, :] % period
    return np.exp(direction * 2j * math.pi / period * product)


def as_bf16(table):
    return jnp.asarray(np.asarray(table, np.float32), jnp.bfloat16)


def line_order(line_len):
    return np.arange(line_len).reshape(line_len // ML_AZ, ML_AZ).T.reshape(-1)


def small_dft(parts, direction):
    count = len(parts)
    if count == 1:
        return parts
    even = small_dft(parts[0::2], direction)
    odd = small_dft(parts[1::2], direction)
    low, high = [], []
    for k in range(count // 2):
        (er, ei), (vr, vi) = even[k], odd[k]
        if k == 0:
            tr, ti = vr, vi
        elif 4 * k == count:
            if direction < 0:
                tr, ti = vi, -vr
            else:
                tr, ti = -vi, vr
        elif 8 * k == count:
            s = math.sqrt(0.5)
            if direction < 0:
                tr, ti = (vr + vi) * s, (vi - vr) * s
            else:
                tr, ti = (vr - vi) * s, (vi + vr) * s
        elif 8 * k == 3 * count:
            s = math.sqrt(0.5)
            if direction < 0:
                tr, ti = (vi - vr) * s, -(vr + vi) * s
            else:
                tr, ti = -(vr + vi) * s, (vr - vi) * s
        else:
            c = math.cos(2 * math.pi * k / count)
            s = direction * math.sin(2 * math.pi * k / count)
            tr, ti = vr * c - vi * s, vr * s + vi * c
        low.append((er + tr, ei + ti))
        high.append((er - tr, ei - ti))
    return low + high


def compress_kernel(
    shape, raw_hbm, filter_hbm, out_hbm, raw_ref, filter_ref, wide_ref, out_ref, raw_sems,
    filter_sems, out_sems,
):
    chunk, dates, step, targets, tiles, gates, lines = shape
    looks_rows = gates // ML_RG
    gates_in = raw_ref.shape[3]
    copies = [
        pltpu.make_async_copy(
            raw_hbm.at[date, part], raw_ref.at[date, part], raw_sems.at[date, part]
        )
        for date in range(dates)
        for part in (0, 1)
    ]
    out_copies = [
        pltpu.make_async_copy(out_ref.at[:, date], out_hbm.at[:, date], out_sems.at[date])
        for date in range(dates)
    ]
    parts = 2
    held = targets // parts
    filter_copies = [
        pltpu.make_async_copy(
            filter_hbm.at[side, pl.ds(part * held, held), chunk],
            filter_ref.at[side, pl.ds(part * held, held)],
            filter_sems.at[part, side],
        )
        for part in range(parts)
        for side in (0, 1)
    ]
    early = 2 * step
    for copy in filter_copies[:2] + copies[:early] + filter_copies[2:] + copies[early:]:
        copy.start()

    def product(w, x):
        return lax.dot_general(
            w, x, (((1,), (1,)), ((), ())), preferred_element_type=jnp.float32
        )

    for first in range(0, dates, step):
        for copy in copies[2 * first : 2 * (first + step)]:
            copy.wait()
        raw = [
            raw_ref[first : first + step, part].reshape(step * lines, gates_in) for part in (0, 1)
        ]
        for group in range(parts):
            if first == 0:
                filter_copies[2 * group].wait()
                filter_copies[2 * group + 1].wait()
            weight = [
                filter_ref[part, group * held : (group + 1) * held].reshape(held * gates, gates_in)
                for part in (0, 1)
            ]
            real = product(weight[0], raw[0]) - product(weight[1], raw[1])
            imag = product(weight[1], raw[0]) + product(weight[0], raw[1])
            rows = slice(group * held * gates, (group + 1) * held * gates)
            for at in range(step):
                wide_ref[first + at, 0, rows] = real[:, at * lines : (at + 1) * lines]
                wide_ref[first + at, 1, rows] = imag[:, at * lines : (at + 1) * lines]
        for date in range(first, first + step):
            for target in range(targets):
                for tile in range(tiles):
                    rows = []
                    for part in (0, 1):
                        begin, count = tile * SUB, min(looks_rows, SUB)
                        for at in range(begin, begin + SUB, count):
                            gate = target * gates + at // looks_rows + ML_RG * (at % looks_rows)
                            rows.append(wide_ref[date, part, pl.ds(gate, count, stride=ML_RG), :])
                    out_ref[target, date, tile] = jnp.concatenate(rows, axis=0).astype(
                        jnp.bfloat16
                    )
            out_copies[date].start()
    for copy in out_copies:
        copy.wait()


def compress(raw_echo, filter_chunks, chunk):
    dates, _, lines, gates_in = raw_echo.shape
    _, targets, _, gates, _ = filter_chunks.shape
    tiles = gates // SUB
    step = 2 if dates % 2 == 0 else 1
    shape = (chunk, dates, step, targets, tiles, gates, lines)
    hbm = pl.BlockSpec(memory_space=pltpu.HBM)
    return pl.pallas_call(
        lambda *refs: compress_kernel(shape, *refs),
        out_shape=jax.ShapeDtypeStruct((targets, dates, tiles, 2 * SUB, lines), jnp.bfloat16),
        in_specs=[hbm, hbm],
        out_specs=pl.BlockSpec(memory_space=pl.ANY),
        scratch_shapes=[
            pltpu.VMEM(raw_echo.shape, jnp.bfloat16),
            pltpu.VMEM((2, targets, gates, gates_in), jnp.bfloat16),
            pltpu.VMEM((dates, 2, targets * gates, lines), jnp.float32),
            pltpu.VMEM((targets, dates, tiles, 2 * SUB, lines), jnp.bfloat16),
            pltpu.SemaphoreType.DMA((dates, 2)),
            pltpu.SemaphoreType.DMA((2, 2)),
            pltpu.SemaphoreType.DMA((dates,)),
        ],
        compiler_params=pltpu.CompilerParams(vmem_limit_bytes=VMEM_BYTES),
        cost_estimate=pl.CostEstimate(
            flops=8 * dates * lines * targets * gates * gates_in,
            bytes_accessed=4 * (raw_echo.size + targets * gates * gates_in),
            transcendentals=0,
        ),
        name="compress",
    )(*[pltpu.with_memory_space_constraint(x, pltpu.HBM) for x in (raw_echo, filter_chunks)])


def focus_kernel(
    shape, offset_ref, data_ref, cos_ref, sin_ref, turn_ref, table_ref, out_ref, image_ref, look_ref,
):
    chunk, dates, blocks, tiles, gates, lines = shape
    looks_rows = gates // ML_RG
    look_lines = lines // ML_AZ
    count = blocks * SUB
    for date in range(dates):
        rows = []
        for tile in range(tiles):
            parts = []
            for a in range(blocks):
                both = data_ref[a, date, tile].astype(jnp.float32)
                parts.append((both[:SUB], both[SUB:]))
            for a, (re, im) in enumerate(small_dft(parts, -1)):
                tr, ti = turn_ref[0, a : a + 1], turn_ref[1, a : a + 1]
                rows.append(jnp.concatenate([re * tr - im * ti, re * ti + im * tr], axis=1))
        rows = jnp.concatenate(rows, axis=0).astype(jnp.bfloat16)
        spectrum = jnp.dot(rows, table_ref[0], preferred_element_type=jnp.float32)
        rows = []
        for tile in range(tiles):
            re = spectrum[tile * count : (tile + 1) * count, :lines]
            im = spectrum[tile * count : (tile + 1) * count, lines:]
            pr, pi = cos_ref[chunk, tile], sin_ref[chunk, tile]
            rows.append(jnp.concatenate([re * pr - im * pi, re * pi + im * pr], axis=1))
        rows = jnp.concatenate(rows, axis=0).astype(jnp.bfloat16)
        back = jnp.dot(rows, table_ref[1], preferred_element_type=jnp.float32)
        for tile in range(tiles):
            parts = []
            for a in range(blocks):
                row = tile * count + a * SUB
                re, im = back[row : row + SUB, :lines], back[row : row + SUB, lines:]
                tr, ti = turn_ref[2, a : a + 1], turn_ref[3, a : a + 1]
                parts.append((re * tr - im * ti, re * ti + im * tr))
            for a, (re, im) in enumerate(small_dft(parts, 1)):
                image_ref[date, tile, a, 0] = re
                image_ref[date, tile, a, 1] = im

    lane = lax.broadcasted_iota(jnp.int32, (SUB, lines), 1)
    first = lane < look_lines
    scale = 1.0 / (ML_RG * ML_AZ)
    for date in range(dates):
        partner = lax.rem(date + offset_ref[date], dates)
        for a in range(blocks):
            sums = {}
            for tile in range(tiles):
                cr, ci = image_ref[date, tile, a, 0], image_ref[date, tile, a, 1]
                pr, pi = image_ref[partner, tile, a, 0], image_ref[partner, tile, a, 1]
                re, im = cr * pr + ci * pi, ci * pr - cr * pi
                at = tile * SUB % looks_rows
                if at in sums:
                    re, im = re + sums[at][0], im + sums[at][1]
                sums[at] = (re, im)
            for at, (re, im) in sums.items():
                look = jnp.where(first, re, im) + pltpu.roll(
                    jnp.where(first, im, re), look_lines, 1
                )
                step = SUB
                while step > looks_rows:
                    step //= 2
                    look = look + pltpu.roll(look, step, 0)
                count = min(SUB, looks_rows)
                row = date * looks_rows + at
                look_ref[a, row : row + count, :] = (look * scale)[:count]

    small = lax.broadcasted_iota(jnp.int32, (looks_rows, lines), 1) % look_lines
    from_high, from_low = small < HALF, small >= look_lines - HALF
    zero = jnp.zeros((looks_rows, lines), jnp.float32)

    def rim(a, date):
        rows = slice(date * looks_rows, (date + 1) * looks_rows)
        high = look_ref[a + 1, rows, :] if a + 1 < blocks else zero
        low = look_ref[a - 1, rows, :] if a > 0 else zero
        return jnp.where(from_high, high, low)

    for a in range(blocks):
        for date in range(0, dates, 2):
            own = rim(a, date)
            other = pltpu.roll(rim(a, date + 1), look_lines // 2, 1)
            row = (dates + date // 2) * looks_rows
            look_ref[a, row : row + looks_rows, :] = jnp.where(from_high | from_low, own, other)
    out_ref[...] = look_ref[...].astype(jnp.bfloat16)


def phase_tables(azimuth_phase, chunks, blocks):
    gates, total = azimuth_phase.shape
    looks_rows = gates // chunks // ML_RG
    lines = total // blocks
    tiles = gates // chunks // SUB
    phase = azimuth_phase.reshape(chunks, looks_rows, ML_RG, lines, blocks)
    phase = phase.transpose(0, 2, 1, 4, 3).reshape(chunks, tiles, SUB, blocks, lines)
    phase = phase.transpose(0, 1, 3, 2, 4).reshape(chunks, tiles, blocks * SUB, lines)
    phase = lax.optimization_barrier(phase)
    return jnp.cos(phase), jnp.sin(phase)


def focus_tables(blocks, lines):
    total = blocks * lines
    order = line_order(lines)
    ahead = wave(np.arange(blocks), np.arange(lines), total, -1)
    behind = wave(np.arange(blocks), order, total, 1)
    turn = np.stack([ahead.real, ahead.imag, behind.real, behind.imag]).astype(np.float32)
    fwd = real_block(wave(np.arange(lines), np.arange(lines), lines, -1))
    back = real_block(wave(np.arange(lines), order, lines, 1) / total)
    return jnp.asarray(turn), as_bf16(np.stack([fwd, back]))


def focus(columns, pair_offset, phases, tables, chunk):
    blocks, dates, tiles, _, lines = columns.shape
    gates = tiles * SUB
    looks_rows = gates // ML_RG
    slots = dates + dates // 2
    shape = (chunk, dates, blocks, tiles, gates, lines)
    whole = pl.BlockSpec(memory_space=pltpu.VMEM)
    return pl.pallas_call(
        lambda *refs: focus_kernel(shape, *refs),
        out_shape=jax.ShapeDtypeStruct((blocks, slots * looks_rows, lines), jnp.bfloat16),
        in_specs=[pl.BlockSpec(memory_space=pltpu.SMEM)] + [whole] * 5,
        out_specs=whole,
        scratch_shapes=[
            pltpu.VMEM((dates, tiles, blocks, 2, SUB, lines), jnp.float32),
            pltpu.VMEM((blocks, slots * looks_rows, lines), jnp.float32),
        ],
        compiler_params=pltpu.CompilerParams(vmem_limit_bytes=VMEM_BYTES),
        cost_estimate=pl.CostEstimate(
            flops=16 * dates * gates * blocks * lines * lines,
            bytes_accessed=4 * columns.size,
            transcendentals=0,
        ),
        name="focus",
    )(pair_offset, columns, *phases, *tables)


def tri_window(offset):
    inside = (offset >= 0) & (offset < PATCH)
    return np.where(inside, 1.0 - np.abs(offset - (PATCH - 1) / 2.0) / HALF, 0.0)


def patch_tables(cells, starts):
    offset = np.asarray(cells)[:, None] - np.asarray(starts)[None, :]
    inside = ((offset >= 0) & (offset < PATCH)).astype(np.float64)
    angle = 2.0 * math.pi / PATCH * (offset[:, :, None] * np.arange(PATCH) % PATCH)
    ahead = np.exp(-1j * angle) * inside[:, :, None]
    behind = np.exp(1j * angle) * tri_window(offset)[:, :, None] / PATCH
    flat = (len(cells), len(starts) * PATCH)
    return ahead.reshape(flat), behind.reshape(flat).T


def goldstein_tables(dates, gate_order, line_looks):
    per = LANES // PATCH
    starts = np.arange(-HALF, line_looks, HALF)
    cells = np.arange(-HALF, line_looks + HALF)
    ahead, behind = patch_tables(cells, starts)
    main = slice(HALF, HALF + line_looks)
    behind = behind[:, main]
    split = per * PATCH

    def lanes_of(table, shift):
        block = np.zeros((2, line_looks, table.shape[1]), complex)
        block[0], block[1] = table[main], 1j * table[main]
        rim = np.zeros((2, line_looks, table.shape[1]), complex)
        for part, turn in enumerate((1.0, 1j)):
            rim[part, :HALF] = turn * table[HALF + line_looks :]
            rim[part, line_looks - HALF :] = turn * table[:HALF]
        flat = (2 * line_looks, table.shape[1])
        return block.reshape(flat), np.roll(rim.reshape(flat), shift, axis=0)

    def out_parts(table):
        return np.concatenate([table.real, table.imag], axis=1)

    near = [
        out_parts(np.concatenate(lanes_of(ahead[:, :split], parity * (line_looks // 2))))
        for parity in (0, 1)
    ]
    rest = ahead.shape[1] - split
    far_block = np.zeros((dates, 2 * line_looks, dates, rest), complex)
    far_rim = np.zeros((dates // 2, 2 * line_looks, dates, rest), complex)
    for date in range(dates):
        block, rim = lanes_of(ahead[:, split:], date % 2 * (line_looks // 2))
        far_block[date, :, date] = block
        far_rim[date // 2, :, date] = rim
    far = np.concatenate([far_block, far_rim]).reshape(-1, dates * rest)
    gate_starts = np.arange(-HALF, len(gate_order), HALF)
    gate_ahead, gate_behind = patch_tables(np.arange(len(gate_order)), gate_starts)
    ahead_rows = real_block(gate_ahead[gate_order]).T
    behind_rows = real_block(gate_behind).T

    lines_back = []
    for date in range(dates):
        far_back = np.zeros((dates, rest, line_looks), complex)
        far_back[date] = behind[split:]
        lines_back.append(
            np.concatenate(
                [real_block(behind[:split]), real_block(far_back.reshape(-1, line_looks))]
            ).T
        )
    gap = (np.arange(PATCH)[:, None] - np.arange(PATCH)[None, :]) % PATCH
    ring = ((gap == 0) | (gap == 1) | (gap == PATCH - 1)).astype(np.float64)
    box = np.concatenate(
        [np.kron(np.eye(per), ring), np.kron(np.eye(per), np.ones((PATCH, PATCH)))], axis=1
    )
    tables = (np.stack(near), out_parts(far), ahead_rows, box, behind_rows, np.stack(lines_back))
    return [as_bf16(table) for table in tables]


def slot_rows(data_ref, slots, looks_rows):
    blocks = data_ref.shape[0]
    data = data_ref[...].astype(jnp.float32)
    if looks_rows % SUB == 0:
        return [
            data[:, slot * looks_rows : (slot + 1) * looks_rows].reshape(-1, LANES)
            for slot in range(slots)
        ]
    top = lax.broadcasted_iota(jnp.int32, (SUB, LANES), 0) < looks_rows
    held = [[] for _ in range(slots)]
    for block in range(0, blocks, 2):
        for slot in range(0, slots, 2):
            rows = slice(slot * looks_rows, (slot + 2) * looks_rows)
            one, two = data[block, rows], data[block + 1, rows]
            held[slot].append(jnp.where(top, one, pltpu.roll(two, looks_rows, 0)))
            held[slot + 1].append(jnp.where(top, pltpu.roll(one, looks_rows, 0), two))
    return [jnp.concatenate(rows, axis=0) for rows in held]


def goldstein_kernel(shape, *refs):
    dates, chunks, looks_rows, gate_looks, line_looks = shape
    data_refs, refs = refs[:chunks], refs[chunks:]
    near_ref, far_ref, ahead_ref, box_ref, behind_ref, back_ref, out_ref = refs[:7]
    half_ref, spec_ref, weighted_ref = refs[7:]
    slots = dates + dates // 2
    cols = dates + 1
    dot = lambda a, b: jnp.dot(a, b, preferred_element_type=jnp.float32)
    if data_refs[0].shape[0] == slots:
        held = [data_refs[0][slot] for slot in range(slots)]
    else:
        held = zip(*[slot_rows(ref, slots, looks_rows) for ref in data_refs])
        held = [jnp.concatenate(rows, axis=0).astype(jnp.bfloat16) for rows in held]
    for parity in (0, 1):
        rows = jnp.concatenate(
            [
                jnp.concatenate([held[date], held[dates + date // 2]], axis=1)
                for date in range(parity, dates, 2)
            ],
            axis=0,
        )
        both = dot(rows, near_ref[parity]).astype(jnp.bfloat16)
        for index, date in enumerate(range(parity, dates, 2)):
            mine = both[index * gate_looks : (index + 1) * gate_looks]
            half_ref[:gate_looks, date * LANES : (date + 1) * LANES] = mine[:, :LANES]
            half_ref[gate_looks:, date * LANES : (date + 1) * LANES] = mine[:, LANES:]
    both = dot(jnp.concatenate(held, axis=1), far_ref[...]).astype(jnp.bfloat16)
    half_ref[:gate_looks, dates * LANES :] = both[:, :LANES]
    half_ref[gate_looks:, dates * LANES :] = both[:, LANES:]

    spec_ref[...] = dot(ahead_ref[...], half_ref[...])
    bins = ahead_ref.shape[0] // 2
    for col in range(cols):
        lanes = slice(col * LANES, (col + 1) * LANES)
        re, im = spec_ref[:bins, lanes], spec_ref[bins:, lanes]
        power = (re * re + im * im).astype(jnp.bfloat16)
        sums = dot(power, box_ref[...])
        for start in range(0, bins, PATCH):
            rows = slice(start, start + PATCH)
            line = sums[rows, :LANES]
            total = jnp.sum(sums[rows, LANES:], axis=0, keepdims=True)
            smooth = line + pltpu.roll(line, 1, 0) + pltpu.roll(line, PATCH - 1, 0)
            level = total * (1.0 / (PATCH * PATCH)) + LEVEL_FLOOR
            square = smooth * (1.0 / (9.0 * level)) + BOX_FLOOR
            weight = square * lax.rsqrt(square)
            weighted_ref[rows, lanes] = (re[rows] * weight).astype(jnp.bfloat16)
            weighted_ref[start + bins : start + bins + PATCH, lanes] = (im[rows] * weight).astype(
                jnp.bfloat16
            )
    inverse = dot(behind_ref[...], weighted_ref[...]).astype(jnp.bfloat16)
    far = [inverse[:gate_looks, dates * LANES :], inverse[gate_looks:, dates * LANES :]]
    for date in range(dates):
        lanes = slice(date * LANES, (date + 1) * LANES)
        rows = jnp.concatenate([inverse[:gate_looks, lanes], inverse[gate_looks:, lanes]] + far, axis=1)
        result = lax.dot_general(
            back_ref[date], rows, (((1,), (1,)), ((), ())), preferred_element_type=jnp.float32
        )
        out_ref[date, 0] = result[:line_looks]
        out_ref[date, 1] = result[line_looks:]


def goldstein(looks, dates, line_looks):
    chunks = len(looks)
    blocks, rows, _ = looks[0].shape
    slots = dates + dates // 2
    looks_rows = rows // slots
    gate_looks = chunks * blocks * looks_rows
    order = np.arange(gate_looks).reshape(blocks, chunks, looks_rows).swapaxes(0, 1).reshape(-1)
    if looks_rows % SUB and 2 * looks_rows != SUB:
        looks = [
            each.reshape(blocks, slots, looks_rows, LANES)
            .swapaxes(0, 1)
            .reshape(slots, blocks * looks_rows, LANES)
            for each in looks
        ]
        looks = [jnp.concatenate(looks, axis=1)]
    tables = goldstein_tables(dates, order, line_looks)
    bins = tables[2].shape[0] // 2
    width = (dates + 1) * LANES
    shape = (dates, len(looks), looks_rows, gate_looks, line_looks)
    whole = pl.BlockSpec(memory_space=pltpu.VMEM)
    filtered = pl.pallas_call(
        lambda *refs: goldstein_kernel(shape, *refs),
        out_shape=jax.ShapeDtypeStruct((dates, 2, line_looks, gate_looks), jnp.float32),
        in_specs=[whole] * (len(looks) + len(tables)),
        out_specs=whole,
        scratch_shapes=[
            pltpu.VMEM((2 * gate_looks, width), jnp.bfloat16),
            pltpu.VMEM((2 * bins, width), jnp.float32),
            pltpu.VMEM((2 * bins, width), jnp.bfloat16),
        ],
        compiler_params=pltpu.CompilerParams(vmem_limit_bytes=VMEM_BYTES),
        name="goldstein",
    )(*looks, *tables)
    return filtered.swapaxes(2, 3)


def body(raw_echo, range_filter, azimuth_phase, pair_offset):
    dates, _, lines, gates_in = raw_echo.shape
    devices = lax.axis_size("lines")
    gates = azimuth_phase.shape[0]
    chunks = 1
    filter_chunks = range_filter.reshape(2, devices, chunks, gates // chunks, gates_in)
    phases = phase_tables(azimuth_phase, chunks, devices)

    def exchange(blocks):
        return lax.all_to_all(blocks, "lines", split_axis=0, concat_axis=0, tiled=True)

    sent = compress(raw_echo, filter_chunks, 0)
    tables = focus_tables(devices, lines)
    looks = [exchange(focus(exchange(sent), pair_offset, phases, tables, 0))]
    return goldstein(looks, dates, lines // ML_AZ)


def solution(mesh):
    placed = (P("groups", None, "lines", None), P(), P("lines", None), P())
    return jax.shard_map(
        body,
        mesh=mesh,
        in_specs=placed,
        out_specs=P("groups", None, None, "lines"),
        check_vma=False,
    )
```

```python
import math

import jax
import jax.numpy as jnp
import numpy as np
from jax import lax
from jax.experimental import pallas as pl
from jax.experimental.pallas import tpu as pltpu
from jax.sharding import PartitionSpec as P

ML_RG = 4
ML_AZ = 2
PATCH = 32
HALF = PATCH // 2
BOX_FLOOR = 0.25
LEVEL_FLOOR = 1e-06
SUB = 8
LANES = 128
VMEM_BYTES = 20 * 1024 * 1024


def real_block(table):
    return np.block([[table.real, table.imag], [-table.imag, table.real]])


def wave(rows, cols, period, direction):
    product = np.asarray(rows)[:, None] * np.asarray(cols)[None, :] % period
    return np.exp(direction * 2j * math.pi / period * product)


def as_bf16(table):
    return jnp.asarray(np.asarray(table, np.float32), jnp.bfloat16)


def line_order(line_len):
    return np.arange(line_len).reshape(line_len // ML_AZ, ML_AZ).T.reshape(-1)


def small_dft(parts, direction):
    count = len(parts)
    if count == 1:
        return parts
    even = small_dft(parts[0::2], direction)
    odd = small_dft(parts[1::2], direction)
    low, high = [], []
    for k in range(count // 2):
        (er, ei), (vr, vi) = even[k], odd[k]
        if k == 0:
            tr, ti = vr, vi
        elif 4 * k == count:
            if direction < 0:
                tr, ti = vi, -vr
            else:
                tr, ti = -vi, vr
        elif 8 * k == count:
            s = math.sqrt(0.5)
            if direction < 0:
                tr, ti = (vr + vi) * s, (vi - vr) * s
            else:
                tr, ti = (vr - vi) * s, (vi + vr) * s
        elif 8 * k == 3 * count:
            s = math.sqrt(0.5)
            if direction < 0:
                tr, ti = (vi - vr) * s, -(vr + vi) * s
            else:
                tr, ti = -(vr + vi) * s, (vr - vi) * s
        else:
            c = math.cos(2 * math.pi * k / count)
            s = direction * math.sin(2 * math.pi * k / count)
            tr, ti = vr * c - vi * s, vr * s + vi * c
        low.append((er + tr, ei + ti))
        high.append((er - tr, ei - ti))
    return low + high


def compress_kernel(
    shape, raw_hbm, filter_hbm, out_hbm, raw_ref, filter_ref, out_ref, raw_sems,
    filter_sems, out_sems,
):
    chunk, dates, step, targets, tiles, gates, lines = shape
    looks_rows = gates // ML_RG
    gates_in = raw_ref.shape[3]
    copies = [
        pltpu.make_async_copy(
            raw_hbm.at[date, part], raw_ref.at[date, part], raw_sems.at[date, part]
        )
        for date in range(dates)
        for part in (0, 1)
    ]
    out_copies = [
        pltpu.make_async_copy(out_ref.at[:, date], out_hbm.at[:, date], out_sems.at[date])
        for date in range(dates)
    ]
    parts = 2
    held = targets // parts
    filter_copies = [
        pltpu.make_async_copy(
            filter_hbm.at[side, pl.ds(part * held, held), chunk],
            filter_ref.at[side, pl.ds(part * held, held)],
            filter_sems.at[part, side],
        )
        for part in range(parts)
        for side in (0, 1)
    ]
    early = 2 * step
    for copy in filter_copies[:2] + copies[:early] + filter_copies[2:] + copies[early:]:
        copy.start()

    def product(w, x):
        return lax.dot_general(
            w, x, (((1,), (1,)), ((), ())), preferred_element_type=jnp.float32
        )

    run = held * gates
    row = lax.broadcasted_iota(jnp.int32, (run, run), 0)
    col = lax.broadcasted_iota(jnp.int32, (run, run), 1)
    within = row & (gates - 1)
    q, r = within & (looks_rows - 1), within >> (looks_rows.bit_length() - 1)
    order = jnp.where(col == row - within + ML_RG * q + r, 1.0, 0.0).astype(jnp.bfloat16)
    weights = {}

    for first in range(0, dates, step):
        for copy in copies[2 * first : 2 * (first + step)]:
            copy.wait()
        raw = [
            raw_ref[first : first + step, part].reshape(step * lines, gates_in) for part in (0, 1)
        ]
        for group in range(parts):
            if first == 0:
                filter_copies[2 * group].wait()
                filter_copies[2 * group + 1].wait()
                weights[group] = [
                    jnp.dot(
                        order,
                        filter_ref[part, group * held : (group + 1) * held].reshape(run, gates_in),
                        preferred_element_type=jnp.float32,
                    ).astype(jnp.bfloat16)
                    for part in (0, 1)
                ]
            weight = weights[group]
            real = product(weight[0], raw[0]) - product(weight[1], raw[1])
            imag = product(weight[1], raw[0]) + product(weight[0], raw[1])
            for at in range(step):
                lanes = slice(at * lines, (at + 1) * lines)
                for target in range(held):
                    for tile in range(tiles):
                        rows = slice(target * gates + tile * SUB, target * gates + (tile + 1) * SUB)
                        out_ref[group * held + target, first + at, tile] = jnp.concatenate(
                            [real[rows, lanes], imag[rows, lanes]], axis=0
                        ).astype(jnp.bfloat16)
        for date in range(first, first + step):
            out_copies[date].start()
    for copy in out_copies:
        copy.wait()


def compress(raw_echo, filter_chunks, chunk):
    dates, _, lines, gates_in = raw_echo.shape
    _, targets, _, gates, _ = filter_chunks.shape
    tiles = gates // SUB
    step = 2 if dates % 2 == 0 else 1
    shape = (chunk, dates, step, targets, tiles, gates, lines)
    hbm = pl.BlockSpec(memory_space=pltpu.HBM)
    return pl.pallas_call(
        lambda *refs: compress_kernel(shape, *refs),
        out_shape=jax.ShapeDtypeStruct((targets, dates, tiles, 2 * SUB, lines), jnp.bfloat16),
        in_specs=[hbm, hbm],
        out_specs=pl.BlockSpec(memory_space=pl.ANY),
        scratch_shapes=[
            pltpu.VMEM(raw_echo.shape, jnp.bfloat16),
            pltpu.VMEM((2, targets, gates, gates_in), jnp.bfloat16),
            pltpu.VMEM((targets, dates, tiles, 2 * SUB, lines), jnp.bfloat16),
            pltpu.SemaphoreType.DMA((dates, 2)),
            pltpu.SemaphoreType.DMA((2, 2)),
            pltpu.SemaphoreType.DMA((dates,)),
        ],
        compiler_params=pltpu.CompilerParams(vmem_limit_bytes=VMEM_BYTES),
        cost_estimate=pl.CostEstimate(
            flops=8 * dates * lines * targets * gates * gates_in,
            bytes_accessed=4 * (raw_echo.size + targets * gates * gates_in),
            transcendentals=0,
        ),
        name="compress",
    )(*[pltpu.with_memory_space_constraint(x, pltpu.HBM) for x in (raw_echo, filter_chunks)])


def focus_kernel(
    shape, offset_ref, data_ref, cos_ref, sin_ref, turn_ref, table_hbm, out_ref, image_ref, look_ref,
    row_ref, table_ref, table_sem,
):
    chunk, dates, blocks, tiles, gates, lines = shape
    looks_rows = gates // ML_RG
    look_lines = lines // ML_AZ
    count = blocks * SUB
    table_copy = pltpu.make_async_copy(table_hbm, table_ref, table_sem)
    table_copy.start()
    for date in range(dates):
        rows = []
        for tile in range(tiles):
            parts = []
            for a in range(blocks):
                both = data_ref[a, date, tile].astype(jnp.float32)
                parts.append((both[:SUB], both[SUB:]))
            for a, (re, im) in enumerate(small_dft(parts, -1)):
                tr, ti = turn_ref[0, a : a + 1], turn_ref[1, a : a + 1]
                rows.append(jnp.concatenate([re * tr - im * ti, re * ti + im * tr], axis=1))
        row_ref[date] = jnp.concatenate(rows, axis=0).astype(jnp.bfloat16)
    table_copy.wait()
    for date in range(dates):
        spectrum = jnp.dot(row_ref[date], table_ref[0], preferred_element_type=jnp.float32)
        rows = []
        for tile in range(tiles):
            re = spectrum[tile * count : (tile + 1) * count, :lines]
            im = spectrum[tile * count : (tile + 1) * count, lines:]
            pr, pi = cos_ref[chunk, tile], sin_ref[chunk, tile]
            rows.append(jnp.concatenate([re * pr - im * pi, re * pi + im * pr], axis=1))
        rows = jnp.concatenate(rows, axis=0).astype(jnp.bfloat16)
        back = jnp.dot(rows, table_ref[1], preferred_element_type=jnp.float32)
        for tile in range(tiles):
            parts = []
            for a in range(blocks):
                row = tile * count + a * SUB
                re, im = back[row : row + SUB, :lines], back[row : row + SUB, lines:]
                tr, ti = turn_ref[2, a : a + 1], turn_ref[3, a : a + 1]
                parts.append((re * tr - im * ti, re * ti + im * tr))
            for a, (re, im) in enumerate(small_dft(parts, 1)):
                image_ref[date, tile, a, 0] = re
                image_ref[date, tile, a, 1] = im

    lane = lax.broadcasted_iota(jnp.int32, (SUB, lines), 1)
    first = lane < look_lines
    scale = 1.0 / (ML_RG * ML_AZ)
    for date in range(dates):
        partner = lax.rem(date + offset_ref[date], dates)
        for a in range(blocks):
            sums = {}
            for tile in range(tiles):
                cr, ci = image_ref[date, tile, a, 0], image_ref[date, tile, a, 1]
                pr, pi = image_ref[partner, tile, a, 0], image_ref[partner, tile, a, 1]
                re, im = cr * pr + ci * pi, ci * pr - cr * pi
                at = tile * SUB % looks_rows
                if at in sums:
                    re, im = re + sums[at][0], im + sums[at][1]
                sums[at] = (re, im)
            for at, (re, im) in sums.items():
                look = jnp.where(first, re, im) + pltpu.roll(
                    jnp.where(first, im, re), look_lines, 1
                )
                step = SUB
                while step > looks_rows:
                    step //= 2
                    look = look + pltpu.roll(look, step, 0)
                count = min(SUB, looks_rows)
                row = date * looks_rows + at
                look_ref[a, row : row + count, :] = (look * scale)[:count]

    small = lax.broadcasted_iota(jnp.int32, (looks_rows, lines), 1) % look_lines
    from_high, from_low = small < HALF, small >= look_lines - HALF
    zero = jnp.zeros((looks_rows, lines), jnp.float32)

    def rim(a, date):
        rows = slice(date * looks_rows, (date + 1) * looks_rows)
        high = look_ref[a + 1, rows, :] if a + 1 < blocks else zero
        low = look_ref[a - 1, rows, :] if a > 0 else zero
        return jnp.where(from_high, high, low)

    for a in range(blocks):
        for date in range(0, dates, 2):
            own = rim(a, date)
            other = pltpu.roll(rim(a, date + 1), look_lines // 2, 1)
            row = (dates + date // 2) * looks_rows
            look_ref[a, row : row + looks_rows, :] = jnp.where(from_high | from_low, own, other)
    out_ref[...] = look_ref[...].astype(jnp.bfloat16)


def phase_tables(azimuth_phase, chunks, blocks):
    gates, total = azimuth_phase.shape
    looks_rows = gates // chunks // ML_RG
    lines = total // blocks
    tiles = gates // chunks // SUB
    phase = azimuth_phase.reshape(chunks, looks_rows, ML_RG, lines, blocks)
    phase = phase.transpose(0, 2, 1, 4, 3).reshape(chunks, tiles, SUB, blocks, lines)
    phase = phase.transpose(0, 1, 3, 2, 4).reshape(chunks, tiles, blocks * SUB, lines)
    phase = lax.optimization_barrier(phase)
    return jnp.cos(phase), jnp.sin(phase)


def focus_tables(blocks, lines):
    total = blocks * lines
    order = line_order(lines)
    ahead = wave(np.arange(blocks), np.arange(lines), total, -1)
    behind = wave(np.arange(blocks), order, total, 1)
    turn = np.stack([ahead.real, ahead.imag, behind.real, behind.imag]).astype(np.float32)
    fwd = real_block(wave(np.arange(lines), np.arange(lines), lines, -1))
    back = real_block(wave(np.arange(lines), order, lines, 1) / total)
    return jnp.asarray(turn), as_bf16(np.stack([fwd, back]))


def focus(columns, pair_offset, phases, tables, chunk):
    blocks, dates, tiles, _, lines = columns.shape
    gates = tiles * SUB
    looks_rows = gates // ML_RG
    slots = dates + dates // 2
    shape = (chunk, dates, blocks, tiles, gates, lines)
    whole = pl.BlockSpec(memory_space=pltpu.VMEM)
    return pl.pallas_call(
        lambda *refs: focus_kernel(shape, *refs),
        out_shape=jax.ShapeDtypeStruct((blocks, slots * looks_rows, lines), jnp.bfloat16),
        in_specs=[pl.BlockSpec(memory_space=pltpu.SMEM)]
        + [whole] * 4
        + [pl.BlockSpec(memory_space=pltpu.HBM)],
        out_specs=whole,
        scratch_shapes=[
            pltpu.VMEM((dates, tiles, blocks, 2, SUB, lines), jnp.float32),
            pltpu.VMEM((blocks, slots * looks_rows, lines), jnp.float32),
            pltpu.VMEM((dates, tiles * blocks * SUB, 2 * lines), jnp.bfloat16),
            pltpu.VMEM(tables[1].shape, jnp.bfloat16),
            pltpu.SemaphoreType.DMA,
        ],
        compiler_params=pltpu.CompilerParams(vmem_limit_bytes=VMEM_BYTES),
        cost_estimate=pl.CostEstimate(
            flops=16 * dates * gates * blocks * lines * lines,
            bytes_accessed=4 * columns.size,
            transcendentals=0,
        ),
        name="focus",
    )(
        pair_offset,
        columns,
        *phases,
        tables[0],
        pltpu.with_memory_space_constraint(tables[1], pltpu.HBM),
    )


def tri_window(offset):
    inside = (offset >= 0) & (offset < PATCH)
    return np.where(inside, 1.0 - np.abs(offset - (PATCH - 1) / 2.0) / HALF, 0.0)


def patch_tables(cells, starts):
    offset = np.asarray(cells)[:, None] - np.asarray(starts)[None, :]
    inside = ((offset >= 0) & (offset < PATCH)).astype(np.float64)
    angle = 2.0 * math.pi / PATCH * (offset[:, :, None] * np.arange(PATCH) % PATCH)
    ahead = np.exp(-1j * angle) * inside[:, :, None]
    behind = np.exp(1j * angle) * tri_window(offset)[:, :, None] / PATCH
    flat = (len(cells), len(starts) * PATCH)
    return ahead.reshape(flat), behind.reshape(flat).T


def goldstein_tables(dates, gate_order, line_looks):
    per = LANES // PATCH
    starts = np.arange(-HALF, line_looks, HALF)
    cells = np.arange(-HALF, line_looks + HALF)
    ahead, behind = patch_tables(cells, starts)
    main = slice(HALF, HALF + line_looks)
    behind = behind[:, main]
    split = per * PATCH

    def lanes_of(table, shift):
        block = np.zeros((2, line_looks, table.shape[1]), complex)
        block[0], block[1] = table[main], 1j * table[main]
        rim = np.zeros((2, line_looks, table.shape[1]), complex)
        for part, turn in enumerate((1.0, 1j)):
            rim[part, :HALF] = turn * table[HALF + line_looks :]
            rim[part, line_looks - HALF :] = turn * table[:HALF]
        flat = (2 * line_looks, table.shape[1])
        return block.reshape(flat), np.roll(rim.reshape(flat), shift, axis=0)

    def out_parts(table):
        return np.concatenate([table.real, table.imag], axis=1)

    near = [
        out_parts(np.concatenate(lanes_of(ahead[:, :split], parity * (line_looks // 2))))
        for parity in (0, 1)
    ]
    rest = ahead.shape[1] - split
    far_block = np.zeros((dates, 2 * line_looks, dates, rest), complex)
    far_rim = np.zeros((dates // 2, 2 * line_looks, dates, rest), complex)
    for date in range(dates):
        block, rim = lanes_of(ahead[:, split:], date % 2 * (line_looks // 2))
        far_block[date, :, date] = block
        far_rim[date // 2, :, date] = rim
    far = np.concatenate([far_block, far_rim]).reshape(-1, dates * rest)
    gate_starts = np.arange(-HALF, len(gate_order), HALF)
    gate_ahead, gate_behind = patch_tables(np.arange(len(gate_order)), gate_starts)
    ahead_rows = real_block(gate_ahead[gate_order]).T
    behind_rows = real_block(gate_behind).T

    lines_back = []
    for date in range(dates):
        far_back = np.zeros((dates, rest, line_looks), complex)
        far_back[date] = behind[split:]
        lines_back.append(
            np.concatenate(
                [real_block(behind[:split]), real_block(far_back.reshape(-1, line_looks))]
            ).T
        )
    gap = (np.arange(PATCH)[:, None] - np.arange(PATCH)[None, :]) % PATCH
    ring = ((gap == 0) | (gap == 1) | (gap == PATCH - 1)).astype(np.float64)
    box = np.concatenate(
        [np.kron(np.eye(per), ring), np.kron(np.eye(per), np.ones((PATCH, PATCH)))], axis=1
    )
    tables = (np.stack(near), out_parts(far), ahead_rows, box, behind_rows, np.stack(lines_back))
    return [as_bf16(table) for table in tables]


def slot_rows(data_ref, slots, looks_rows):
    blocks = data_ref.shape[0]
    data = data_ref[...].astype(jnp.float32)
    if looks_rows % SUB == 0:
        return [
            data[:, slot * looks_rows : (slot + 1) * looks_rows].reshape(-1, LANES)
            for slot in range(slots)
        ]
    top = lax.broadcasted_iota(jnp.int32, (SUB, LANES), 0) < looks_rows
    held = [[] for _ in range(slots)]
    for block in range(0, blocks, 2):
        for slot in range(0, slots, 2):
            rows = slice(slot * looks_rows, (slot + 2) * looks_rows)
            one, two = data[block, rows], data[block + 1, rows]
            held[slot].append(jnp.where(top, one, pltpu.roll(two, looks_rows, 0)))
            held[slot + 1].append(jnp.where(top, pltpu.roll(one, looks_rows, 0), two))
    return [jnp.concatenate(rows, axis=0) for rows in held]


def goldstein_kernel(shape, *refs):
    dates, chunks, looks_rows, gate_looks, line_looks = shape
    data_refs, refs = refs[:chunks], refs[chunks:]
    near_ref, far_ref, ahead_ref, box_ref, behind_ref, back_ref, out_ref = refs[:7]
    half_ref, spec_ref, weighted_ref = refs[7:]
    slots = dates + dates // 2
    cols = dates + 1
    dot = lambda a, b: jnp.dot(a, b, preferred_element_type=jnp.float32)
    if data_refs[0].shape[0] == slots:
        held = [data_refs[0][slot] for slot in range(slots)]
    else:
        held = zip(*[slot_rows(ref, slots, looks_rows) for ref in data_refs])
        held = [jnp.concatenate(rows, axis=0).astype(jnp.bfloat16) for rows in held]
    for parity in (0, 1):
        rows = jnp.concatenate(
            [
                jnp.concatenate([held[date], held[dates + date // 2]], axis=1)
                for date in range(parity, dates, 2)
            ],
            axis=0,
        )
        both = dot(rows, near_ref[parity]).astype(jnp.bfloat16)
        for index, date in enumerate(range(parity, dates, 2)):
            mine = both[index * gate_looks : (index + 1) * gate_looks]
            half_ref[:gate_looks, date * LANES : (date + 1) * LANES] = mine[:, :LANES]
            half_ref[gate_looks:, date * LANES : (date + 1) * LANES] = mine[:, LANES:]
    both = dot(jnp.concatenate(held, axis=1), far_ref[...]).astype(jnp.bfloat16)
    half_ref[:gate_looks, dates * LANES :] = both[:, :LANES]
    half_ref[gate_looks:, dates * LANES :] = both[:, LANES:]

    spec_ref[...] = dot(ahead_ref[...], half_ref[...])
    bins = ahead_ref.shape[0] // 2
    for col in range(cols):
        lanes = slice(col * LANES, (col + 1) * LANES)
        re, im = spec_ref[:bins, lanes], spec_ref[bins:, lanes]
        power = (re * re + im * im).astype(jnp.bfloat16)
        sums = dot(power, box_ref[...])
        for start in range(0, bins, PATCH):
            rows = slice(start, start + PATCH)
            line = sums[rows, :LANES]
            total = jnp.sum(sums[rows, LANES:], axis=0, keepdims=True)
            smooth = line + pltpu.roll(line, 1, 0) + pltpu.roll(line, PATCH - 1, 0)
            level = total * (1.0 / (PATCH * PATCH)) + LEVEL_FLOOR
            square = smooth * (1.0 / (9.0 * level)) + BOX_FLOOR
            weight = square * lax.rsqrt(square)
            weighted_ref[rows, lanes] = (re[rows] * weight).astype(jnp.bfloat16)
            weighted_ref[start + bins : start + bins + PATCH, lanes] = (im[rows] * weight).astype(
                jnp.bfloat16
            )
    inverse = dot(behind_ref[...], weighted_ref[...]).astype(jnp.bfloat16)
    far = [inverse[:gate_looks, dates * LANES :], inverse[gate_looks:, dates * LANES :]]
    for date in range(dates):
        lanes = slice(date * LANES, (date + 1) * LANES)
        rows = jnp.concatenate([inverse[:gate_looks, lanes], inverse[gate_looks:, lanes]] + far, axis=1)
        result = lax.dot_general(
            back_ref[date], rows, (((1,), (1,)), ((), ())), preferred_element_type=jnp.float32
        )
        out_ref[date, 0] = result[:line_looks]
        out_ref[date, 1] = result[line_looks:]


def goldstein(looks, dates, line_looks):
    chunks = len(looks)
    blocks, rows, _ = looks[0].shape
    slots = dates + dates // 2
    looks_rows = rows // slots
    gate_looks = chunks * blocks * looks_rows
    order = np.arange(gate_looks).reshape(blocks, chunks, looks_rows).swapaxes(0, 1).reshape(-1)
    if looks_rows % SUB and 2 * looks_rows != SUB:
        looks = [
            each.reshape(blocks, slots, looks_rows, LANES)
            .swapaxes(0, 1)
            .reshape(slots, blocks * looks_rows, LANES)
            for each in looks
        ]
        looks = [jnp.concatenate(looks, axis=1)]
    tables = goldstein_tables(dates, order, line_looks)
    bins = tables[2].shape[0] // 2
    width = (dates + 1) * LANES
    shape = (dates, len(looks), looks_rows, gate_looks, line_looks)
    whole = pl.BlockSpec(memory_space=pltpu.VMEM)
    filtered = pl.pallas_call(
        lambda *refs: goldstein_kernel(shape, *refs),
        out_shape=jax.ShapeDtypeStruct((dates, 2, line_looks, gate_looks), jnp.float32),
        in_specs=[whole] * (len(looks) + len(tables)),
        out_specs=whole,
        scratch_shapes=[
            pltpu.VMEM((2 * gate_looks, width), jnp.bfloat16),
            pltpu.VMEM((2 * bins, width), jnp.float32),
            pltpu.VMEM((2 * bins, width), jnp.bfloat16),
        ],
        compiler_params=pltpu.CompilerParams(vmem_limit_bytes=VMEM_BYTES),
        name="goldstein",
    )(*looks, *tables)
    return filtered.swapaxes(2, 3)


def body(raw_echo, range_filter, azimuth_phase, pair_offset):
    dates, _, lines, gates_in = raw_echo.shape
    devices = lax.axis_size("lines")
    gates = azimuth_phase.shape[0]
    chunks = 1
    filter_chunks = range_filter.reshape(2, devices, chunks, gates // chunks, gates_in)
    phases = phase_tables(azimuth_phase, chunks, devices)

    def exchange(blocks):
        return lax.all_to_all(blocks, "lines", split_axis=0, concat_axis=0, tiled=True)

    sent = compress(raw_echo, filter_chunks, 0)
    tables = focus_tables(devices, lines)
    looks = [exchange(focus(exchange(sent), pair_offset, phases, tables, 0))]
    return goldstein(looks, dates, lines // ML_AZ)


def solution(mesh):
    placed = (P("groups", None, "lines", None), P(), P("lines", None), P())
    return jax.shard_map(
        body,
        mesh=mesh,
        in_specs=placed,
        out_specs=P("groups", None, None, "lines"),
        check_vma=False,
    )
```

```python
import math

import jax
import jax.numpy as jnp
import numpy as np
from jax import lax
from jax.experimental import pallas as pl
from jax.experimental.pallas import tpu as pltpu
from jax.sharding import PartitionSpec as P

ML_RG = 4
ML_AZ = 2
PATCH = 32
HALF = PATCH // 2
BOX_FLOOR = 0.25
LEVEL_FLOOR = 1e-06
SUB = 8
LANES = 128
VMEM_BYTES = 20 * 1024 * 1024


def real_block(table):
    return np.block([[table.real, table.imag], [-table.imag, table.real]])


def wave(rows, cols, period, direction):
    product = np.asarray(rows)[:, None] * np.asarray(cols)[None, :] % period
    return np.exp(direction * 2j * math.pi / period * product)


def as_bf16(table):
    return jnp.asarray(np.asarray(table, np.float32), jnp.bfloat16)


def line_order(line_len):
    return np.arange(line_len).reshape(line_len // ML_AZ, ML_AZ).T.reshape(-1)


def small_dft(parts, direction):
    count = len(parts)
    if count == 1:
        return parts
    even = small_dft(parts[0::2], direction)
    odd = small_dft(parts[1::2], direction)
    low, high = [], []
    for k in range(count // 2):
        (er, ei), (vr, vi) = even[k], odd[k]
        if k == 0:
            tr, ti = vr, vi
        elif 4 * k == count:
            if direction < 0:
                tr, ti = vi, -vr
            else:
                tr, ti = -vi, vr
        elif 8 * k == count:
            s = math.sqrt(0.5)
            if direction < 0:
                tr, ti = (vr + vi) * s, (vi - vr) * s
            else:
                tr, ti = (vr - vi) * s, (vi + vr) * s
        elif 8 * k == 3 * count:
            s = math.sqrt(0.5)
            if direction < 0:
                tr, ti = (vi - vr) * s, -(vr + vi) * s
            else:
                tr, ti = -(vr + vi) * s, (vr - vi) * s
        else:
            c = math.cos(2 * math.pi * k / count)
            s = direction * math.sin(2 * math.pi * k / count)
            tr, ti = vr * c - vi * s, vr * s + vi * c
        low.append((er + tr, ei + ti))
        high.append((er - tr, ei - ti))
    return low + high


def compress_kernel(
    shape, raw_hbm, filter_hbm, out_hbm, raw_ref, filter_ref, wide_ref, out_ref, raw_sems,
    filter_sems, out_sems,
):
    chunk, dates, step, targets, tiles, gates, lines = shape
    looks_rows = gates // ML_RG
    gates_in = raw_ref.shape[3]
    copies = [
        pltpu.make_async_copy(
            raw_hbm.at[date, part], raw_ref.at[date, part], raw_sems.at[date, part]
        )
        for date in range(dates)
        for part in (0, 1)
    ]
    out_copies = [
        pltpu.make_async_copy(out_ref.at[:, date], out_hbm.at[:, date], out_sems.at[date])
        for date in range(dates)
    ]
    parts = 2
    held = targets // parts
    filter_copies = [
        pltpu.make_async_copy(
            filter_hbm.at[side, pl.ds(part * held, held), chunk],
            filter_ref.at[part, side],
            filter_sems.at[part, side],
        )
        for part in range(parts)
        for side in (0, 1)
    ]
    early = 2 * step
    for copy in filter_copies[:2] + copies[:early] + filter_copies[2:] + copies[early:]:
        copy.start()

    def product(w, x):
        return lax.dot_general(
            w, x, (((1,), (1,)), ((), ())), preferred_element_type=jnp.float32
        )

    run = held * gates
    for first in range(0, dates, step):
        for copy in copies[2 * first : 2 * (first + step)]:
            copy.wait()
        raw = [
            raw_ref[first : first + step, part].reshape(step * lines, gates_in) for part in (0, 1)
        ]
        for group in range(parts):
            if first == 0:
                filter_copies[2 * group].wait()
                filter_copies[2 * group + 1].wait()
            both = filter_ref[group].reshape(2 * run, gates_in)
            by_real, by_imag = product(both, raw[0]), product(both, raw[1])
            real = by_real[:run] - by_imag[run:]
            imag = by_real[run:] + by_imag[:run]
            rows = slice(group * run, (group + 1) * run)
            for at in range(step):
                wide_ref[first + at, 0, rows] = real[:, at * lines : (at + 1) * lines]
                wide_ref[first + at, 1, rows] = imag[:, at * lines : (at + 1) * lines]
        for date in range(first, first + step):
            for target in range(targets):
                for tile in range(tiles):
                    rows = []
                    for part in (0, 1):
                        begin, count = tile * SUB, min(looks_rows, SUB)
                        for at in range(begin, begin + SUB, count):
                            gate = target * gates + at // looks_rows + ML_RG * (at % looks_rows)
                            rows.append(wide_ref[date, part, pl.ds(gate, count, stride=ML_RG), :])
                    out_ref[target, date, tile] = jnp.concatenate(rows, axis=0).astype(
                        jnp.bfloat16
                    )
            out_copies[date].start()
    for copy in out_copies:
        copy.wait()


def compress(raw_echo, filter_chunks, chunk):
    dates, _, lines, gates_in = raw_echo.shape
    _, targets, _, gates, _ = filter_chunks.shape
    tiles = gates // SUB
    step = 2 if dates % 2 == 0 else 1
    shape = (chunk, dates, step, targets, tiles, gates, lines)
    hbm = pl.BlockSpec(memory_space=pltpu.HBM)
    return pl.pallas_call(
        lambda *refs: compress_kernel(shape, *refs),
        out_shape=jax.ShapeDtypeStruct((targets, dates, tiles, 2 * SUB, lines), jnp.bfloat16),
        in_specs=[hbm, hbm],
        out_specs=pl.BlockSpec(memory_space=pl.ANY),
        scratch_shapes=[
            pltpu.VMEM(raw_echo.shape, jnp.bfloat16),
            pltpu.VMEM((2, 2, targets // 2, gates, gates_in), jnp.bfloat16),
            pltpu.VMEM((dates, 2, targets * gates, lines), jnp.float32),
            pltpu.VMEM((targets, dates, tiles, 2 * SUB, lines), jnp.bfloat16),
            pltpu.SemaphoreType.DMA((dates, 2)),
            pltpu.SemaphoreType.DMA((2, 2)),
            pltpu.SemaphoreType.DMA((dates,)),
        ],
        compiler_params=pltpu.CompilerParams(vmem_limit_bytes=VMEM_BYTES),
        cost_estimate=pl.CostEstimate(
            flops=8 * dates * lines * targets * gates * gates_in,
            bytes_accessed=4 * (raw_echo.size + targets * gates * gates_in),
            transcendentals=0,
        ),
        name="compress",
    )(*[pltpu.with_memory_space_constraint(x, pltpu.HBM) for x in (raw_echo, filter_chunks)])


def focus_kernel(
    shape, offset_ref, data_ref, cos_ref, sin_ref, turn_ref, table_hbm, out_ref, image_ref, look_ref,
    row_ref, table_ref, table_sem,
):
    chunk, dates, blocks, tiles, gates, lines = shape
    looks_rows = gates // ML_RG
    look_lines = lines // ML_AZ
    count = blocks * SUB
    table_copy = pltpu.make_async_copy(table_hbm, table_ref, table_sem)
    table_copy.start()
    for date in range(dates):
        rows = []
        for tile in range(tiles):
            parts = []
            for a in range(blocks):
                both = data_ref[a, date, tile].astype(jnp.float32)
                parts.append((both[:SUB], both[SUB:]))
            for a, (re, im) in enumerate(small_dft(parts, -1)):
                tr, ti = turn_ref[0, a : a + 1], turn_ref[1, a : a + 1]
                rows.append(jnp.concatenate([re * tr - im * ti, re * ti + im * tr], axis=1))
        row_ref[date] = jnp.concatenate(rows, axis=0).astype(jnp.bfloat16)
    table_copy.wait()
    for date in range(dates):
        spectrum = jnp.dot(row_ref[date], table_ref[0], preferred_element_type=jnp.float32)
        rows = []
        for tile in range(tiles):
            re = spectrum[tile * count : (tile + 1) * count, :lines]
            im = spectrum[tile * count : (tile + 1) * count, lines:]
            pr, pi = cos_ref[chunk, tile], sin_ref[chunk, tile]
            rows.append(jnp.concatenate([re * pr - im * pi, re * pi + im * pr], axis=1))
        rows = jnp.concatenate(rows, axis=0).astype(jnp.bfloat16)
        back = jnp.dot(rows, table_ref[1], preferred_element_type=jnp.float32)
        for tile in range(tiles):
            parts = []
            for a in range(blocks):
                row = tile * count + a * SUB
                re, im = back[row : row + SUB, :lines], back[row : row + SUB, lines:]
                tr, ti = turn_ref[2, a : a + 1], turn_ref[3, a : a + 1]
                parts.append((re * tr - im * ti, re * ti + im * tr))
            for a, (re, im) in enumerate(small_dft(parts, 1)):
                image_ref[date, tile, a, 0] = re
                image_ref[date, tile, a, 1] = im

    lane = lax.broadcasted_iota(jnp.int32, (SUB, lines), 1)
    first = lane < look_lines
    scale = 1.0 / (ML_RG * ML_AZ)
    for date in range(dates):
        partner = lax.rem(date + offset_ref[date], dates)
        for a in range(blocks):
            sums = {}
            for tile in range(tiles):
                cr, ci = image_ref[date, tile, a, 0], image_ref[date, tile, a, 1]
                pr, pi = image_ref[partner, tile, a, 0], image_ref[partner, tile, a, 1]
                re, im = cr * pr + ci * pi, ci * pr - cr * pi
                at = tile * SUB % looks_rows
                if at in sums:
                    re, im = re + sums[at][0], im + sums[at][1]
                sums[at] = (re, im)
            for at, (re, im) in sums.items():
                look = jnp.where(first, re, im) + pltpu.roll(
                    jnp.where(first, im, re), look_lines, 1
                )
                step = SUB
                while step > looks_rows:
                    step //= 2
                    look = look + pltpu.roll(look, step, 0)
                count = min(SUB, looks_rows)
                row = date * looks_rows + at
                look_ref[a, row : row + count, :] = (look * scale)[:count]

    small = lax.broadcasted_iota(jnp.int32, (looks_rows, lines), 1) % look_lines
    from_high, from_low = small < HALF, small >= look_lines - HALF
    zero = jnp.zeros((looks_rows, lines), jnp.float32)

    def rim(a, date):
        rows = slice(date * looks_rows, (date + 1) * looks_rows)
        high = look_ref[a + 1, rows, :] if a + 1 < blocks else zero
        low = look_ref[a - 1, rows, :] if a > 0 else zero
        return jnp.where(from_high, high, low)

    for a in range(blocks):
        for date in range(0, dates, 2):
            own = rim(a, date)
            other = pltpu.roll(rim(a, date + 1), look_lines // 2, 1)
            row = (dates + date // 2) * looks_rows
            look_ref[a, row : row + looks_rows, :] = jnp.where(from_high | from_low, own, other)
    out_ref[...] = look_ref[...].astype(jnp.bfloat16)


def phase_tables(azimuth_phase, chunks, blocks):
    gates, total = azimuth_phase.shape
    looks_rows = gates // chunks // ML_RG
    lines = total // blocks
    tiles = gates // chunks // SUB
    phase = azimuth_phase.reshape(chunks, looks_rows, ML_RG, lines, blocks)
    phase = phase.transpose(0, 2, 1, 4, 3).reshape(chunks, tiles, SUB, blocks, lines)
    phase = phase.transpose(0, 1, 3, 2, 4).reshape(chunks, tiles, blocks * SUB, lines)
    phase = lax.optimization_barrier(phase)
    return jnp.cos(phase), jnp.sin(phase)


def focus_tables(blocks, lines):
    total = blocks * lines
    order = line_order(lines)
    ahead = wave(np.arange(blocks), np.arange(lines), total, -1)
    behind = wave(np.arange(blocks), order, total, 1)
    turn = np.stack([ahead.real, ahead.imag, behind.real, behind.imag]).astype(np.float32)
    fwd = real_block(wave(np.arange(lines), np.arange(lines), lines, -1))
    back = real_block(wave(np.arange(lines), order, lines, 1) / total)
    return jnp.asarray(turn), as_bf16(np.stack([fwd, back]))


def focus(columns, pair_offset, phases, tables, chunk):
    blocks, dates, tiles, _, lines = columns.shape
    gates = tiles * SUB
    looks_rows = gates // ML_RG
    slots = dates + dates // 2
    shape = (chunk, dates, blocks, tiles, gates, lines)
    whole = pl.BlockSpec(memory_space=pltpu.VMEM)
    return pl.pallas_call(
        lambda *refs: focus_kernel(shape, *refs),
        out_shape=jax.ShapeDtypeStruct((blocks, slots * looks_rows, lines), jnp.bfloat16),
        in_specs=[pl.BlockSpec(memory_space=pltpu.SMEM)]
        + [whole] * 4
        + [pl.BlockSpec(memory_space=pltpu.HBM)],
        out_specs=whole,
        scratch_shapes=[
            pltpu.VMEM((dates, tiles, blocks, 2, SUB, lines), jnp.float32),
            pltpu.VMEM((blocks, slots * looks_rows, lines), jnp.float32),
            pltpu.VMEM((dates, tiles * blocks * SUB, 2 * lines), jnp.bfloat16),
            pltpu.VMEM(tables[1].shape, jnp.bfloat16),
            pltpu.SemaphoreType.DMA,
        ],
        compiler_params=pltpu.CompilerParams(vmem_limit_bytes=VMEM_BYTES),
        cost_estimate=pl.CostEstimate(
            flops=16 * dates * gates * blocks * lines * lines,
            bytes_accessed=4 * columns.size,
            transcendentals=0,
        ),
        name="focus",
    )(
        pair_offset,
        columns,
        *phases,
        tables[0],
        pltpu.with_memory_space_constraint(tables[1], pltpu.HBM),
    )


def tri_window(offset):
    inside = (offset >= 0) & (offset < PATCH)
    return np.where(inside, 1.0 - np.abs(offset - (PATCH - 1) / 2.0) / HALF, 0.0)


def patch_tables(cells, starts):
    offset = np.asarray(cells)[:, None] - np.asarray(starts)[None, :]
    inside = ((offset >= 0) & (offset < PATCH)).astype(np.float64)
    angle = 2.0 * math.pi / PATCH * (offset[:, :, None] * np.arange(PATCH) % PATCH)
    ahead = np.exp(-1j * angle) * inside[:, :, None]
    behind = np.exp(1j * angle) * tri_window(offset)[:, :, None] / PATCH
    flat = (len(cells), len(starts) * PATCH)
    return ahead.reshape(flat), behind.reshape(flat).T


def goldstein_tables(dates, gate_order, line_looks):
    per = LANES // PATCH
    starts = np.arange(-HALF, line_looks, HALF)
    cells = np.arange(-HALF, line_looks + HALF)
    ahead, behind = patch_tables(cells, starts)
    main = slice(HALF, HALF + line_looks)
    behind = behind[:, main]
    split = per * PATCH

    def lanes_of(table, shift):
        block = np.zeros((2, line_looks, table.shape[1]), complex)
        block[0], block[1] = table[main], 1j * table[main]
        rim = np.zeros((2, line_looks, table.shape[1]), complex)
        for part, turn in enumerate((1.0, 1j)):
            rim[part, :HALF] = turn * table[HALF + line_looks :]
            rim[part, line_looks - HALF :] = turn * table[:HALF]
        flat = (2 * line_looks, table.shape[1])
        return block.reshape(flat), np.roll(rim.reshape(flat), shift, axis=0)

    def out_parts(table):
        return np.concatenate([table.real, table.imag], axis=1)

    near = [
        out_parts(np.concatenate(lanes_of(ahead[:, :split], parity * (line_looks // 2))))
        for parity in (0, 1)
    ]
    rest = ahead.shape[1] - split
    far_block = np.zeros((dates, 2 * line_looks, dates, rest), complex)
    far_rim = np.zeros((dates // 2, 2 * line_looks, dates, rest), complex)
    for date in range(dates):
        block, rim = lanes_of(ahead[:, split:], date % 2 * (line_looks // 2))
        far_block[date, :, date] = block
        far_rim[date // 2, :, date] = rim
    far = np.concatenate([far_block, far_rim]).reshape(-1, dates * rest)
    gate_starts = np.arange(-HALF, len(gate_order), HALF)
    gate_ahead, gate_behind = patch_tables(np.arange(len(gate_order)), gate_starts)
    ahead_rows = real_block(gate_ahead[gate_order]).T
    behind_rows = real_block(gate_behind).T

    lines_back = []
    for date in range(dates):
        far_back = np.zeros((dates, rest, line_looks), complex)
        far_back[date] = behind[split:]
        lines_back.append(
            np.concatenate(
                [real_block(behind[:split]), real_block(far_back.reshape(-1, line_looks))]
            ).T
        )
    gap = (np.arange(PATCH)[:, None] - np.arange(PATCH)[None, :]) % PATCH
    ring = ((gap == 0) | (gap == 1) | (gap == PATCH - 1)).astype(np.float64)
    box = np.concatenate(
        [np.kron(np.eye(per), ring), np.kron(np.eye(per), np.ones((PATCH, PATCH)))], axis=1
    )
    tables = (np.stack(near), out_parts(far), ahead_rows, box, behind_rows, np.stack(lines_back))
    return [as_bf16(table) for table in tables]


def slot_rows(data_ref, slots, looks_rows):
    blocks = data_ref.shape[0]
    data = data_ref[...].astype(jnp.float32)
    if looks_rows % SUB == 0:
        return [
            data[:, slot * looks_rows : (slot + 1) * looks_rows].reshape(-1, LANES)
            for slot in range(slots)
        ]
    top = lax.broadcasted_iota(jnp.int32, (SUB, LANES), 0) < looks_rows
    held = [[] for _ in range(slots)]
    for block in range(0, blocks, 2):
        for slot in range(0, slots, 2):
            rows = slice(slot * looks_rows, (slot + 2) * looks_rows)
            one, two = data[block, rows], data[block + 1, rows]
            held[slot].append(jnp.where(top, one, pltpu.roll(two, looks_rows, 0)))
            held[slot + 1].append(jnp.where(top, pltpu.roll(one, looks_rows, 0), two))
    return [jnp.concatenate(rows, axis=0) for rows in held]


def goldstein_kernel(shape, *refs):
    dates, chunks, looks_rows, gate_looks, line_looks = shape
    data_refs, refs = refs[:chunks], refs[chunks:]
    near_ref, far_ref, ahead_ref, box_ref, behind_ref, back_ref, out_ref = refs[:7]
    half_ref, spec_ref, weighted_ref = refs[7:]
    slots = dates + dates // 2
    cols = dates + 1
    dot = lambda a, b: jnp.dot(a, b, preferred_element_type=jnp.float32)
    if data_refs[0].shape[0] == slots:
        held = [data_refs[0][slot] for slot in range(slots)]
    else:
        held = zip(*[slot_rows(ref, slots, looks_rows) for ref in data_refs])
        held = [jnp.concatenate(rows, axis=0).astype(jnp.bfloat16) for rows in held]
    for parity in (0, 1):
        rows = jnp.concatenate(
            [
                jnp.concatenate([held[date], held[dates + date // 2]], axis=1)
                for date in range(parity, dates, 2)
            ],
            axis=0,
        )
        both = dot(rows, near_ref[parity]).astype(jnp.bfloat16)
        for index, date in enumerate(range(parity, dates, 2)):
            mine = both[index * gate_looks : (index + 1) * gate_looks]
            half_ref[:gate_looks, date * LANES : (date + 1) * LANES] = mine[:, :LANES]
            half_ref[gate_looks:, date * LANES : (date + 1) * LANES] = mine[:, LANES:]
    both = dot(jnp.concatenate(held, axis=1), far_ref[...]).astype(jnp.bfloat16)
    half_ref[:gate_looks, dates * LANES :] = both[:, :LANES]
    half_ref[gate_looks:, dates * LANES :] = both[:, LANES:]

    spec_ref[...] = dot(ahead_ref[...], half_ref[...])
    bins = ahead_ref.shape[0] // 2
    for col in range(cols):
        lanes = slice(col * LANES, (col + 1) * LANES)
        re, im = spec_ref[:bins, lanes], spec_ref[bins:, lanes]
        power = (re * re + im * im).astype(jnp.bfloat16)
        sums = dot(power, box_ref[...])
        for start in range(0, bins, PATCH):
            rows = slice(start, start + PATCH)
            line = sums[rows, :LANES]
            total = jnp.sum(sums[rows, LANES:], axis=0, keepdims=True)
            smooth = line + pltpu.roll(line, 1, 0) + pltpu.roll(line, PATCH - 1, 0)
            level = total * (1.0 / (PATCH * PATCH)) + LEVEL_FLOOR
            square = smooth * (1.0 / (9.0 * level)) + BOX_FLOOR
            weight = square * lax.rsqrt(square)
            weighted_ref[rows, lanes] = (re[rows] * weight).astype(jnp.bfloat16)
            weighted_ref[start + bins : start + bins + PATCH, lanes] = (im[rows] * weight).astype(
                jnp.bfloat16
            )
    inverse = dot(behind_ref[...], weighted_ref[...]).astype(jnp.bfloat16)
    far = [inverse[:gate_looks, dates * LANES :], inverse[gate_looks:, dates * LANES :]]
    for date in range(dates):
        lanes = slice(date * LANES, (date + 1) * LANES)
        rows = jnp.concatenate([inverse[:gate_looks, lanes], inverse[gate_looks:, lanes]] + far, axis=1)
        result = lax.dot_general(
            back_ref[date], rows, (((1,), (1,)), ((), ())), preferred_element_type=jnp.float32
        )
        out_ref[date, 0] = result[:line_looks]
        out_ref[date, 1] = result[line_looks:]


def goldstein(looks, dates, line_looks):
    chunks = len(looks)
    blocks, rows, _ = looks[0].shape
    slots = dates + dates // 2
    looks_rows = rows // slots
    gate_looks = chunks * blocks * looks_rows
    order = np.arange(gate_looks).reshape(blocks, chunks, looks_rows).swapaxes(0, 1).reshape(-1)
    if looks_rows % SUB and 2 * looks_rows != SUB:
        looks = [
            each.reshape(blocks, slots, looks_rows, LANES)
            .swapaxes(0, 1)
            .reshape(slots, blocks * looks_rows, LANES)
            for each in looks
        ]
        looks = [jnp.concatenate(looks, axis=1)]
    tables = goldstein_tables(dates, order, line_looks)
    bins = tables[2].shape[0] // 2
    width = (dates + 1) * LANES
    shape = (dates, len(looks), looks_rows, gate_looks, line_looks)
    whole = pl.BlockSpec(memory_space=pltpu.VMEM)
    filtered = pl.pallas_call(
        lambda *refs: goldstein_kernel(shape, *refs),
        out_shape=jax.ShapeDtypeStruct((dates, 2, line_looks, gate_looks), jnp.float32),
        in_specs=[whole] * (len(looks) + len(tables)),
        out_specs=whole,
        scratch_shapes=[
            pltpu.VMEM((2 * gate_looks, width), jnp.bfloat16),
            pltpu.VMEM((2 * bins, width), jnp.float32),
            pltpu.VMEM((2 * bins, width), jnp.bfloat16),
        ],
        compiler_params=pltpu.CompilerParams(vmem_limit_bytes=VMEM_BYTES),
        name="goldstein",
    )(*looks, *tables)
    return filtered.swapaxes(2, 3)


def body(raw_echo, range_filter, azimuth_phase, pair_offset):
    dates, _, lines, gates_in = raw_echo.shape
    devices = lax.axis_size("lines")
    gates = azimuth_phase.shape[0]
    chunks = 1
    filter_chunks = range_filter.reshape(2, devices, chunks, gates // chunks, gates_in)
    phases = phase_tables(azimuth_phase, chunks, devices)

    def exchange(blocks):
        return lax.all_to_all(blocks, "lines", split_axis=0, concat_axis=0, tiled=True)

    sent = compress(raw_echo, filter_chunks, 0)
    tables = focus_tables(devices, lines)
    looks = [exchange(focus(exchange(sent), pair_offset, phases, tables, 0))]
    return goldstein(looks, dates, lines // ML_AZ)


def solution(mesh):
    placed = (P("groups", None, "lines", None), P(), P("lines", None), P())
    return jax.shard_map(
        body,
        mesh=mesh,
        in_specs=placed,
        out_specs=P("groups", None, None, "lines"),
        check_vma=False,
    )
```

```python
import math

import jax
import jax.numpy as jnp
import numpy as np
from jax import lax
from jax.experimental import pallas as pl
from jax.experimental.pallas import tpu as pltpu
from jax.sharding import PartitionSpec as P

ML_RG = 4
ML_AZ = 2
PATCH = 32
HALF = PATCH // 2
BOX_FLOOR = 0.25
LEVEL_FLOOR = 1e-06
SUB = 8
LANES = 128
VMEM_BYTES = 20 * 1024 * 1024


def real_block(table):
    return np.block([[table.real, table.imag], [-table.imag, table.real]])


def wave(rows, cols, period, direction):
    product = np.asarray(rows)[:, None] * np.asarray(cols)[None, :] % period
    return np.exp(direction * 2j * math.pi / period * product)


def as_bf16(table):
    return jnp.asarray(np.asarray(table, np.float32), jnp.bfloat16)


def line_order(line_len):
    return np.arange(line_len).reshape(line_len // ML_AZ, ML_AZ).T.reshape(-1)


def small_dft(parts, direction):
    count = len(parts)
    if count == 1:
        return parts
    even = small_dft(parts[0::2], direction)
    odd = small_dft(parts[1::2], direction)
    low, high = [], []
    for k in range(count // 2):
        (er, ei), (vr, vi) = even[k], odd[k]
        if k == 0:
            tr, ti = vr, vi
        elif 4 * k == count:
            if direction < 0:
                tr, ti = vi, -vr
            else:
                tr, ti = -vi, vr
        elif 8 * k == count:
            s = math.sqrt(0.5)
            if direction < 0:
                tr, ti = (vr + vi) * s, (vi - vr) * s
            else:
                tr, ti = (vr - vi) * s, (vi + vr) * s
        elif 8 * k == 3 * count:
            s = math.sqrt(0.5)
            if direction < 0:
                tr, ti = (vi - vr) * s, -(vr + vi) * s
            else:
                tr, ti = -(vr + vi) * s, (vr - vi) * s
        else:
            c = math.cos(2 * math.pi * k / count)
            s = direction * math.sin(2 * math.pi * k / count)
            tr, ti = vr * c - vi * s, vr * s + vi * c
        low.append((er + tr, ei + ti))
        high.append((er - tr, ei - ti))
    return low + high


def compress_kernel(
    shape, raw_hbm, filter_hbm, out_hbm, raw_ref, filter_ref, wide_ref, out_ref, raw_sems,
    filter_sems, out_sems,
):
    chunk, dates, step, targets, tiles, gates, lines = shape
    looks_rows = gates // ML_RG
    gates_in = raw_ref.shape[3]
    copies = [
        pltpu.make_async_copy(
            raw_hbm.at[pl.ds(first, step)], raw_ref.at[pl.ds(first, step)], raw_sems.at[first // step]
        )
        for first in range(0, dates, step)
    ]
    out_copies = [
        pltpu.make_async_copy(out_ref.at[:, date], out_hbm.at[:, date], out_sems.at[date])
        for date in range(dates)
    ]
    parts = 2
    held = targets // parts
    filter_copies = [
        pltpu.make_async_copy(
            filter_hbm.at[:, pl.ds(part * held, held), chunk],
            filter_ref.at[:, pl.ds(part * held, held)],
            filter_sems.at[part],
        )
        for part in range(parts)
    ]
    for copy in [filter_copies[0], *copies[:1], *filter_copies[1:], *copies[1:]]:
        copy.start()

    def product(w, x):
        return lax.dot_general(
            w, x, (((1,), (1,)), ((), ())), preferred_element_type=jnp.float32
        )

    for first in range(0, dates, step):
        copies[first // step].wait()
        raw = [
            raw_ref[first : first + step, part].reshape(step * lines, gates_in) for part in (0, 1)
        ]
        for group in range(parts):
            if first == 0:
                filter_copies[group].wait()
            weight = [
                filter_ref[part, group * held : (group + 1) * held].reshape(held * gates, gates_in)
                for part in (0, 1)
            ]
            real = product(weight[0], raw[0]) - product(weight[1], raw[1])
            imag = product(weight[1], raw[0]) + product(weight[0], raw[1])
            rows = slice(group * held * gates, (group + 1) * held * gates)
            for at in range(step):
                wide_ref[first + at, 0, rows] = real[:, at * lines : (at + 1) * lines]
                wide_ref[first + at, 1, rows] = imag[:, at * lines : (at + 1) * lines]
        for date in range(first, first + step):
            for target in range(targets):
                for tile in range(tiles):
                    rows = []
                    for part in (0, 1):
                        begin, count = tile * SUB, min(looks_rows, SUB)
                        for at in range(begin, begin + SUB, count):
                            gate = target * gates + at // looks_rows + ML_RG * (at % looks_rows)
                            rows.append(wide_ref[date, part, pl.ds(gate, count, stride=ML_RG), :])
                    out_ref[target, date, tile] = jnp.concatenate(rows, axis=0).astype(
                        jnp.bfloat16
                    )
            out_copies[date].start()
    for copy in out_copies:
        copy.wait()


def compress(raw_echo, filter_chunks, chunk):
    dates, _, lines, gates_in = raw_echo.shape
    _, targets, _, gates, _ = filter_chunks.shape
    tiles = gates // SUB
    step = 2 if dates % 2 == 0 else 1
    shape = (chunk, dates, step, targets, tiles, gates, lines)
    hbm = pl.BlockSpec(memory_space=pltpu.HBM)
    return pl.pallas_call(
        lambda *refs: compress_kernel(shape, *refs),
        out_shape=jax.ShapeDtypeStruct((targets, dates, tiles, 2 * SUB, lines), jnp.bfloat16),
        in_specs=[hbm, hbm],
        out_specs=pl.BlockSpec(memory_space=pl.ANY),
        scratch_shapes=[
            pltpu.VMEM(raw_echo.shape, jnp.bfloat16),
            pltpu.VMEM((2, targets, gates, gates_in), jnp.bfloat16),
            pltpu.VMEM((dates, 2, targets * gates, lines), jnp.float32),
            pltpu.VMEM((targets, dates, tiles, 2 * SUB, lines), jnp.bfloat16),
            pltpu.SemaphoreType.DMA((dates // step,)),
            pltpu.SemaphoreType.DMA((2,)),
            pltpu.SemaphoreType.DMA((dates,)),
        ],
        compiler_params=pltpu.CompilerParams(vmem_limit_bytes=VMEM_BYTES),
        cost_estimate=pl.CostEstimate(
            flops=8 * dates * lines * targets * gates * gates_in,
            bytes_accessed=4 * (raw_echo.size + targets * gates * gates_in),
            transcendentals=0,
        ),
        name="compress",
    )(*[pltpu.with_memory_space_constraint(x, pltpu.HBM) for x in (raw_echo, filter_chunks)])


def focus_kernel(
    shape, offset_ref, data_ref, cos_ref, sin_ref, turn_ref, table_hbm, out_ref, image_ref, look_ref,
    row_ref, table_ref, table_sem,
):
    chunk, dates, blocks, tiles, gates, lines = shape
    looks_rows = gates // ML_RG
    look_lines = lines // ML_AZ
    count = blocks * SUB
    table_copy = pltpu.make_async_copy(table_hbm, table_ref, table_sem)
    table_copy.start()
    for date in range(dates):
        rows = []
        for tile in range(tiles):
            parts = []
            for a in range(blocks):
                both = data_ref[a, date, tile].astype(jnp.float32)
                parts.append((both[:SUB], both[SUB:]))
            for a, (re, im) in enumerate(small_dft(parts, -1)):
                tr, ti = turn_ref[0, a : a + 1], turn_ref[1, a : a + 1]
                rows.append(jnp.concatenate([re * tr - im * ti, re * ti + im * tr], axis=1))
        row_ref[date] = jnp.concatenate(rows, axis=0).astype(jnp.bfloat16)
    table_copy.wait()
    for date in range(dates):
        spectrum = jnp.dot(row_ref[date], table_ref[0], preferred_element_type=jnp.float32)
        rows = []
        for tile in range(tiles):
            re = spectrum[tile * count : (tile + 1) * count, :lines]
            im = spectrum[tile * count : (tile + 1) * count, lines:]
            pr, pi = cos_ref[chunk, tile], sin_ref[chunk, tile]
            rows.append(jnp.concatenate([re * pr - im * pi, re * pi + im * pr], axis=1))
        rows = jnp.concatenate(rows, axis=0).astype(jnp.bfloat16)
        back = jnp.dot(rows, table_ref[1], preferred_element_type=jnp.float32)
        for tile in range(tiles):
            parts = []
            for a in range(blocks):
                row = tile * count + a * SUB
                re, im = back[row : row + SUB, :lines], back[row : row + SUB, lines:]
                tr, ti = turn_ref[2, a : a + 1], turn_ref[3, a : a + 1]
                parts.append((re * tr - im * ti, re * ti + im * tr))
            for a, (re, im) in enumerate(small_dft(parts, 1)):
                image_ref[date, tile, a, 0] = re
                image_ref[date, tile, a, 1] = im

    lane = lax.broadcasted_iota(jnp.int32, (SUB, lines), 1)
    first = lane < look_lines
    scale = 1.0 / (ML_RG * ML_AZ)
    for date in range(dates):
        partner = lax.rem(date + offset_ref[date], dates)
        for a in range(blocks):
            sums = {}
            for tile in range(tiles):
                cr, ci = image_ref[date, tile, a, 0], image_ref[date, tile, a, 1]
                pr, pi = image_ref[partner, tile, a, 0], image_ref[partner, tile, a, 1]
                re, im = cr * pr + ci * pi, ci * pr - cr * pi
                at = tile * SUB % looks_rows
                if at in sums:
                    re, im = re + sums[at][0], im + sums[at][1]
                sums[at] = (re, im)
            for at, (re, im) in sums.items():
                look = jnp.where(first, re, im) + pltpu.roll(
                    jnp.where(first, im, re), look_lines, 1
                )
                step = SUB
                while step > looks_rows:
                    step //= 2
                    look = look + pltpu.roll(look, step, 0)
                count = min(SUB, looks_rows)
                row = date * looks_rows + at
                look_ref[a, row : row + count, :] = (look * scale)[:count]

    small = lax.broadcasted_iota(jnp.int32, (looks_rows, lines), 1) % look_lines
    from_high, from_low = small < HALF, small >= look_lines - HALF
    zero = jnp.zeros((looks_rows, lines), jnp.float32)

    def rim(a, date):
        rows = slice(date * looks_rows, (date + 1) * looks_rows)
        high = look_ref[a + 1, rows, :] if a + 1 < blocks else zero
        low = look_ref[a - 1, rows, :] if a > 0 else zero
        return jnp.where(from_high, high, low)

    for a in range(blocks):
        for date in range(0, dates, 2):
            own = rim(a, date)
            other = pltpu.roll(rim(a, date + 1), look_lines // 2, 1)
            row = (dates + date // 2) * looks_rows
            look_ref[a, row : row + looks_rows, :] = jnp.where(from_high | from_low, own, other)
    out_ref[...] = look_ref[...].astype(jnp.bfloat16)


def phase_tables(azimuth_phase, chunks, blocks):
    gates, total = azimuth_phase.shape
    looks_rows = gates // chunks // ML_RG
    lines = total // blocks
    tiles = gates // chunks // SUB
    phase = azimuth_phase.reshape(chunks, looks_rows, ML_RG, lines, blocks)
    phase = phase.transpose(0, 2, 1, 4, 3).reshape(chunks, tiles, SUB, blocks, lines)
    phase = phase.transpose(0, 1, 3, 2, 4).reshape(chunks, tiles, blocks * SUB, lines)
    phase = lax.optimization_barrier(phase)
    return jnp.cos(phase), jnp.sin(phase)


def focus_tables(blocks, lines):
    total = blocks * lines
    order = line_order(lines)
    ahead = wave(np.arange(blocks), np.arange(lines), total, -1)
    behind = wave(np.arange(blocks), order, total, 1)
    turn = np.stack([ahead.real, ahead.imag, behind.real, behind.imag]).astype(np.float32)
    fwd = real_block(wave(np.arange(lines), np.arange(lines), lines, -1))
    back = real_block(wave(np.arange(lines), order, lines, 1) / total)
    return jnp.asarray(turn), as_bf16(np.stack([fwd, back]))


def focus(columns, pair_offset, phases, tables, chunk):
    blocks, dates, tiles, _, lines = columns.shape
    gates = tiles * SUB
    looks_rows = gates // ML_RG
    slots = dates + dates // 2
    shape = (chunk, dates, blocks, tiles, gates, lines)
    whole = pl.BlockSpec(memory_space=pltpu.VMEM)
    return pl.pallas_call(
        lambda *refs: focus_kernel(shape, *refs),
        out_shape=jax.ShapeDtypeStruct((blocks, slots * looks_rows, lines), jnp.bfloat16),
        in_specs=[pl.BlockSpec(memory_space=pltpu.SMEM)]
        + [whole] * 4
        + [pl.BlockSpec(memory_space=pltpu.HBM)],
        out_specs=whole,
        scratch_shapes=[
            pltpu.VMEM((dates, tiles, blocks, 2, SUB, lines), jnp.float32),
            pltpu.VMEM((blocks, slots * looks_rows, lines), jnp.float32),
            pltpu.VMEM((dates, tiles * blocks * SUB, 2 * lines), jnp.bfloat16),
            pltpu.VMEM(tables[1].shape, jnp.bfloat16),
            pltpu.SemaphoreType.DMA,
        ],
        compiler_params=pltpu.CompilerParams(vmem_limit_bytes=VMEM_BYTES),
        cost_estimate=pl.CostEstimate(
            flops=16 * dates * gates * blocks * lines * lines,
            bytes_accessed=4 * columns.size,
            transcendentals=0,
        ),
        name="focus",
    )(
        pair_offset,
        columns,
        *phases,
        tables[0],
        pltpu.with_memory_space_constraint(tables[1], pltpu.HBM),
    )


def tri_window(offset):
    inside = (offset >= 0) & (offset < PATCH)
    return np.where(inside, 1.0 - np.abs(offset - (PATCH - 1) / 2.0) / HALF, 0.0)


def patch_tables(cells, starts):
    offset = np.asarray(cells)[:, None] - np.asarray(starts)[None, :]
    inside = ((offset >= 0) & (offset < PATCH)).astype(np.float64)
    angle = 2.0 * math.pi / PATCH * (offset[:, :, None] * np.arange(PATCH) % PATCH)
    ahead = np.exp(-1j * angle) * inside[:, :, None]
    behind = np.exp(1j * angle) * tri_window(offset)[:, :, None] / PATCH
    flat = (len(cells), len(starts) * PATCH)
    return ahead.reshape(flat), behind.reshape(flat).T


def goldstein_tables(dates, gate_order, line_looks):
    per = LANES // PATCH
    starts = np.arange(-HALF, line_looks, HALF)
    cells = np.arange(-HALF, line_looks + HALF)
    ahead, behind = patch_tables(cells, starts)
    main = slice(HALF, HALF + line_looks)
    behind = behind[:, main]
    split = per * PATCH

    def lanes_of(table, shift):
        block = np.zeros((2, line_looks, table.shape[1]), complex)
        block[0], block[1] = table[main], 1j * table[main]
        rim = np.zeros((2, line_looks, table.shape[1]), complex)
        for part, turn in enumerate((1.0, 1j)):
            rim[part, :HALF] = turn * table[HALF + line_looks :]
            rim[part, line_looks - HALF :] = turn * table[:HALF]
        flat = (2 * line_looks, table.shape[1])
        return block.reshape(flat), np.roll(rim.reshape(flat), shift, axis=0)

    def out_parts(table):
        return np.concatenate([table.real, table.imag], axis=1)

    near = [
        out_parts(np.concatenate(lanes_of(ahead[:, :split], parity * (line_looks // 2))))
        for parity in (0, 1)
    ]
    rest = ahead.shape[1] - split
    far_block = np.zeros((dates, 2 * line_looks, dates, rest), complex)
    far_rim = np.zeros((dates // 2, 2 * line_looks, dates, rest), complex)
    for date in range(dates):
        block, rim = lanes_of(ahead[:, split:], date % 2 * (line_looks // 2))
        far_block[date, :, date] = block
        far_rim[date // 2, :, date] = rim
    far = np.concatenate([far_block, far_rim]).reshape(-1, dates * rest)
    gate_starts = np.arange(-HALF, len(gate_order), HALF)
    gate_ahead, gate_behind = patch_tables(np.arange(len(gate_order)), gate_starts)
    ahead_rows = real_block(gate_ahead[gate_order]).T
    behind_rows = real_block(gate_behind).T

    lines_back = []
    for date in range(dates):
        far_back = np.zeros((dates, rest, line_looks), complex)
        far_back[date] = behind[split:]
        lines_back.append(
            np.concatenate(
                [real_block(behind[:split]), real_block(far_back.reshape(-1, line_looks))]
            ).T
        )
    gap = (np.arange(PATCH)[:, None] - np.arange(PATCH)[None, :]) % PATCH
    ring = ((gap == 0) | (gap == 1) | (gap == PATCH - 1)).astype(np.float64)
    box = np.concatenate(
        [np.kron(np.eye(per), ring), np.kron(np.eye(per), np.ones((PATCH, PATCH)))], axis=1
    )
    tables = (np.stack(near), out_parts(far), ahead_rows, box, behind_rows, np.stack(lines_back))
    return [as_bf16(table) for table in tables]


def slot_rows(data_ref, slots, looks_rows):
    blocks = data_ref.shape[0]
    data = data_ref[...].astype(jnp.float32)
    if looks_rows % SUB == 0:
        return [
            data[:, slot * looks_rows : (slot + 1) * looks_rows].reshape(-1, LANES)
            for slot in range(slots)
        ]
    top = lax.broadcasted_iota(jnp.int32, (SUB, LANES), 0) < looks_rows
    held = [[] for _ in range(slots)]
    for block in range(0, blocks, 2):
        for slot in range(0, slots, 2):
            rows = slice(slot * looks_rows, (slot + 2) * looks_rows)
            one, two = data[block, rows], data[block + 1, rows]
            held[slot].append(jnp.where(top, one, pltpu.roll(two, looks_rows, 0)))
            held[slot + 1].append(jnp.where(top, pltpu.roll(one, looks_rows, 0), two))
    return [jnp.concatenate(rows, axis=0) for rows in held]


def goldstein_kernel(shape, *refs):
    dates, chunks, looks_rows, gate_looks, line_looks = shape
    data_refs, refs = refs[:chunks], refs[chunks:]
    near_ref, far_ref, ahead_ref, box_ref, behind_ref, back_ref, out_ref = refs[:7]
    half_ref, spec_ref, weighted_ref = refs[7:]
    slots = dates + dates // 2
    cols = dates + 1
    dot = lambda a, b: jnp.dot(a, b, preferred_element_type=jnp.float32)
    if data_refs[0].shape[0] == slots:
        held = [data_refs[0][slot] for slot in range(slots)]
    else:
        held = zip(*[slot_rows(ref, slots, looks_rows) for ref in data_refs])
        held = [jnp.concatenate(rows, axis=0).astype(jnp.bfloat16) for rows in held]
    for parity in (0, 1):
        rows = jnp.concatenate(
            [
                jnp.concatenate([held[date], held[dates + date // 2]], axis=1)
                for date in range(parity, dates, 2)
            ],
            axis=0,
        )
        both = dot(rows, near_ref[parity]).astype(jnp.bfloat16)
        for index, date in enumerate(range(parity, dates, 2)):
            mine = both[index * gate_looks : (index + 1) * gate_looks]
            half_ref[:gate_looks, date * LANES : (date + 1) * LANES] = mine[:, :LANES]
            half_ref[gate_looks:, date * LANES : (date + 1) * LANES] = mine[:, LANES:]
    both = dot(jnp.concatenate(held, axis=1), far_ref[...]).astype(jnp.bfloat16)
    half_ref[:gate_looks, dates * LANES :] = both[:, :LANES]
    half_ref[gate_looks:, dates * LANES :] = both[:, LANES:]

    spec_ref[...] = dot(ahead_ref[...], half_ref[...])
    bins = ahead_ref.shape[0] // 2
    for col in range(cols):
        lanes = slice(col * LANES, (col + 1) * LANES)
        re, im = spec_ref[:bins, lanes], spec_ref[bins:, lanes]
        power = (re * re + im * im).astype(jnp.bfloat16)
        sums = dot(power, box_ref[...])
        for start in range(0, bins, PATCH):
            rows = slice(start, start + PATCH)
            line = sums[rows, :LANES]
            total = jnp.sum(sums[rows, LANES:], axis=0, keepdims=True)
            smooth = line + pltpu.roll(line, 1, 0) + pltpu.roll(line, PATCH - 1, 0)
            level = total * (1.0 / (PATCH * PATCH)) + LEVEL_FLOOR
            square = smooth * (1.0 / (9.0 * level)) + BOX_FLOOR
            weight = square * lax.rsqrt(square)
            weighted_ref[rows, lanes] = (re[rows] * weight).astype(jnp.bfloat16)
            weighted_ref[start + bins : start + bins + PATCH, lanes] = (im[rows] * weight).astype(
                jnp.bfloat16
            )
    inverse = dot(behind_ref[...], weighted_ref[...]).astype(jnp.bfloat16)
    far = [inverse[:gate_looks, dates * LANES :], inverse[gate_looks:, dates * LANES :]]
    for date in range(dates):
        lanes = slice(date * LANES, (date + 1) * LANES)
        rows = jnp.concatenate([inverse[:gate_looks, lanes], inverse[gate_looks:, lanes]] + far, axis=1)
        result = lax.dot_general(
            back_ref[date], rows, (((1,), (1,)), ((), ())), preferred_element_type=jnp.float32
        )
        out_ref[date, 0] = result[:line_looks]
        out_ref[date, 1] = result[line_looks:]


def goldstein(looks, dates, line_looks):
    chunks = len(looks)
    blocks, rows, _ = looks[0].shape
    slots = dates + dates // 2
    looks_rows = rows // slots
    gate_looks = chunks * blocks * looks_rows
    order = np.arange(gate_looks).reshape(blocks, chunks, looks_rows).swapaxes(0, 1).reshape(-1)
    if looks_rows % SUB and 2 * looks_rows != SUB:
        looks = [
            each.reshape(blocks, slots, looks_rows, LANES)
            .swapaxes(0, 1)
            .reshape(slots, blocks * looks_rows, LANES)
            for each in looks
        ]
        looks = [jnp.concatenate(looks, axis=1)]
    tables = goldstein_tables(dates, order, line_looks)
    bins = tables[2].shape[0] // 2
    width = (dates + 1) * LANES
    shape = (dates, len(looks), looks_rows, gate_looks, line_looks)
    whole = pl.BlockSpec(memory_space=pltpu.VMEM)
    filtered = pl.pallas_call(
        lambda *refs: goldstein_kernel(shape, *refs),
        out_shape=jax.ShapeDtypeStruct((dates, 2, line_looks, gate_looks), jnp.float32),
        in_specs=[whole] * (len(looks) + len(tables)),
        out_specs=whole,
        scratch_shapes=[
            pltpu.VMEM((2 * gate_looks, width), jnp.bfloat16),
            pltpu.VMEM((2 * bins, width), jnp.float32),
            pltpu.VMEM((2 * bins, width), jnp.bfloat16),
        ],
        compiler_params=pltpu.CompilerParams(vmem_limit_bytes=VMEM_BYTES),
        name="goldstein",
    )(*looks, *tables)
    return filtered.swapaxes(2, 3)


def body(raw_echo, range_filter, azimuth_phase, pair_offset):
    dates, _, lines, gates_in = raw_echo.shape
    devices = lax.axis_size("lines")
    gates = azimuth_phase.shape[0]
    chunks = 1
    filter_chunks = range_filter.reshape(2, devices, chunks, gates // chunks, gates_in)
    phases = phase_tables(azimuth_phase, chunks, devices)

    def exchange(blocks):
        return lax.all_to_all(blocks, "lines", split_axis=0, concat_axis=0, tiled=True)

    sent = compress(raw_echo, filter_chunks, 0)
    tables = focus_tables(devices, lines)
    looks = [exchange(focus(exchange(sent), pair_offset, phases, tables, 0))]
    return goldstein(looks, dates, lines // ML_AZ)


def solution(mesh):
    placed = (P("groups", None, "lines", None), P(), P("lines", None), P())
    return jax.shard_map(
        body,
        mesh=mesh,
        in_specs=placed,
        out_specs=P("groups", None, None, "lines"),
        check_vma=False,
    )
```

```python
import math

import jax
import jax.numpy as jnp
import numpy as np
from jax import lax
from jax.experimental import pallas as pl
from jax.experimental.pallas import tpu as pltpu
from jax.sharding import PartitionSpec as P

ML_RG = 4
ML_AZ = 2
PATCH = 32
HALF = PATCH // 2
BOX_FLOOR = 0.25
LEVEL_FLOOR = 1e-06
SUB = 8
LANES = 128
VMEM_BYTES = 20 * 1024 * 1024


def real_block(table):
    return np.block([[table.real, table.imag], [-table.imag, table.real]])


def wave(rows, cols, period, direction):
    product = np.asarray(rows)[:, None] * np.asarray(cols)[None, :] % period
    return np.exp(direction * 2j * math.pi / period * product)


def as_bf16(table):
    return jnp.asarray(np.asarray(table, np.float32), jnp.bfloat16)


def line_order(line_len):
    return np.arange(line_len).reshape(line_len // ML_AZ, ML_AZ).T.reshape(-1)


def small_dft(parts, direction):
    count = len(parts)
    if count == 1:
        return parts
    even = small_dft(parts[0::2], direction)
    odd = small_dft(parts[1::2], direction)
    low, high = [], []
    for k in range(count // 2):
        (er, ei), (vr, vi) = even[k], odd[k]
        if k == 0:
            tr, ti = vr, vi
        elif 4 * k == count:
            if direction < 0:
                tr, ti = vi, -vr
            else:
                tr, ti = -vi, vr
        elif 8 * k == count:
            s = math.sqrt(0.5)
            if direction < 0:
                tr, ti = (vr + vi) * s, (vi - vr) * s
            else:
                tr, ti = (vr - vi) * s, (vi + vr) * s
        elif 8 * k == 3 * count:
            s = math.sqrt(0.5)
            if direction < 0:
                tr, ti = (vi - vr) * s, -(vr + vi) * s
            else:
                tr, ti = -(vr + vi) * s, (vr - vi) * s
        else:
            c = math.cos(2 * math.pi * k / count)
            s = direction * math.sin(2 * math.pi * k / count)
            tr, ti = vr * c - vi * s, vr * s + vi * c
        low.append((er + tr, ei + ti))
        high.append((er - tr, ei - ti))
    return low + high


def compress_kernel(
    shape, raw_hbm, filter_hbm, out_hbm, raw_ref, filter_ref, wide_ref, out_ref, raw_sems,
    filter_sems, out_sems,
):
    chunk, dates, step, targets, tiles, gates, lines = shape
    looks_rows = gates // ML_RG
    gates_in = raw_ref.shape[3]
    copies = [
        pltpu.make_async_copy(
            raw_hbm.at[pl.ds(first, step)], raw_ref.at[pl.ds(first, step)], raw_sems.at[first // step]
        )
        for first in range(0, dates, step)
    ]
    out_copies = [
        pltpu.make_async_copy(out_ref.at[:, date], out_hbm.at[:, date], out_sems.at[date])
        for date in range(dates)
    ]
    parts = 2
    held = targets // parts
    filter_copies = [
        pltpu.make_async_copy(
            filter_hbm.at[:, pl.ds(part * held, held), chunk],
            filter_ref.at[:, pl.ds(part * held, held)],
            filter_sems.at[part],
        )
        for part in range(parts)
    ]
    for copy in [filter_copies[0], *copies[:1], *filter_copies[1:], *copies[1:]]:
        copy.start()

    def product(w, x):
        return lax.dot_general(
            w, x, (((1,), (1,)), ((), ())), preferred_element_type=jnp.float32
        )

    for first in range(0, dates, step):
        copies[first // step].wait()
        raw = [
            raw_ref[first : first + step, part].reshape(step * lines, gates_in) for part in (0, 1)
        ]
        for group in range(parts):
            if first == 0:
                filter_copies[group].wait()
            weight = [
                filter_ref[part, group * held : (group + 1) * held].reshape(held * gates, gates_in)
                for part in (0, 1)
            ]
            real = product(weight[0], raw[0]) - product(weight[1], raw[1])
            imag = product(weight[1], raw[0]) + product(weight[0], raw[1])
            rows = slice(group * held * gates, (group + 1) * held * gates)
            for at in range(step):
                wide_ref[first + at, 0, rows] = real[:, at * lines : (at + 1) * lines]
                wide_ref[first + at, 1, rows] = imag[:, at * lines : (at + 1) * lines]
        for date in range(first, first + step):
            for target in range(targets):
                for tile in range(tiles):
                    rows = []
                    for part in (0, 1):
                        begin, count = tile * SUB, min(looks_rows, SUB)
                        for at in range(begin, begin + SUB, count):
                            gate = target * gates + at // looks_rows + ML_RG * (at % looks_rows)
                            rows.append(wide_ref[date, part, pl.ds(gate, count, stride=ML_RG), :])
                    out_ref[target, date, tile] = jnp.concatenate(rows, axis=0).astype(
                        jnp.bfloat16
                    )
            out_copies[date].start()
    for copy in out_copies:
        copy.wait()


def compress(raw_echo, filter_chunks, chunk):
    dates, _, lines, gates_in = raw_echo.shape
    _, targets, _, gates, _ = filter_chunks.shape
    tiles = gates // SUB
    step = 2 if dates % 2 == 0 else 1
    shape = (chunk, dates, step, targets, tiles, gates, lines)
    hbm = pl.BlockSpec(memory_space=pltpu.HBM)
    return pl.pallas_call(
        lambda *refs: compress_kernel(shape, *refs),
        out_shape=jax.ShapeDtypeStruct((targets, dates, tiles, 2 * SUB, lines), jnp.bfloat16),
        in_specs=[hbm, hbm],
        out_specs=pl.BlockSpec(memory_space=pl.ANY),
        scratch_shapes=[
            pltpu.VMEM(raw_echo.shape, jnp.bfloat16),
            pltpu.VMEM((2, targets, gates, gates_in), jnp.bfloat16),
            pltpu.VMEM((dates, 2, targets * gates, lines), jnp.float32),
            pltpu.VMEM((targets, dates, tiles, 2 * SUB, lines), jnp.bfloat16),
            pltpu.SemaphoreType.DMA((dates // step,)),
            pltpu.SemaphoreType.DMA((2,)),
            pltpu.SemaphoreType.DMA((dates,)),
        ],
        compiler_params=pltpu.CompilerParams(vmem_limit_bytes=VMEM_BYTES),
        cost_estimate=pl.CostEstimate(
            flops=8 * dates * lines * targets * gates * gates_in,
            bytes_accessed=4 * (raw_echo.size + targets * gates * gates_in),
            transcendentals=0,
        ),
        name="compress",
    )(*[pltpu.with_memory_space_constraint(x, pltpu.HBM) for x in (raw_echo, filter_chunks)])


def focus_kernel(
    shape, offset_ref, data_ref, cos_ref, sin_ref, turn_ref, table_hbm, out_ref, image_ref, look_ref,
    row_ref, table_ref, table_sem,
):
    chunk, dates, blocks, tiles, gates, lines = shape
    looks_rows = gates // ML_RG
    look_lines = lines // ML_AZ
    count = blocks * SUB
    table_copy = pltpu.make_async_copy(table_hbm, table_ref, table_sem)
    table_copy.start()

    def ahead(date):
        rows = []
        for tile in range(tiles):
            parts = []
            for a in range(blocks):
                both = data_ref[a, date, tile].astype(jnp.float32)
                parts.append((both[:SUB], both[SUB:]))
            for a, (re, im) in enumerate(small_dft(parts, -1)):
                tr, ti = turn_ref[0, a : a + 1], turn_ref[1, a : a + 1]
                rows.append(jnp.concatenate([re * tr - im * ti, re * ti + im * tr], axis=1))
        row_ref[date] = jnp.concatenate(rows, axis=0).astype(jnp.bfloat16)

    lead = min(2, dates)
    for date in range(lead):
        ahead(date)
    table_copy.wait()
    for date in range(dates):
        if date + lead < dates:
            ahead(date + lead)
        spectrum = jnp.dot(row_ref[date], table_ref[0], preferred_element_type=jnp.float32)
        rows = []
        for tile in range(tiles):
            re = spectrum[tile * count : (tile + 1) * count, :lines]
            im = spectrum[tile * count : (tile + 1) * count, lines:]
            pr, pi = cos_ref[chunk, tile], sin_ref[chunk, tile]
            rows.append(jnp.concatenate([re * pr - im * pi, re * pi + im * pr], axis=1))
        rows = jnp.concatenate(rows, axis=0).astype(jnp.bfloat16)
        back = jnp.dot(rows, table_ref[1], preferred_element_type=jnp.float32)
        for tile in range(tiles):
            parts = []
            for a in range(blocks):
                row = tile * count + a * SUB
                re, im = back[row : row + SUB, :lines], back[row : row + SUB, lines:]
                tr, ti = turn_ref[2, a : a + 1], turn_ref[3, a : a + 1]
                parts.append((re * tr - im * ti, re * ti + im * tr))
            for a, (re, im) in enumerate(small_dft(parts, 1)):
                image_ref[date, tile, a, 0] = re
                image_ref[date, tile, a, 1] = im

    lane = lax.broadcasted_iota(jnp.int32, (SUB, lines), 1)
    first = lane < look_lines
    scale = 1.0 / (ML_RG * ML_AZ)
    for date in range(dates):
        partner = lax.rem(date + offset_ref[date], dates)
        for a in range(blocks):
            sums = {}
            for tile in range(tiles):
                cr, ci = image_ref[date, tile, a, 0], image_ref[date, tile, a, 1]
                pr, pi = image_ref[partner, tile, a, 0], image_ref[partner, tile, a, 1]
                re, im = cr * pr + ci * pi, ci * pr - cr * pi
                at = tile * SUB % looks_rows
                if at in sums:
                    re, im = re + sums[at][0], im + sums[at][1]
                sums[at] = (re, im)
            for at, (re, im) in sums.items():
                look = jnp.where(first, re, im) + pltpu.roll(
                    jnp.where(first, im, re), look_lines, 1
                )
                step = SUB
                while step > looks_rows:
                    step //= 2
                    look = look + pltpu.roll(look, step, 0)
                count = min(SUB, looks_rows)
                row = date * looks_rows + at
                look_ref[a, row : row + count, :] = (look * scale)[:count]

    small = lax.broadcasted_iota(jnp.int32, (looks_rows, lines), 1) % look_lines
    from_high, from_low = small < HALF, small >= look_lines - HALF
    zero = jnp.zeros((looks_rows, lines), jnp.float32)

    def rim(a, date):
        rows = slice(date * looks_rows, (date + 1) * looks_rows)
        high = look_ref[a + 1, rows, :] if a + 1 < blocks else zero
        low = look_ref[a - 1, rows, :] if a > 0 else zero
        return jnp.where(from_high, high, low)

    for a in range(blocks):
        for date in range(0, dates, 2):
            own = rim(a, date)
            other = pltpu.roll(rim(a, date + 1), look_lines // 2, 1)
            row = (dates + date // 2) * looks_rows
            look_ref[a, row : row + looks_rows, :] = jnp.where(from_high | from_low, own, other)
    out_ref[...] = look_ref[...].astype(jnp.bfloat16)


def phase_tables(azimuth_phase, chunks, blocks):
    gates, total = azimuth_phase.shape
    looks_rows = gates // chunks // ML_RG
    lines = total // blocks
    tiles = gates // chunks // SUB
    phase = azimuth_phase.reshape(chunks, looks_rows, ML_RG, lines, blocks)
    phase = phase.transpose(0, 2, 1, 4, 3).reshape(chunks, tiles, SUB, blocks, lines)
    phase = phase.transpose(0, 1, 3, 2, 4).reshape(chunks, tiles, blocks * SUB, lines)
    phase = lax.optimization_barrier(phase)
    return jnp.cos(phase), jnp.sin(phase)


def focus_tables(blocks, lines):
    total = blocks * lines
    order = line_order(lines)
    ahead = wave(np.arange(blocks), np.arange(lines), total, -1)
    behind = wave(np.arange(blocks), order, total, 1)
    turn = np.stack([ahead.real, ahead.imag, behind.real, behind.imag]).astype(np.float32)
    fwd = real_block(wave(np.arange(lines), np.arange(lines), lines, -1))
    back = real_block(wave(np.arange(lines), order, lines, 1) / total)
    return jnp.asarray(turn), as_bf16(np.stack([fwd, back]))


def focus(columns, pair_offset, phases, tables, chunk):
    blocks, dates, tiles, _, lines = columns.shape
    gates = tiles * SUB
    looks_rows = gates // ML_RG
    slots = dates + dates // 2
    shape = (chunk, dates, blocks, tiles, gates, lines)
    whole = pl.BlockSpec(memory_space=pltpu.VMEM)
    return pl.pallas_call(
        lambda *refs: focus_kernel(shape, *refs),
        out_shape=jax.ShapeDtypeStruct((blocks, slots * looks_rows, lines), jnp.bfloat16),
        in_specs=[pl.BlockSpec(memory_space=pltpu.SMEM)]
        + [whole] * 4
        + [pl.BlockSpec(memory_space=pltpu.HBM)],
        out_specs=whole,
        scratch_shapes=[
            pltpu.VMEM((dates, tiles, blocks, 2, SUB, lines), jnp.float32),
            pltpu.VMEM((blocks, slots * looks_rows, lines), jnp.float32),
            pltpu.VMEM((dates, tiles * blocks * SUB, 2 * lines), jnp.bfloat16),
            pltpu.VMEM(tables[1].shape, jnp.bfloat16),
            pltpu.SemaphoreType.DMA,
        ],
        compiler_params=pltpu.CompilerParams(vmem_limit_bytes=VMEM_BYTES),
        cost_estimate=pl.CostEstimate(
            flops=16 * dates * gates * blocks * lines * lines,
            bytes_accessed=4 * columns.size,
            transcendentals=0,
        ),
        name="focus",
    )(
        pair_offset,
        columns,
        *phases,
        tables[0],
        pltpu.with_memory_space_constraint(tables[1], pltpu.HBM),
    )


def tri_window(offset):
    inside = (offset >= 0) & (offset < PATCH)
    return np.where(inside, 1.0 - np.abs(offset - (PATCH - 1) / 2.0) / HALF, 0.0)


def patch_tables(cells, starts):
    offset = np.asarray(cells)[:, None] - np.asarray(starts)[None, :]
    inside = ((offset >= 0) & (offset < PATCH)).astype(np.float64)
    angle = 2.0 * math.pi / PATCH * (offset[:, :, None] * np.arange(PATCH) % PATCH)
    ahead = np.exp(-1j * angle) * inside[:, :, None]
    behind = np.exp(1j * angle) * tri_window(offset)[:, :, None] / PATCH
    flat = (len(cells), len(starts) * PATCH)
    return ahead.reshape(flat), behind.reshape(flat).T


def goldstein_tables(dates, gate_order, line_looks):
    per = LANES // PATCH
    starts = np.arange(-HALF, line_looks, HALF)
    cells = np.arange(-HALF, line_looks + HALF)
    ahead, behind = patch_tables(cells, starts)
    main = slice(HALF, HALF + line_looks)
    behind = behind[:, main]
    split = per * PATCH

    def lanes_of(table, shift):
        block = np.zeros((2, line_looks, table.shape[1]), complex)
        block[0], block[1] = table[main], 1j * table[main]
        rim = np.zeros((2, line_looks, table.shape[1]), complex)
        for part, turn in enumerate((1.0, 1j)):
            rim[part, :HALF] = turn * table[HALF + line_looks :]
            rim[part, line_looks - HALF :] = turn * table[:HALF]
        flat = (2 * line_looks, table.shape[1])
        return block.reshape(flat), np.roll(rim.reshape(flat), shift, axis=0)

    def out_parts(table):
        return np.concatenate([table.real, table.imag], axis=1)

    near = [
        out_parts(np.concatenate(lanes_of(ahead[:, :split], parity * (line_looks // 2))))
        for parity in (0, 1)
    ]
    rest = ahead.shape[1] - split
    far_block = np.zeros((dates, 2 * line_looks, dates, rest), complex)
    far_rim = np.zeros((dates // 2, 2 * line_looks, dates, rest), complex)
    for date in range(dates):
        block, rim = lanes_of(ahead[:, split:], date % 2 * (line_looks // 2))
        far_block[date, :, date] = block
        far_rim[date // 2, :, date] = rim
    far = np.concatenate([far_block, far_rim]).reshape(-1, dates * rest)
    gate_starts = np.arange(-HALF, len(gate_order), HALF)
    gate_ahead, gate_behind = patch_tables(np.arange(len(gate_order)), gate_starts)
    ahead_rows = real_block(gate_ahead[gate_order]).T
    behind_rows = real_block(gate_behind).T

    lines_back = []
    for date in range(dates):
        far_back = np.zeros((dates, rest, line_looks), complex)
        far_back[date] = behind[split:]
        lines_back.append(
            np.concatenate(
                [real_block(behind[:split]), real_block(far_back.reshape(-1, line_looks))]
            ).T
        )
    gap = (np.arange(PATCH)[:, None] - np.arange(PATCH)[None, :]) % PATCH
    ring = ((gap == 0) | (gap == 1) | (gap == PATCH - 1)).astype(np.float64)
    box = np.concatenate(
        [np.kron(np.eye(per), ring), np.kron(np.eye(per), np.ones((PATCH, PATCH)))], axis=1
    )
    tables = (np.stack(near), out_parts(far), ahead_rows, box, behind_rows, np.stack(lines_back))
    return [as_bf16(table) for table in tables]


def slot_rows(data_ref, slots, looks_rows):
    blocks = data_ref.shape[0]
    data = data_ref[...].astype(jnp.float32)
    if looks_rows % SUB == 0:
        return [
            data[:, slot * looks_rows : (slot + 1) * looks_rows].reshape(-1, LANES)
            for slot in range(slots)
        ]
    top = lax.broadcasted_iota(jnp.int32, (SUB, LANES), 0) < looks_rows
    held = [[] for _ in range(slots)]
    for block in range(0, blocks, 2):
        for slot in range(0, slots, 2):
            rows = slice(slot * looks_rows, (slot + 2) * looks_rows)
            one, two = data[block, rows], data[block + 1, rows]
            held[slot].append(jnp.where(top, one, pltpu.roll(two, looks_rows, 0)))
            held[slot + 1].append(jnp.where(top, pltpu.roll(one, looks_rows, 0), two))
    return [jnp.concatenate(rows, axis=0) for rows in held]


def goldstein_kernel(shape, *refs):
    dates, chunks, looks_rows, gate_looks, line_looks = shape
    data_refs, refs = refs[:chunks], refs[chunks:]
    near_ref, far_ref, ahead_ref, box_ref, behind_ref, back_ref, out_ref = refs[:7]
    half_ref, spec_ref, weighted_ref = refs[7:]
    slots = dates + dates // 2
    cols = dates + 1
    dot = lambda a, b: jnp.dot(a, b, preferred_element_type=jnp.float32)
    if data_refs[0].shape[0] == slots:
        held = [data_refs[0][slot] for slot in range(slots)]
    else:
        held = zip(*[slot_rows(ref, slots, looks_rows) for ref in data_refs])
        held = [jnp.concatenate(rows, axis=0).astype(jnp.bfloat16) for rows in held]
    for parity in (0, 1):
        rows = jnp.concatenate(
            [
                jnp.concatenate([held[date], held[dates + date // 2]], axis=1)
                for date in range(parity, dates, 2)
            ],
            axis=0,
        )
        both = dot(rows, near_ref[parity]).astype(jnp.bfloat16)
        for index, date in enumerate(range(parity, dates, 2)):
            mine = both[index * gate_looks : (index + 1) * gate_looks]
            half_ref[:gate_looks, date * LANES : (date + 1) * LANES] = mine[:, :LANES]
            half_ref[gate_looks:, date * LANES : (date + 1) * LANES] = mine[:, LANES:]
    both = dot(jnp.concatenate(held, axis=1), far_ref[...]).astype(jnp.bfloat16)
    half_ref[:gate_looks, dates * LANES :] = both[:, :LANES]
    half_ref[gate_looks:, dates * LANES :] = both[:, LANES:]

    spec_ref[...] = dot(ahead_ref[...], half_ref[...])
    bins = ahead_ref.shape[0] // 2
    for col in range(cols):
        lanes = slice(col * LANES, (col + 1) * LANES)
        re, im = spec_ref[:bins, lanes], spec_ref[bins:, lanes]
        power = (re * re + im * im).astype(jnp.bfloat16)
        sums = dot(power, box_ref[...])
        for start in range(0, bins, PATCH):
            rows = slice(start, start + PATCH)
            line = sums[rows, :LANES]
            total = jnp.sum(sums[rows, LANES:], axis=0, keepdims=True)
            smooth = line + pltpu.roll(line, 1, 0) + pltpu.roll(line, PATCH - 1, 0)
            level = total * (1.0 / (PATCH * PATCH)) + LEVEL_FLOOR
            square = smooth * (1.0 / (9.0 * level)) + BOX_FLOOR
            weight = square * lax.rsqrt(square)
            weighted_ref[rows, lanes] = (re[rows] * weight).astype(jnp.bfloat16)
            weighted_ref[start + bins : start + bins + PATCH, lanes] = (im[rows] * weight).astype(
                jnp.bfloat16
            )
    inverse = dot(behind_ref[...], weighted_ref[...]).astype(jnp.bfloat16)
    far = [inverse[:gate_looks, dates * LANES :], inverse[gate_looks:, dates * LANES :]]
    for date in range(dates):
        lanes = slice(date * LANES, (date + 1) * LANES)
        rows = jnp.concatenate([inverse[:gate_looks, lanes], inverse[gate_looks:, lanes]] + far, axis=1)
        result = lax.dot_general(
            back_ref[date], rows, (((1,), (1,)), ((), ())), preferred_element_type=jnp.float32
        )
        out_ref[date, 0] = result[:line_looks]
        out_ref[date, 1] = result[line_looks:]


def goldstein(looks, dates, line_looks):
    chunks = len(looks)
    blocks, rows, _ = looks[0].shape
    slots = dates + dates // 2
    looks_rows = rows // slots
    gate_looks = chunks * blocks * looks_rows
    order = np.arange(gate_looks).reshape(blocks, chunks, looks_rows).swapaxes(0, 1).reshape(-1)
    if looks_rows % SUB and 2 * looks_rows != SUB:
        looks = [
            each.reshape(blocks, slots, looks_rows, LANES)
            .swapaxes(0, 1)
            .reshape(slots, blocks * looks_rows, LANES)
            for each in looks
        ]
        looks = [jnp.concatenate(looks, axis=1)]
    tables = goldstein_tables(dates, order, line_looks)
    bins = tables[2].shape[0] // 2
    width = (dates + 1) * LANES
    shape = (dates, len(looks), looks_rows, gate_looks, line_looks)
    whole = pl.BlockSpec(memory_space=pltpu.VMEM)
    filtered = pl.pallas_call(
        lambda *refs: goldstein_kernel(shape, *refs),
        out_shape=jax.ShapeDtypeStruct((dates, 2, line_looks, gate_looks), jnp.float32),
        in_specs=[whole] * (len(looks) + len(tables)),
        out_specs=whole,
        scratch_shapes=[
            pltpu.VMEM((2 * gate_looks, width), jnp.bfloat16),
            pltpu.VMEM((2 * bins, width), jnp.float32),
            pltpu.VMEM((2 * bins, width), jnp.bfloat16),
        ],
        compiler_params=pltpu.CompilerParams(vmem_limit_bytes=VMEM_BYTES),
        name="goldstein",
    )(*looks, *tables)
    return filtered.swapaxes(2, 3)


def body(raw_echo, range_filter, azimuth_phase, pair_offset):
    dates, _, lines, gates_in = raw_echo.shape
    devices = lax.axis_size("lines")
    gates = azimuth_phase.shape[0]
    chunks = 1
    filter_chunks = range_filter.reshape(2, devices, chunks, gates // chunks, gates_in)
    phases = phase_tables(azimuth_phase, chunks, devices)

    def exchange(blocks):
        return lax.all_to_all(blocks, "lines", split_axis=0, concat_axis=0, tiled=True)

    sent = compress(raw_echo, filter_chunks, 0)
    tables = focus_tables(devices, lines)
    looks = [exchange(focus(exchange(sent), pair_offset, phases, tables, 0))]
    return goldstein(looks, dates, lines // ML_AZ)


def solution(mesh):
    placed = (P("groups", None, "lines", None), P(), P("lines", None), P())
    return jax.shard_map(
        body,
        mesh=mesh,
        in_specs=placed,
        out_specs=P("groups", None, None, "lines"),
        check_vma=False,
    )
```
